512 devices in a mesh: lat: 64 (over x, z_lo, core), tp: 8 (over z_hi, y).
Axes of the slice: x: 4, y: 4, z: 16 (z_hi: 2, z_lo: 8; z = z_hi * 8 + z_lo), core: 2. Of those that a mesh axis runs over, the one named last changes fastest.
Arguments:
- fields: bfloat16 [128, 4, 64, 512], P('lat'), may hold values from -16 to 16
- classes: int32 [128, 64], P('lat'), may hold values from 0 to 7
- class_table: bfloat16 [8, 512], replicated, may hold values from -4 to 4
- gain_fine: float32 [512], replicated, may hold values from 0.1 to 1.9
- fine_qkv: bfloat16 [512, 8, 192], P(None, 'tp'), may hold values from -1.5 to 1.5
- fine_out: bfloat16 [8, 64, 512], P('tp'), may hold values from -0.25 to 0.25
- gain_merge: float32 [2048], replicated, may hold values from 0.1 to 1.9
- merge_weight: bfloat16 [2048, 1024], P(None, 'tp'), may hold values from -0.125 to 0.125
- gain_coarse: float32 [1024], replicated, may hold values from 0.1 to 1.9
- coarse_qkv: bfloat16 [1024, 16, 192], P(None, 'tp'), may hold values from -1.5 to 1.5
- coarse_out: bfloat16 [16, 64, 1024], P('tp'), may hold values from -0.1875 to 0.1875
- up_weight: bfloat16 [1024, 2048], P(None, 'tp'), may hold values from -0.1875 to 0.1875
- cotangent: bfloat16 [128, 4, 64, 512], P('lat'), may hold values from -6 to 6
Outputs:
- next_fields: bfloat16 [128, 4, 64, 512], P('lat')
- fields_grad: bfloat16 [128, 4, 64, 512], P('lat', None, 'tp')
- fine_qkv_grad: float32 [512, 8, 192], P('lat', 'tp')
- merge_weight_grad: float32 [2048, 1024], P('lat', 'tp')
The draws below stay inside these ranges and needn't reach their ends.
All inputs are finite; a program needn't handle non-finite values.
Results may differ from the reference program's by a relative error of at most 0.035.
Values may be sent and summed in bfloat16 or wider, within the bound.
A program may use at most 64 MiB of HBM per device.

```python
import math
import jax
import jax.numpy as jnp
import numpy as np
from jax import lax

D = 512
DC = 1024
HEADS = 8
CHEADS = 16
HD = 64
CHD = 64
CLASSES = 8
LEV = 4
WIN = 8
LON = 64
NLAT = 128


def projection(key, row_count, head_count, head_depth):
    shape = (row_count, head_count, 3 * head_depth)
    return jax.random.truncated_normal(key, -3.0, 3.0, shape, jnp.float32) / math.sqrt(row_count)


def draw_fine_qkv(key, part):
    key = jax.random.fold_in(key, 11)
    values = projection(key, D, HEADS, D // HEADS)
    return jnp.clip(values, -1.5, 1.5).astype(jnp.bfloat16)


def draw_coarse_qkv(key, part):
    key = jax.random.fold_in(key, 23)
    values = projection(key, DC, CHEADS, DC // CHEADS)
    return jnp.clip(values, -1.5, 1.5).astype(jnp.bfloat16)


def with_ends(result, key, smallest, high):
    extent = result.shape
    spot = [jax.random.randint(jax.random.fold_in(key, axis), (), 0, extent[axis]) for axis in range(len(extent))]
    result = result.at[tuple(spot)].set(smallest)
    longest = extent.index(max(extent))
    spot[longest] = (spot[longest] + 1) % extent[longest]
    return result.at[tuple(spot)].set(high)


def strengthened(result, own_key, source, target, parts, factor):
    owner, partner = [(jnp.arange(result.shape[axis_at]) // (result.shape[axis_at] // parts)).reshape([-1 if axis == axis_at else 1 for axis in range(result.ndim)]) for axis_at in (source, target)]
    chosen = jax.random.permutation(own_key, parts)[partner]
    strong = (owner == chosen) | (owner == (partner + parts // 2) % parts)
    return jnp.where(strong, factor * result, result)


def level_of(own_key, shape, split, smallest, high):
    def one(position, shards_of):
        draws = jax.random.uniform(jax.random.fold_in(jax.random.fold_in(own_key, 6), position), (shards_of,), jnp.float32, smallest / len(split), high / len(split))
        return jnp.repeat(jnp.exp(draws), shape[position] // shards_of).reshape((-1,) + (1,) * (len(shape) - position - 1))

    level = one(*split[0])
    for cut in split[1:]:
        level = level * one(*cut)
    return level


def bell_draw(stream_key, shape, scale, most, pieces=(), kind=jnp.bfloat16):
    level = level_of(stream_key, shape, pieces, -0.22, 0.18) if pieces else 1.0
    values = jax.random.normal(stream_key, shape, jnp.float32) * scale * level
    return jnp.minimum(jnp.maximum(values, -most), most).astype(kind)


def bell_draw_with(rng, extent, scale, limit, pieces, heavy, kind=jnp.bfloat16):
    values = scale * jax.random.normal(rng, extent, jnp.float32)
    if pieces:
        values = values * level_of(rng, extent, pieces, -0.22, 0.18)
    return jnp.clip(strengthened(values, jax.random.fold_in(rng, 3), *heavy), -limit, limit).astype(kind)


def setup_inputs(seed: int = 0) -> dict:
    key_list = jax.random.split(jax.random.key(seed), 14)
    fields = bell_draw_with(key_list[0], (NLAT, LEV, LON, D), 1.0, 16.0, ((0, 64),), (0, 3, 64, 4.0))
    classes = with_ends(jax.random.randint(key_list[1], (NLAT, LON), 0, CLASSES), jax.random.fold_in(key_list[1], 1), 0, CLASSES - 1).astype(jnp.int32)
    class_table = bell_draw(key_list[2], (CLASSES, D), 1.0, 4.0)
    gain_fine = jnp.clip(1.0 + 0.18 * jax.random.normal(key_list[3], (D,), jnp.float32), 0.1, 1.9)
    fine_qkv = draw_fine_qkv(jax.random.fold_in(key_list[13], 71), 0)
    fine_out = bell_draw(key_list[5], (HEADS, HD, D), D ** -0.5, 0.25, ((0, 8),))
    gain_merge = jnp.clip(1.0 + 0.18 * jax.random.normal(key_list[6], (4 * D,), jnp.float32), 0.1, 1.9)
    merge_weight = bell_draw(key_list[7], (4 * D, DC), (4 * D) ** -0.5, 0.125, ((1, 8),))
    gain_coarse = jnp.clip(1.0 + 0.18 * jax.random.normal(key_list[8], (DC,), jnp.float32), 0.1, 1.9)
    coarse_qkv = draw_coarse_qkv(jax.random.fold_in(key_list[13], 71), 0)
    coarse_out = bell_draw(key_list[10], (CHEADS, CHD, DC), DC ** -0.5, 0.1875, ((0, 8),))
    up_weight = bell_draw(key_list[11], (DC, 4 * D), DC ** -0.5, 0.1875, ((1, 8),))
    cotangent = bell_draw(key_list[12], (NLAT, LEV, LON, D), 1.0, 6.0, ((0, 64),))
    return dict(fields=fields, classes=classes, class_table=class_table, gain_fine=gain_fine, fine_qkv=fine_qkv, fine_out=fine_out, gain_merge=gain_merge, merge_weight=merge_weight, gain_coarse=gain_coarse, coarse_qkv=coarse_qkv, coarse_out=coarse_out, up_weight=up_weight, cotangent=cotangent)


EPSILON = 1e-05
NEGATIVE = -1e+30

def normalize(values, gain_vector):
    average = lax.optimization_barrier(jnp.mean(values, axis=-1, keepdims=True))
    centred = values - average
    spread = lax.optimization_barrier(jnp.mean(centred * centred, axis=-1, keepdims=True))
    return centred * lax.rsqrt(spread + EPSILON) * gain_vector

def normalize_back(values, gain_vector, incoming):
    return jax.vjp(lambda argument: normalize(argument, gain_vector), values)[1](incoming)[0]

def contract(pattern, operand_a, operand_b):
    return jnp.einsum(pattern, operand_a.astype(jnp.float32), operand_b.astype(jnp.float32))

def widen_keys(kv_term, head_size):
    return jnp.concatenate([jnp.zeros_like(kv_term[..., :head_size]), kv_term], axis=-1)

def to_windows(values, offset, window_width):
    row_count, levels, lon_count, head_count, head_depth = values.shape
    rolled = jnp.roll(values, -offset, axis=2)
    grouped = rolled.reshape(row_count, levels, lon_count // window_width, window_width, head_count, head_depth)
    grouped = grouped.transpose(0, 2, 4, 1, 3, 5)
    return grouped.reshape(row_count, lon_count // window_width, head_count, levels * window_width, head_depth)

def from_windows(values, offset, levels):
    row_count, window_count, head_count, window_tokens, head_depth = values.shape
    window_width = window_tokens // levels
    grouped = values.reshape(row_count, window_count, head_count, levels, window_width, head_depth)
    grouped = grouped.transpose(0, 3, 1, 4, 2, 5)
    joined = grouped.reshape(row_count, levels, window_count * window_width, head_count, head_depth)
    return jnp.roll(joined, offset, axis=2)

def pack_quads(values):
    row_count, levels, lon_count, feature_width = values.shape
    grouped = values.reshape(row_count // 2, 2, levels, lon_count // 2, 2, feature_width)
    return grouped.transpose(0, 2, 3, 1, 4, 5).reshape(row_count // 2, levels, lon_count // 2, 4 * feature_width)

def unpack_quads(values):
    row_count, levels, lon_count, packed_width = values.shape
    grouped = values.reshape(row_count, levels, lon_count, 2, 2, packed_width // 4)
    return grouped.transpose(0, 3, 1, 2, 4, 5).reshape(2 * row_count, levels, 2 * lon_count, packed_width // 4)

def window_attend(queries, key_own, value_own, key_partner, value_partner, present, score_scale):
    score_own = contract('rwhqe,rwhke->rwhqk', queries, key_own) * score_scale
    score_partner = contract('rwhqe,rwhke->rwhqk', queries, key_partner) * score_scale
    score_partner = jnp.where(present, score_partner, NEGATIVE)
    largest = jnp.maximum(lax.optimization_barrier(jnp.max(score_own, axis=-1, keepdims=True)), lax.optimization_barrier(jnp.max(score_partner, axis=-1, keepdims=True)))
    exp_own = jnp.exp(score_own - largest)
    exp_partner = jnp.exp(score_partner - largest)
    denominator = lax.optimization_barrier(jnp.sum(exp_own, axis=-1, keepdims=True)) + lax.optimization_barrier(jnp.sum(exp_partner, axis=-1, keepdims=True))
    prob_own = exp_own / denominator
    prob_partner = exp_partner / denominator
    mixture = contract('rwhqk,rwhke->rwhqe', prob_own.astype(jnp.bfloat16), value_own)
    mixture = mixture + contract('rwhqk,rwhke->rwhqe', prob_partner.astype(jnp.bfloat16), value_partner)
    return (mixture.astype(jnp.bfloat16), prob_own, prob_partner)

def window_back(queries, key_own, value_own, key_partner, value_partner, prob_own, prob_partner, grad_out, score_scale):
    half_own = prob_own.astype(jnp.bfloat16)
    half_partner = prob_partner.astype(jnp.bfloat16)
    value_grad_own = contract('rwhqk,rwhqe->rwhke', half_own, grad_out)
    value_grad_partner = contract('rwhqk,rwhqe->rwhke', half_partner, grad_out)
    prob_grad_own = contract('rwhqe,rwhke->rwhqk', grad_out, value_own)
    prob_grad_partner = contract('rwhqe,rwhke->rwhqk', grad_out, value_partner)
    row_dot = lax.optimization_barrier(jnp.sum(prob_grad_own * prob_own, axis=-1, keepdims=True))
    row_dot = row_dot + lax.optimization_barrier(jnp.sum(prob_grad_partner * prob_partner, axis=-1, keepdims=True))
    score_grad_own = (prob_own * (prob_grad_own - row_dot) * score_scale).astype(jnp.bfloat16)
    score_grad_partner = (prob_partner * (prob_grad_partner - row_dot) * score_scale).astype(jnp.bfloat16)
    query_grad = contract('rwhqk,rwhke->rwhqe', score_grad_own, key_own)
    query_grad = query_grad + contract('rwhqk,rwhke->rwhqe', score_grad_partner, key_partner)
    key_grad_own = contract('rwhqk,rwhqe->rwhke', score_grad_own, queries)
    key_grad_partner = contract('rwhqk,rwhqe->rwhke', score_grad_partner, queries)
    return (query_grad, key_grad_own, value_grad_own, key_grad_partner, value_grad_partner)

def reference(fields, classes, class_table, gain_fine, fine_qkv, fine_out, gain_merge, merge_weight, gain_coarse, coarse_qkv, coarse_out, up_weight, cotangent):
    row_count, levels, lon_count, feature_width = fields.shape
    head_size = fine_qkv.shape[2] // 3
    coarse_head = coarse_qkv.shape[2] // 3
    norm_scale = (row_count * levels * lon_count) ** (-0.5)
    offset = WIN // 2
    onehot = (classes[..., None] == jnp.arange(CLASSES, dtype=jnp.int32)).astype(jnp.bfloat16)
    embedded = jnp.dot(onehot.reshape(-1, CLASSES), class_table, preferred_element_type=jnp.float32)
    hidden = fields.astype(jnp.float32) + embedded.reshape(row_count, 1, lon_count, feature_width)
    normed = normalize(hidden, gain_fine).astype(jnp.bfloat16)
    qkv = contract('tvxd,dhe->tvxhe', normed, fine_qkv).astype(jnp.bfloat16)
    row_index = np.arange(row_count)
    partner = np.where(row_index % 2 == 1, row_index + 1, row_index - 1)
    present_rows = (partner >= 0) & (partner < row_count)
    partner = np.clip(partner, 0, row_count - 1)
    present = jnp.asarray(present_rows).reshape(row_count, 1, 1, 1, 1)
    queries = to_windows(qkv[..., :head_size], offset, WIN)
    key_own = to_windows(qkv[..., head_size:2 * head_size], offset, WIN)
    value_own = to_windows(qkv[..., 2 * head_size:], offset, WIN)
    score_scale = head_size ** (-0.5)
    mixture, prob_own, prob_partner = window_attend(queries, key_own, value_own, key_own[partner], value_own[partner], present, score_scale)
    fine_heads = from_windows(mixture, offset, levels)
    resid = hidden + contract('tvxhe,hed->tvxd', fine_heads, fine_out)
    merged = pack_quads(resid)
    merged_norm = normalize(merged, gain_merge).astype(jnp.bfloat16)
    coarse = contract('tvxm,mc->tvxc', merged_norm, merge_weight).astype(jnp.bfloat16)
    coarse_wide = coarse.astype(jnp.float32)
    coarse_norm = normalize(coarse_wide, gain_coarse).astype(jnp.bfloat16)
    cqkv = contract('tvxc,che->tvxhe', coarse_norm, coarse_qkv).astype(jnp.bfloat16)
    coarse_partner = np.arange(row_count // 2) ^ 1
    coarse_queries = to_windows(cqkv[..., :coarse_head], 0, WIN)
    coarse_keys = to_windows(cqkv[..., coarse_head:2 * coarse_head], 0, WIN)
    coarse_values = to_windows(cqkv[..., 2 * coarse_head:], 0, WIN)
    coarse_scale = coarse_head ** (-0.5)
    coarse_mix, coarse_own, coarse_other = window_attend(coarse_queries, coarse_keys, coarse_values, coarse_keys[coarse_partner], coarse_values[coarse_partner], True, coarse_scale)
    coarse_heads = from_windows(coarse_mix, 0, levels)
    lifted = (coarse_wide + contract('tvxhe,hec->tvxc', coarse_heads, coarse_out)).astype(jnp.bfloat16)
    upsampled = contract('tvxc,cu->tvxu', lifted, up_weight).astype(jnp.bfloat16)
    next_fields = (resid + unpack_quads(upsampled).astype(jnp.float32)).astype(jnp.bfloat16)
    grad_up = pack_quads(cotangent)
    grad_lift = contract('tvxu,cu->tvxc', grad_up, up_weight).astype(jnp.bfloat16)
    grad_cheads = contract('tvxc,hec->tvxhe', grad_lift, coarse_out).astype(jnp.bfloat16)
    coarse_terms = window_back(coarse_queries, coarse_keys, coarse_values, coarse_keys[coarse_partner], coarse_values[coarse_partner], coarse_own, coarse_other, to_windows(grad_cheads, 0, WIN), coarse_scale)
    grad_cqkv = from_windows(jnp.concatenate(coarse_terms[:3], axis=-1), 0, levels).astype(jnp.bfloat16)
    grad_ckv = from_windows(jnp.concatenate(coarse_terms[3:], axis=-1), 0, levels).astype(jnp.bfloat16)
    grad_cnorm = contract('tvxhe,che->tvxc', grad_cqkv, coarse_qkv)
    grad_cnorm = grad_cnorm + contract('tvxhe,che->tvxc', grad_ckv[coarse_partner], coarse_qkv[..., coarse_head:])
    grad_coarse = (grad_lift.astype(jnp.float32) + normalize_back(coarse_wide, gain_coarse, grad_cnorm)).astype(jnp.bfloat16)
    merge_weight_grad = contract('tvxm,tvxc->mc', merged_norm, grad_coarse) * norm_scale
    grad_mnorm = contract('tvxc,mc->tvxm', grad_coarse, merge_weight)
    grad_merged = normalize_back(merged, gain_merge, grad_mnorm)
    grad_resid = (cotangent.astype(jnp.float32) + unpack_quads(grad_merged)).astype(jnp.bfloat16)
    grad_heads = contract('tvxd,hed->tvxhe', grad_resid, fine_out).astype(jnp.bfloat16)
    fine_terms = window_back(queries, key_own, value_own, key_own[partner], value_own[partner], prob_own, prob_partner, to_windows(grad_heads, offset, WIN), score_scale)
    grad_qkv = from_windows(jnp.concatenate(fine_terms[:3], axis=-1), offset, levels).astype(jnp.bfloat16)
    grad_kv = from_windows(jnp.concatenate(fine_terms[3:], axis=-1), offset, levels).astype(jnp.bfloat16)
    grad_kv = jnp.where(present, grad_kv, jnp.zeros_like(grad_kv))
    moved_kv = jnp.where(present, grad_kv[partner], jnp.zeros_like(grad_kv))
    grad_norm = contract('tvxhe,dhe->tvxd', grad_qkv, fine_qkv)
    grad_norm = grad_norm + contract('tvxhe,dhe->tvxd', moved_kv, fine_qkv[..., head_size:])
    fine_qkv_grad = contract('tvxd,tvxhe->dhe', normed, grad_qkv)
    fine_qkv_grad = (fine_qkv_grad + widen_keys(contract('tvxd,tvxhe->dhe', normed, moved_kv), head_size)) * norm_scale
    fields_grad = (grad_resid.astype(jnp.float32) + normalize_back(hidden, gain_fine, grad_norm)).astype(jnp.bfloat16)
    return (next_fields, fields_grad, fine_qkv_grad, merge_weight_grad)
```

```python
import functools

import jax
import jax.numpy as jnp
from jax import lax
from jax.experimental import pallas as pl
from jax.experimental.pallas import tpu as pltpu
from jax.sharding import PartitionSpec as P

MESH = pl.DeviceIdType.MESH
F32 = jnp.float32
BF16 = jnp.bfloat16
EPSILON = 1e-05
NEGATIVE = -1e30

D = 512
DC = 1024
LEV = 4
LON = 64
ZH = 2
YS = 4
TP = ZH * YS
ROW = LEV * LON
CTOK = ROW // 2
SHARE = ROW // TP
CSHARE = CTOK // TP
SCALE = 0.125


def dot(a, b):
    return lax.dot_general(a, b, (((1,), (0,)), ((), ())), preferred_element_type=F32)


def dot_nt(a, b):
    return lax.dot_general(a, b, (((1,), (1,)), ((), ())), preferred_element_type=F32)


def dot_tn(a, b):
    return lax.dot_general(a, b, (((0,), (0,)), ((), ())), preferred_element_type=F32)


def normalize(values, gain):
    centred = values - jnp.mean(values, axis=-1, keepdims=True)
    spread = jnp.mean(centred * centred, axis=-1, keepdims=True)
    return centred * lax.rsqrt(spread + EPSILON) * gain


def normalize_back(values, gain, incoming):
    centred = values - jnp.mean(values, axis=-1, keepdims=True)
    spread = jnp.mean(centred * centred, axis=-1, keepdims=True)
    inverse = lax.rsqrt(spread + EPSILON)
    unit = centred * inverse
    inner = incoming * gain
    first = jnp.mean(inner, axis=-1, keepdims=True)
    second = jnp.mean(inner * unit, axis=-1, keepdims=True)
    return inverse * (inner - first - unit * second)


class Links:
    def __init__(self, send_sems, recv_sems):
        self.send_sems, self.recv_sems = send_sems, recv_sems
        self.copies = []

    def copy(self, src, dst, device):
        at = len(self.copies)
        made = pltpu.make_async_remote_copy(
            src_ref=src,
            dst_ref=dst,
            send_sem=self.send_sems.at[at],
            recv_sem=self.recv_sems.at[at],
            device_id=device,
            device_id_type=MESH,
        )
        self.copies.append(made)
        return made

    def finish(self):
        for made in self.copies:
            made.wait_send()


class Group:
    def __init__(self, links):
        self.links = links
        self.tp = lax.axis_index("tp")
        self.zh, self.y = lax.div(self.tp, YS), lax.rem(self.tp, YS)
        self.other = lax.rem(self.tp + YS, TP)

    def y_at(self, k):
        return lax.rem(self.y + k, YS)

    def along_y(self, k):
        return {"tp": self.zh * YS + self.y_at(k)}


class Gather:
    def __init__(self, group, view):
        links = group.links
        own, far = view(group.tp), view(group.other)
        self.over_z = links.copy(own, own, {"tp": group.other})
        self.over_y = [links.copy(own, own, group.along_y(k)) for k in range(1, YS)]
        self.passed = [links.copy(far, far, group.along_y(k)) for k in range(1, YS)]

    def start(self):
        for made in [self.over_z] + self.over_y:
            made.start()

    def forward(self):
        self.over_z.wait_recv()
        for made in self.passed:
            made.start()

    def finish(self):
        for made in self.over_y + self.passed:
            made.wait_recv()


class Scatter:
    def __init__(self, group, terms, came_y, half, came_z):
        self.group, self.terms = group, terms
        self.came_y, self.half, self.came_z = came_y, half, came_z
        links = group.links
        self.over_y = [
            links.copy(terms.at[:, group.y_at(k)], came_y.at[k - 1], group.along_y(k))
            for k in range(1, YS)
        ]
        self.over_z = links.copy(half, came_z, {"tp": group.other})

    def start(self):
        for made in self.over_y:
            made.start()

    def summed(self, zh):
        total = self.terms[zh, self.group.y].astype(F32)
        for k in range(YS - 1):
            total = total + self.came_y[k, zh].astype(F32)
        return total

    def middle(self):
        for made in self.over_y:
            made.wait_recv()
        self.half[...] = self.summed(1 - self.group.zh).astype(BF16)
        self.over_z.start()

    def finish(self):
        own = self.summed(self.group.zh)
        self.over_z.wait_recv()
        return own + self.came_z[...].astype(F32)


class Exchange:
    def __init__(self, group, source, target):
        self.copies = []
        for k in range(1, TP):
            peer = lax.rem(group.tp + k, TP)
            self.copies.append(group.links.copy(source(peer), target(group.tp), {"tp": peer}))

    def start(self):
        for made in self.copies:
            made.start()

    def finish(self):
        for made in self.copies:
            made.wait_recv()


def aligned(index, size):
    return pl.ds(pl.multiple_of(index * size, size), size)


def put(ref, rows, values):
    for j in range(values.shape[1] // 128):
        ref[j, rows, :] = values[:, 128 * j : 128 * j + 128]


def get(ref, rows):
    return jnp.concatenate([ref[j, rows, :] for j in range(ref.shape[0])], axis=1)


def softmax_pair(own, other):
    largest = jnp.maximum(
        jnp.max(own, axis=-1, keepdims=True), jnp.max(other, axis=-1, keepdims=True)
    )
    own, other = jnp.exp(own - largest), jnp.exp(other - largest)
    total = jnp.sum(own, axis=-1, keepdims=True) + jnp.sum(other, axis=-1, keepdims=True)
    return own / total, other / total


def score_grads(prob_own, prob_other, grad_own, grad_other):
    mean = jnp.sum(grad_own * prob_own, axis=-1, keepdims=True)
    mean = mean + jnp.sum(grad_other * prob_other, axis=-1, keepdims=True)
    return (
        (prob_own * (grad_own - mean) * SCALE).astype(BF16),
        (prob_other * (grad_other - mean) * SCALE).astype(BF16),
    )


def low_lanes(values):
    lane = lax.broadcasted_iota(jnp.int32, values.shape, 1)
    return jnp.where(lane < 64, values, 0.0)


def high_lanes(values):
    lane = lax.broadcasted_iota(jnp.int32, values.shape, 1)
    return jnp.where(lane >= 64, values, 0.0)


def fine_mask(start):
    def window(index):
        return ((index >> 5) + 7 + ((index & 7) >> 2)) & 7

    query = lax.broadcasted_iota(jnp.int32, (CTOK, ROW), 0) + start
    key = lax.broadcasted_iota(jnp.int32, (CTOK, ROW), 1)
    return window(query) == window(key)


def main_kernel(
    lat_count,
    fields,
    classes,
    class_table,
    gain_fine,
    fine_w,
    fine_out,
    gain_merge,
    merge_weight,
    gain_coarse,
    coarse_w,
    coarse_out,
    up_weight,
    cotangent,
    next_fields,
    fields_grad,
    terms,
    send_sems,
    recv_sems,
    hid,
    cotf,
    normed,
    queries,
    keys,
    keys_sent,
    keys_came,
    prob_own,
    prob_other,
    mixture,
    heads_all,
    wexp,
    cexp,
    resid,
    merged_norm,
    coarse_all,
    coarse_f,
    lift_all,
    lift_terms,
    lift_y,
    lift_half,
    lift_z,
    ckeys,
    ckeys_came,
    cback,
    cback_came,
    cs_terms,
    cs_y,
    cs_half,
    cs_z,
    cn_terms,
    cn_y,
    cn_half,
    cn_z,
    grad_chunk,
    grad_columns,
    lifted_all,
    mn_terms,
    mn_y,
    mn_half,
    mn_z,
    up_all,
    up_wide,
    grad_mix,
    grad_mix_send,
    grad_mix_all,
    grad_mix_rows,
    grad_resid,
    grad_q,
    grad_kv,
    grad_other,
    back,
    back_came,
    gn_terms,
    gn_y,
    gn_half,
    gn_z,
):
    links = Links(send_sems, recv_sems)
    group = Group(links)
    tp = group.tp
    lat = lax.axis_index("lat")
    before, after = lax.rem(lat + lat_count - 1, lat_count), lax.rem(lat + 1, lat_count)
    twin = lat + 1 - 2 * lax.rem(lat, 2)

    barrier = pltpu.get_barrier_semaphore()
    for k in range(1, TP):
        pl.semaphore_signal(
            barrier, inc=1, device_id={"tp": lax.rem(tp + k, TP)}, device_id_type=MESH
        )
    for peer in (before, after):
        pl.semaphore_signal(barrier, inc=1, device_id={"lat": peer}, device_id_type=MESH)

    blank = jnp.zeros((TP, 64, D), BF16)
    wexp[:, 0:64] = blank
    wexp[:, 128:192] = blank
    wexp[tp, 64:128] = fine_out[...]
    for head in range(2):
        cexp[head, 0:64] = jnp.zeros((64, DC), BF16)
        cexp[head, 64:128] = coarse_out[64 * head : 64 * head + 64]

    gather_w = Gather(group, lambda at: wexp.at[at, pl.ds(64, 64)])
    lift = Scatter(group, lift_terms, lift_y, lift_half, lift_z)
    send_keys = [
        links.copy(keys_sent.at[1], keys_came.at[0], {"lat": after}),
        links.copy(keys_sent.at[0], keys_came.at[1], {"lat": before}),
    ]
    gather_heads = Gather(group, lambda at: heads_all.at[:, aligned(at, 128)])
    gather_lift = Gather(group, lambda at: lift_all.at[aligned(at, CSHARE)])
    gather_coarse = Gather(group, lambda at: coarse_all.at[:, aligned(at, 128)])
    send_ckeys = links.copy(ckeys, ckeys_came, {"lat": twin})
    send_cback = links.copy(cback, cback_came, {"lat": twin})
    csum = Scatter(group, cs_terms, cs_y, cs_half, cs_z)
    cnorm = Scatter(group, cn_terms, cn_y, cn_half, cn_z)
    columns = Exchange(
        group,
        lambda at: grad_chunk.at[:, aligned(at, 128)],
        lambda at: grad_columns.at[aligned(at, CSHARE)],
    )
    gather_lifted = Gather(group, lambda at: lifted_all.at[aligned(at, CSHARE)])
    mnorm = Scatter(group, mn_terms, mn_y, mn_half, mn_z)
    gather_up = Gather(group, lambda at: up_all.at[at])
    mix = Exchange(
        group,
        lambda at: grad_mix_send.at[:, aligned(at, 128)],
        lambda at: grad_mix_all.at[aligned(at, SHARE)],
    )
    send_back = [
        links.copy(back.at[0], back_came.at[1], {"lat": before}),
        links.copy(back.at[1], back_came.at[0], {"lat": after}),
    ]
    gnorm = Scatter(group, gn_terms, gn_y, gn_half, gn_z)

    embedded = []
    for r in range(2):
        kinds = lax.broadcasted_iota(jnp.int32, (LON, 8), 1)
        onehot = jnp.where(classes[r] == kinds, 1.0, 0.0).astype(BF16)
        embedded.append(dot(onehot, class_table[...]))
    for r in range(2):
        for level in range(LEV):
            full = fields[r, level].astype(F32) + embedded[r]
            cots = cotangent[r, level].astype(F32)
            for block in range(TP):
                at = r * ROW + block * SHARE + level * 8
                hid[at : at + 8] = full[8 * block : 8 * block + 8]
                put(cotf, pl.ds(at, 8), cots[8 * block : 8 * block + 8])

    for i in range(4):
        chunk = pl.ds(i * 128, 128)
        normed[chunk] = normalize(hid[chunk], gain_fine[...]).astype(BF16)
    for r in range(2):
        rows = pl.ds(r * ROW, ROW)
        both = dot(normed[rows], fine_w[...])
        queries[rows] = both[:, 0:128].astype(BF16)
        kv = both[:, 128:256].astype(BF16)
        keys[r] = kv
        keys_sent[r] = kv

    pl.semaphore_wait(barrier, TP + 1)
    for made in send_keys:
        made.start()
    gather_w.start()

    kind = lax.div(tp, 2)
    quad = get(cotf, pl.ds(lax.div(kind, 2) * ROW + lax.rem(kind, 2), CTOK, stride=2))
    quad = jnp.where(lax.rem(tp, 2) == 0, quad[:, 0:256], quad[:, 256:512]).astype(BF16)
    lift_terms[...] = dot_nt(quad, up_weight[...]).astype(BF16).reshape(ZH, YS, CSHARE, DC)
    lift.start()

    for made in send_keys:
        made.wait_recv()
    gather_w.forward()

    present = (lat > 0, lat < lat_count - 1)

    def attend(r, half):
        start = r * ROW + half * CTOK
        chunk = pl.ds(start, CTOK)
        mask = fine_mask(half * CTOK)
        query = queries[chunk]
        own = jnp.where(mask, dot_nt(query, keys[r]) * SCALE, NEGATIVE)
        far = dot_nt(query, keys_came[r]) * SCALE
        far = jnp.where(jnp.logical_and(mask, present[r]), far, NEGATIVE)
        own, far = softmax_pair(own, far)
        prob_own[chunk] = own
        prob_other[chunk] = far
        mixture[chunk] = dot(own.astype(BF16), keys[r]) + dot(far.astype(BF16), keys_came[r])

    for r in range(2):
        for half in range(2):
            attend(r, half)
    lane = lax.broadcasted_iota(jnp.int32, (ROW, 128), 1)
    packed = jnp.where(lane < 64, pltpu.roll(mixture[ROW : 2 * ROW], 64, 1), mixture[0:ROW])
    heads_all[:, aligned(tp, 128)] = packed.astype(BF16)
    gather_heads.start()

    lift.middle()
    gather_w.finish()
    gather_heads.forward()
    lift_chunk = lift.finish().astype(BF16)
    lift_all[aligned(tp, CSHARE)] = lift_chunk
    gather_lift.start()
    gather_heads.finish()

    for r in range(2):
        first = 64 if r == 1 else 0
        weight = wexp[:, first : first + 128].reshape(TP * 128, D)
        rows = pl.ds(r * ROW, ROW)
        put(resid, rows, hid[rows] + dot(heads_all[...], weight))

    merged = [get(resid, pl.ds(r * ROW + s, CTOK, stride=2)) for r in range(2) for s in range(2)]
    merged = jnp.concatenate(merged, axis=1)
    merged_norm[...] = normalize(merged, gain_merge[...]).astype(BF16)
    coarse_all[:, aligned(tp, 128)] = dot(merged_norm[...], merge_weight[...]).astype(BF16)
    gather_coarse.start()
    gather_lift.forward()
    gather_coarse.forward()
    gather_lift.finish()
    grad_cmix = [dot_nt(lift_all[...], cexp[head]).astype(BF16) for head in range(2)]
    gather_coarse.finish()

    coarse_f[...] = coarse_all[...].astype(F32)
    cnormed = normalize(coarse_f[...], gain_coarse[...]).astype(BF16)
    cqkv = dot(cnormed, coarse_w[...]).astype(BF16)
    cq = [cqkv[:, 256 * head : 256 * head + 128] for head in range(2)]
    for head in range(2):
        ckeys[head] = cqkv[:, 256 * head + 128 : 256 * head + 256]
    send_ckeys.start()

    row_at = lax.broadcasted_iota(jnp.int32, (CTOK, CTOK), 0)
    col_at = lax.broadcasted_iota(jnp.int32, (CTOK, CTOK), 1)
    cmask = (row_at >> 5) == (col_at >> 5)
    own_scores = [
        jnp.where(cmask, dot_nt(cq[head], ckeys[head]) * SCALE, NEGATIVE) for head in range(2)
    ]
    send_ckeys.wait_recv()
    cgrad_q, cgrad_kv = [], []
    cheads = []
    for head in range(2):
        far = jnp.where(cmask, dot_nt(cq[head], ckeys_came[head]) * SCALE, NEGATIVE)
        own, far = softmax_pair(own_scores[head], far)
        own16, far16 = own.astype(BF16), far.astype(BF16)
        grad_own = dot_nt(grad_cmix[head], ckeys[head])
        grad_far = dot_nt(grad_cmix[head], ckeys_came[head])
        ds_own, ds_far = score_grads(own, far, grad_own, grad_far)
        cback[head] = (dot_tn(ds_far, cq[head]) + dot_tn(far16, grad_cmix[head])).astype(BF16)
        cgrad_kv.append(dot_tn(ds_own, cq[head]) + dot_tn(own16, grad_cmix[head]))
        query_grad = dot(ds_own, ckeys[head]) + dot(ds_far, ckeys_came[head])
        cgrad_q.append(low_lanes(query_grad).astype(BF16))
        cheads.append((dot(own16, ckeys[head]) + dot(far16, ckeys_came[head])).astype(BF16))
    send_cback.start()
    part = dot(cheads[0], cexp[0]) + dot(cheads[1], cexp[1])
    cs_terms[...] = part.astype(BF16).reshape(ZH, YS, CSHARE, DC)
    csum.start()
    part = dot_nt(cgrad_q[0], coarse_w[:, 0:128]) + dot_nt(cgrad_q[1], coarse_w[:, 256:384])
    send_cback.wait_recv()
    for head in range(2):
        total = (cgrad_kv[head] + cback_came[head].astype(F32)).astype(BF16)
        part = part + dot_nt(total, coarse_w[:, 256 * head + 128 : 256 * head + 256])
    cn_terms[...] = part.astype(BF16).reshape(ZH, YS, CSHARE, DC)
    cnorm.start()
    csum.middle()
    cnorm.middle()

    mine = aligned(tp, CSHARE)
    coarse_chunk = coarse_f[mine]
    grad_cn = cnorm.finish()
    grad_chunk[...] = (
        lift_chunk.astype(F32) + normalize_back(coarse_chunk, gain_coarse[...], grad_cn)
    ).astype(BF16)
    columns.start()
    grad_columns[mine] = grad_chunk[:, aligned(tp, 128)]
    lifted_all[mine] = (coarse_chunk + csum.finish()).astype(BF16)
    gather_lifted.start()
    columns.finish()
    part = dot_nt(grad_columns[...], merge_weight[...])
    mn_terms[...] = part.astype(BF16).reshape(ZH, YS, CSHARE, 4 * D)
    mnorm.start()

    scale = (2 * lat_count * LEV * LON) ** -0.5
    merge_rows = 4 * D // lat_count
    weight_rows = D // lat_count
    term = dot_tn(merged_norm[...], grad_columns[...]) * scale
    terms[:, 0:merge_rows] = term.astype(BF16).reshape(lat_count, merge_rows, 128)
    gather_lifted.forward()
    mnorm.middle()
    gather_lifted.finish()
    up_all[tp] = dot(lifted_all[...], up_weight[...]).astype(BF16)
    gather_up.start()

    grad_mn = mnorm.finish()
    merged_chunk, cot_chunk = [], []
    for r in range(2):
        for s in range(2):
            some = pl.ds(r * ROW + s + tp * SHARE, CSHARE, stride=2)
            merged_chunk.append(get(resid, some))
            cot_chunk.append(get(cotf, some))
    merged_chunk = jnp.concatenate(merged_chunk, axis=1)
    cot_chunk = jnp.concatenate(cot_chunk, axis=1)
    grad_merged = normalize_back(merged_chunk, gain_merge[...], grad_mn)
    grad_quads = (cot_chunk + grad_merged).astype(BF16)
    low = wexp[:, 0:128].reshape(TP * 128, D)
    high = wexp[:, 64:192].reshape(TP * 128, D)
    for s in range(2):
        top = grad_quads[:, s * D : (s + 1) * D]
        bottom = grad_quads[:, (2 + s) * D : (3 + s) * D]
        put(grad_mix, pl.ds(s, CSHARE, stride=2), dot_nt(top, low) + dot_nt(bottom, high))
        put(grad_resid, pl.ds(s, CSHARE, stride=2), top.astype(F32))
        put(grad_resid, pl.ds(SHARE + s, CSHARE, stride=2), bottom.astype(F32))
    grad_mix_send[...] = get(grad_mix, pl.ds(0, SHARE)).astype(BF16)
    mix.start()
    grad_mix_all[aligned(tp, SHARE)] = grad_mix_send[:, aligned(tp, 128)]
    gather_up.forward()
    mix.finish()

    both = grad_mix_all[...].astype(F32)
    grad_mix_rows[0:ROW] = high_lanes(both).astype(BF16)
    grad_mix_rows[ROW : 2 * ROW] = high_lanes(pltpu.roll(both, 64, 1)).astype(BF16)

    def attend_back(r, half):
        chunk = pl.ds(r * ROW + half * CTOK, CTOK)
        query, grad_out = queries[chunk], grad_mix_rows[chunk]
        own, far = prob_own[chunk], prob_other[chunk]
        ds_own, ds_far = score_grads(
            own, far, dot_nt(grad_out, keys[r]), dot_nt(grad_out, keys_came[r])
        )
        own16, far16 = own.astype(BF16), far.astype(BF16)
        to_own = dot_tn(ds_own, query) + dot_tn(own16, grad_out)
        to_far = dot_tn(ds_far, query) + dot_tn(far16, grad_out)
        grad_q[chunk] = low_lanes(dot(ds_own, keys[r]) + dot(ds_far, keys_came[r])).astype(BF16)
        return to_own, to_far

    for r in range(2):
        own_a, far_a = attend_back(r, 0)
        own_b, far_b = attend_back(r, 1)
        back[r] = (far_a + far_b).astype(BF16)
        send_back[r].start()
        grad_other[r] = own_a + own_b
    for made in send_back:
        made.wait_recv()
    for r in range(2):
        grad_kv[pl.ds(r * ROW, ROW)] = (grad_other[r] + back_came[r].astype(F32)).astype(BF16)
    for r in range(2):
        rows = pl.ds(r * ROW, ROW)
        part = dot_nt(grad_q[rows], fine_w[:, 0:128]) + dot_nt(grad_kv[rows], fine_w[:, 128:256])
        gn_terms[:, :, r] = part.astype(BF16).reshape(ZH, YS, SHARE, D)
    gnorm.start()

    term_q = dot_tn(normed[...], grad_q[...]) * scale
    term_kv = dot_tn(normed[...], grad_kv[...]) * scale
    term = jnp.concatenate(
        [term_q.reshape(lat_count, weight_rows, 128), term_kv.reshape(lat_count, weight_rows, 128)],
        axis=1,
    )
    terms[:, merge_rows : merge_rows + 2 * weight_rows] = term.astype(BF16)
    gnorm.middle()

    gather_up.finish()
    for r in range(2):
        for s in range(2):
            for part in range(2):
                wide = up_all[4 * r + 2 * s + part].astype(F32)
                some = pl.ds(r * ROW + s, CTOK, stride=2)
                up_wide[2 * part, some, :] = wide[:, 0:128]
                up_wide[2 * part + 1, some, :] = wide[:, 128:256]
    for r in range(2):
        for level in range(LEV):
            pieces = []
            for block in range(TP):
                at = r * ROW + block * SHARE + level * 8
                pieces.append(get(resid, pl.ds(at, 8)) + get(up_wide, pl.ds(at, 8)))
            next_fields[r, level] = jnp.concatenate(pieces, axis=0).astype(BF16)

    grad_norm = gnorm.finish()
    for r in range(2):
        own_hidden = hid[pl.ds(pl.multiple_of(r * ROW + tp * SHARE, SHARE), SHARE)]
        grad_hidden = normalize_back(own_hidden, gain_fine[...], grad_norm[r])
        grad_hidden = grad_hidden + get(grad_resid, pl.ds(r * SHARE, SHARE))
        fields_grad[r] = grad_hidden.astype(BF16)
    links.finish()


def lat_kernel(
    lat_count, nx, nz, terms, out, send_sems, recv_sems, came_c, part_x, came_x, part_z, came_z
):
    links = Links(send_sems, recv_sems)
    lat = lax.axis_index("lat")
    core = lax.rem(lat, 2)
    z = lax.rem(lax.div(lat, 2), nz)
    x = lax.div(lat, 2 * nz)

    def place(x_at, z_at, core_at):
        return {"lat": (x_at * nz + z_at) * 2 + core_at}

    def x_at(k):
        return lax.rem(x + k, nx)

    def z_at(k):
        return lax.rem(z + k, nz)

    twin = place(x, z, 1 - core)
    x_peers = [place(x_at(k), z, core) for k in range(1, nx)]
    z_peers = [place(x, z_at(k), core) for k in range(1, nz)]
    barrier = pltpu.get_barrier_semaphore()
    for peer in [twin] + x_peers + z_peers:
        pl.semaphore_signal(barrier, inc=1, device_id=peer, device_id_type=MESH)
    pl.semaphore_wait(barrier, 1 + len(x_peers) + len(z_peers))

    over_core = links.copy(terms.at[:, :, 1 - core], came_c, twin)
    over_core.start()
    over_core.wait_recv()
    for i in range(nx):
        part_x[i] = (terms[i, :, core].astype(F32) + came_c[i].astype(F32)).astype(BF16)
    over_x = [
        links.copy(part_x.at[x_at(k)], came_x.at[k - 1], x_peers[k - 1]) for k in range(1, nx)
    ]
    for made in over_x:
        made.start()
    total = part_x[x].astype(F32)
    for k in range(1, nx):
        over_x[k - 1].wait_recv()
        total = total + came_x[k - 1].astype(F32)
    part_z[...] = total.astype(BF16)
    over_z = [
        links.copy(part_z.at[z_at(k)], came_z.at[k - 1], z_peers[k - 1]) for k in range(1, nz)
    ]
    for made in over_z:
        made.start()
    total = part_z[z].astype(F32)
    for k in range(1, nz):
        over_z[k - 1].wait_recv()
        total = total + came_z[k - 1].astype(F32)
    out[...] = total
    links.finish()


def vmem(*shape, kind=BF16):
    return pltpu.VMEM(shape, kind)


def scatter_buffers(*chunk):
    return [vmem(ZH, YS, *chunk), vmem(YS - 1, ZH, *chunk), vmem(*chunk), vmem(*chunk)]


def split_heads(weight):
    query, rest = weight[..., :64], weight[..., 64:]
    wide = jnp.concatenate([query, jnp.zeros_like(query), rest], axis=-1)
    return wide.reshape(weight.shape[0], -1)


def local(
    lat_count,
    fields,
    classes,
    class_table,
    gain_fine,
    fine_qkv,
    fine_out,
    gain_merge,
    merge_weight,
    gain_coarse,
    coarse_qkv,
    coarse_out,
    up_weight,
    cotangent,
):
    block_rows = 4 * D // lat_count + 2 * (D // lat_count)
    nz = min(8, lat_count // 4)
    nx = lat_count // (2 * nz)
    whole = pl.BlockSpec(memory_space=pltpu.VMEM)
    copies = 120
    scratch = [
        pltpu.SemaphoreType.DMA((copies,)),
        pltpu.SemaphoreType.DMA((copies,)),
        vmem(2 * ROW, D, kind=F32),
        vmem(4, 2 * ROW, 128, kind=F32),
        vmem(2 * ROW, D),
        vmem(2 * ROW, 128),
        vmem(2, ROW, 128),
        vmem(2, ROW, 128),
        vmem(2, ROW, 128),
        vmem(2 * ROW, ROW, kind=F32),
        vmem(2 * ROW, ROW, kind=F32),
        vmem(2 * ROW, 128, kind=F32),
        vmem(ROW, TP * 128),
        vmem(TP, 192, D),
        vmem(2, 128, DC),
        vmem(4, 2 * ROW, 128, kind=F32),
        vmem(CTOK, 4 * D),
        vmem(CTOK, DC),
        vmem(CTOK, DC, kind=F32),
        vmem(CTOK, DC),
        *scatter_buffers(CSHARE, DC),
        vmem(2, CTOK, 128),
        vmem(2, CTOK, 128),
        vmem(2, CTOK, 128),
        vmem(2, CTOK, 128),
        *scatter_buffers(CSHARE, DC),
        *scatter_buffers(CSHARE, DC),
        vmem(CSHARE, DC),
        vmem(CTOK, 128),
        vmem(CTOK, DC),
        *scatter_buffers(CSHARE, 4 * D),
        vmem(TP, CTOK, 256),
        vmem(4, 2 * ROW, 128, kind=F32),
        vmem(TP, SHARE, 128, kind=F32),
        vmem(SHARE, TP * 128),
        vmem(ROW, 128),
        vmem(2 * ROW, 128),
        vmem(4, 2 * SHARE, 128, kind=F32),
        vmem(2 * ROW, 128),
        vmem(2 * ROW, 128),
        vmem(2, ROW, 128, kind=F32),
        vmem(2, ROW, 128),
        vmem(2, ROW, 128),
        *scatter_buffers(2, SHARE, D),
    ]
    next_fields, fields_grad, terms = pl.pallas_call(
        functools.partial(main_kernel, lat_count),
        out_shape=(
            jax.ShapeDtypeStruct((2, LEV, LON, D), BF16),
            jax.ShapeDtypeStruct((2, SHARE, D), BF16),
            jax.ShapeDtypeStruct((lat_count, block_rows, 128), BF16),
        ),
        in_specs=[whole] * 13,
        out_specs=[whole] * 3,
        scratch_shapes=scratch,
        compiler_params=pltpu.CompilerParams(
            collective_id=0, has_side_effects=True, vmem_limit_bytes=56 * 2**20
        ),
    )(
        fields,
        classes.reshape(2, LON, 1),
        class_table,
        gain_fine.reshape(1, -1),
        split_heads(fine_qkv),
        fine_out.reshape(64, D),
        gain_merge.reshape(1, -1),
        merge_weight,
        gain_coarse.reshape(1, -1),
        split_heads(coarse_qkv),
        coarse_out.reshape(128, DC),
        up_weight,
        cotangent,
    )
    sums = pl.pallas_call(
        functools.partial(lat_kernel, lat_count, nx, nz),
        out_shape=jax.ShapeDtypeStruct((block_rows, 128), F32),
        in_specs=[whole],
        out_specs=whole,
        scratch_shapes=[
            pltpu.SemaphoreType.DMA((nx + nz,)),
            pltpu.SemaphoreType.DMA((nx + nz,)),
            vmem(nx, nz, block_rows, 128),
            vmem(nx, nz, block_rows, 128),
            vmem(nx - 1, nz, block_rows, 128),
            vmem(nz, block_rows, 128),
            vmem(nz - 1, block_rows, 128),
        ],
        compiler_params=pltpu.CompilerParams(collective_id=1, has_side_effects=True),
    )(terms.reshape(nx, nz, 2, block_rows, 128))
    merge_rows, weight_rows = 4 * D // lat_count, D // lat_count
    query_rows = sums[merge_rows : merge_rows + weight_rows, :64]
    weight_grad = jnp.concatenate([query_rows, sums[merge_rows + weight_rows :]], axis=-1)
    return (
        next_fields,
        fields_grad.reshape(2, LEV, LON // TP, D),
        weight_grad.reshape(weight_rows, 1, 192),
        sums[:merge_rows],
    )


def solution(mesh):
    placed = (
        P("lat", None, None, None),
        P("lat", None),
        P(),
        P(),
        P(None, "tp", None),
        P("tp", None, None),
        P(),
        P(None, "tp"),
        P(),
        P(None, "tp", None),
        P("tp", None, None),
        P(None, "tp"),
        P("lat", None, None, None),
    )
    return jax.shard_map(
        functools.partial(local, mesh.shape["lat"]),
        mesh=mesh,
        in_specs=placed,
        out_specs=(
            P("lat", None, None, None),
            P("lat", None, "tp", None),
            P("lat", "tp", None),
            P("lat", "tp"),
        ),
        check_vma=False,
    )
```

```python
import functools

import jax
import jax.numpy as jnp
from jax import lax
from jax.experimental import pallas as pl
from jax.experimental.pallas import tpu as pltpu
from jax.sharding import PartitionSpec as P

MESH = pl.DeviceIdType.MESH
F32 = jnp.float32
BF16 = jnp.bfloat16
EPSILON = 1e-05
NEGATIVE = -1e30

D = 512
DC = 1024
LEV = 4
LON = 64
ZH = 2
YS = 4
TP = ZH * YS
ROW = LEV * LON
CTOK = ROW // 2
SHARE = ROW // TP
CSHARE = CTOK // TP
SCALE = 0.125


def dot(a, b):
    return lax.dot_general(a, b, (((1,), (0,)), ((), ())), preferred_element_type=F32)


def dot_nt(a, b):
    return lax.dot_general(a, b, (((1,), (1,)), ((), ())), preferred_element_type=F32)


def dot_tn(a, b):
    return lax.dot_general(a, b, (((0,), (0,)), ((), ())), preferred_element_type=F32)


def normalize(values, gain):
    centred = values - jnp.mean(values, axis=-1, keepdims=True)
    spread = jnp.mean(centred * centred, axis=-1, keepdims=True)
    return centred * lax.rsqrt(spread + EPSILON) * gain


def normalize_back(values, gain, incoming):
    centred = values - jnp.mean(values, axis=-1, keepdims=True)
    spread = jnp.mean(centred * centred, axis=-1, keepdims=True)
    inverse = lax.rsqrt(spread + EPSILON)
    unit = centred * inverse
    inner = incoming * gain
    first = jnp.mean(inner, axis=-1, keepdims=True)
    second = jnp.mean(inner * unit, axis=-1, keepdims=True)
    return inverse * (inner - first - unit * second)


class Links:
    def __init__(self, send_sems, recv_sems):
        self.send_sems, self.recv_sems = send_sems, recv_sems
        self.copies = []

    def copy(self, src, dst, device):
        at = len(self.copies)
        made = pltpu.make_async_remote_copy(
            src_ref=src,
            dst_ref=dst,
            send_sem=self.send_sems.at[at],
            recv_sem=self.recv_sems.at[at],
            device_id=device,
            device_id_type=MESH,
        )
        self.copies.append(made)
        return made

    def finish(self):
        for made in self.copies:
            made.wait_send()


class Group:
    def __init__(self, links):
        self.links = links
        self.tp = lax.axis_index("tp")
        self.zh, self.y = lax.div(self.tp, YS), lax.rem(self.tp, YS)
        self.other = lax.rem(self.tp + YS, TP)

    def y_at(self, k):
        return lax.rem(self.y + k, YS)

    def along_y(self, k):
        return {"tp": self.zh * YS + self.y_at(k)}


class Gather:
    def __init__(self, group, view):
        links = group.links
        own, far = view(group.tp), view(group.other)
        self.over_z = links.copy(own, own, {"tp": group.other})
        self.over_y = [links.copy(own, own, group.along_y(k)) for k in range(1, YS)]
        self.passed = [links.copy(far, far, group.along_y(k)) for k in range(1, YS)]

    def start(self):
        for made in [self.over_z] + self.over_y:
            made.start()

    def forward(self):
        self.over_z.wait_recv()
        for made in self.passed:
            made.start()

    def finish(self):
        for made in self.over_y + self.passed:
            made.wait_recv()


class Scatter:
    def __init__(self, group, terms, came_y, half, came_z):
        self.group, self.terms = group, terms
        self.came_y, self.half, self.came_z = came_y, half, came_z
        links = group.links
        self.over_y = [
            links.copy(terms.at[:, group.y_at(k)], came_y.at[k - 1], group.along_y(k))
            for k in range(1, YS)
        ]
        self.over_z = links.copy(half, came_z, {"tp": group.other})

    def start(self):
        for made in self.over_y:
            made.start()

    def summed(self, zh):
        total = self.terms[zh, self.group.y].astype(F32)
        for k in range(YS - 1):
            total = total + self.came_y[k, zh].astype(F32)
        return total

    def middle(self):
        for made in self.over_y:
            made.wait_recv()
        self.half[...] = self.summed(1 - self.group.zh).astype(BF16)
        self.over_z.start()

    def finish(self):
        own = self.summed(self.group.zh)
        self.over_z.wait_recv()
        return own + self.came_z[...].astype(F32)


class Exchange:
    def __init__(self, group, source, target):
        self.copies = []
        for k in range(1, TP):
            peer = lax.rem(group.tp + k, TP)
            self.copies.append(group.links.copy(source(peer), target(group.tp), {"tp": peer}))

    def start(self):
        for made in self.copies:
            made.start()

    def finish(self):
        for made in self.copies:
            made.wait_recv()


class LatSum:
    def __init__(self, links, place, terms, came_x, part, came_z):
        self.place, self.terms, self.came_x, self.part, self.came_z = (
            place,
            terms,
            came_x,
            part,
            came_z,
        )
        self.over_x = [
            links.copy(terms.at[x, :, core], came_x.at[k], place.at(x, place.z, core))
            for k, (x, core) in enumerate(place.x_peers)
        ]
        self.over_z = [
            links.copy(part.at[z], came_z.at[k], place.at(place.x, z, place.core))
            for k, z in enumerate(place.z_peers)
        ]

    def start(self):
        for made in self.over_x:
            made.start()

    def middle(self):
        for made in self.over_x:
            made.wait_recv()
        total = self.terms[self.place.x, :, self.place.core].astype(F32)
        for k in range(len(self.over_x)):
            total = total + self.came_x[k].astype(F32)
        self.part[...] = total.astype(BF16)
        for made in self.over_z:
            made.start()

    def finish(self):
        for made in self.over_z:
            made.wait_recv()
        total = self.part[self.place.z].astype(F32)
        for k in range(len(self.over_z)):
            total = total + self.came_z[k].astype(F32)
        return total


class Place:
    def __init__(self, nx, nz):
        lat = lax.axis_index("lat")
        self.nz = nz
        self.core = lax.rem(lat, 2)
        self.z = lax.rem(lax.div(lat, 2), nz)
        self.x = lax.div(lat, 2 * nz)
        self.x_peers = [
            (lax.rem(self.x + i, nx), lax.rem(self.core + j, 2))
            for i in range(nx)
            for j in range(2)
            if i or j
        ]
        self.z_peers = [lax.rem(self.z + k, nz) for k in range(1, nz)]

    def at(self, x, z, core):
        return {"lat": (x * self.nz + z) * 2 + core}


def aligned(index, size):
    return pl.ds(pl.multiple_of(index * size, size), size)


def put(ref, rows, values):
    for j in range(values.shape[1] // 128):
        ref[j, rows, :] = values[:, 128 * j : 128 * j + 128]


def get(ref, rows):
    return jnp.concatenate([ref[j, rows, :] for j in range(ref.shape[0])], axis=1)


def softmax_pair(own, other):
    largest = jnp.maximum(
        jnp.max(own, axis=-1, keepdims=True), jnp.max(other, axis=-1, keepdims=True)
    )
    own, other = jnp.exp(own - largest), jnp.exp(other - largest)
    total = jnp.sum(own, axis=-1, keepdims=True) + jnp.sum(other, axis=-1, keepdims=True)
    return own / total, other / total


def score_grads(prob_own, prob_other, grad_own, grad_other):
    mean = jnp.sum(grad_own * prob_own, axis=-1, keepdims=True)
    mean = mean + jnp.sum(grad_other * prob_other, axis=-1, keepdims=True)
    return (
        (prob_own * (grad_own - mean) * SCALE).astype(BF16),
        (prob_other * (grad_other - mean) * SCALE).astype(BF16),
    )


def low_lanes(values):
    lane = lax.broadcasted_iota(jnp.int32, values.shape, 1)
    return jnp.where(lane < 64, values, 0.0)


def high_lanes(values):
    lane = lax.broadcasted_iota(jnp.int32, values.shape, 1)
    return jnp.where(lane >= 64, values, 0.0)


def fine_mask(start):
    def window(index):
        return ((index >> 5) + 7 + ((index & 7) >> 2)) & 7

    query = lax.broadcasted_iota(jnp.int32, (CTOK, ROW), 0) + start
    key = lax.broadcasted_iota(jnp.int32, (CTOK, ROW), 1)
    return window(query) == window(key)


def main_kernel(
    lat_count,
    nx,
    nz,
    fields,
    classes,
    class_table,
    gain_fine,
    fine_w,
    fine_out,
    gain_merge,
    merge_weight,
    gain_coarse,
    coarse_w,
    coarse_out,
    up_weight,
    cotangent,
    next_fields,
    fields_grad,
    fine_grad,
    merge_grad,
    send_sems,
    recv_sems,
    hid,
    cotf,
    normed,
    queries,
    keys,
    keys_sent,
    keys_came,
    prob_own,
    prob_other,
    mixture,
    heads_all,
    wexp,
    cexp,
    resid,
    merged_norm,
    coarse_all,
    coarse_f,
    lift_all,
    lift_terms,
    lift_y,
    lift_half,
    lift_z,
    ckeys,
    ckeys_came,
    cback,
    cback_came,
    cs_terms,
    cs_y,
    cs_half,
    cs_z,
    cn_terms,
    cn_y,
    cn_half,
    cn_z,
    grad_chunk,
    grad_columns,
    lifted_all,
    mn_terms,
    mn_y,
    mn_half,
    mn_z,
    up_all,
    up_wide,
    grad_mix,
    grad_mix_send,
    grad_mix_all,
    grad_mix_rows,
    grad_resid,
    grad_q,
    grad_kv,
    grad_other,
    back,
    back_came,
    gn_terms,
    gn_y,
    gn_half,
    gn_z,
    mterms,
    mcame_x,
    mpart,
    mcame_z,
    fterms,
    fcame_x,
    fpart,
    fcame_z,
):
    links = Links(send_sems, recv_sems)
    group = Group(links)
    tp = group.tp
    lat = lax.axis_index("lat")
    before, after = lax.rem(lat + lat_count - 1, lat_count), lax.rem(lat + 1, lat_count)
    twin = lat + 1 - 2 * lax.rem(lat, 2)

    barrier = pltpu.get_barrier_semaphore()
    for k in range(1, TP):
        pl.semaphore_signal(
            barrier, inc=1, device_id={"tp": lax.rem(tp + k, TP)}, device_id_type=MESH
        )
    place = Place(nx, nz)
    lat_peers = [{"lat": before}, {"lat": after}]
    lat_peers += [place.at(x, place.z, core) for x, core in place.x_peers]
    lat_peers += [place.at(place.x, z, place.core) for z in place.z_peers]
    for peer in lat_peers:
        pl.semaphore_signal(barrier, inc=1, device_id=peer, device_id_type=MESH)

    blank = jnp.zeros((TP, 64, D), BF16)
    wexp[:, 0:64] = blank
    wexp[:, 128:192] = blank
    wexp[tp, 64:128] = fine_out[...]
    for head in range(2):
        cexp[head, 0:64] = jnp.zeros((64, DC), BF16)
        cexp[head, 64:128] = coarse_out[64 * head : 64 * head + 64]

    gather_w = Gather(group, lambda at: wexp.at[at, pl.ds(64, 64)])
    lift = Scatter(group, lift_terms, lift_y, lift_half, lift_z)
    send_keys = [
        links.copy(keys_sent.at[1], keys_came.at[0], {"lat": after}),
        links.copy(keys_sent.at[0], keys_came.at[1], {"lat": before}),
    ]
    gather_heads = Gather(group, lambda at: heads_all.at[:, aligned(at, 128)])
    gather_lift = Gather(group, lambda at: lift_all.at[aligned(at, CSHARE)])
    gather_coarse = Gather(group, lambda at: coarse_all.at[:, aligned(at, 128)])
    send_ckeys = links.copy(ckeys, ckeys_came, {"lat": twin})
    send_cback = links.copy(cback, cback_came, {"lat": twin})
    csum = Scatter(group, cs_terms, cs_y, cs_half, cs_z)
    cnorm = Scatter(group, cn_terms, cn_y, cn_half, cn_z)
    columns = Exchange(
        group,
        lambda at: grad_chunk.at[:, aligned(at, 128)],
        lambda at: grad_columns.at[aligned(at, CSHARE)],
    )
    gather_lifted = Gather(group, lambda at: lifted_all.at[aligned(at, CSHARE)])
    mnorm = Scatter(group, mn_terms, mn_y, mn_half, mn_z)
    gather_up = Gather(group, lambda at: up_all.at[at])
    mix = Exchange(
        group,
        lambda at: grad_mix_send.at[:, aligned(at, 128)],
        lambda at: grad_mix_all.at[aligned(at, SHARE)],
    )
    send_back = [
        links.copy(back.at[0], back_came.at[1], {"lat": before}),
        links.copy(back.at[1], back_came.at[0], {"lat": after}),
    ]
    gnorm = Scatter(group, gn_terms, gn_y, gn_half, gn_z)
    merge_sum = LatSum(links, place, mterms, mcame_x, mpart, mcame_z)
    fine_sum = LatSum(links, place, fterms, fcame_x, fpart, fcame_z)

    embedded = []
    for r in range(2):
        kinds = lax.broadcasted_iota(jnp.int32, (8, LON), 0)
        onehot = jnp.where(classes[r : r + 1, :] == kinds, 1.0, 0.0).astype(BF16)
        embedded.append(dot_tn(onehot, class_table[...]))
    for r in range(2):
        for level in range(LEV):
            full = fields[r, level].astype(F32) + embedded[r]
            cots = cotangent[r, level].astype(F32)
            for block in range(TP):
                at = r * ROW + block * SHARE + level * 8
                hid[at : at + 8] = full[8 * block : 8 * block + 8]
                put(cotf, pl.ds(at, 8), cots[8 * block : 8 * block + 8])

    for i in range(4):
        chunk = pl.ds(i * 128, 128)
        normed[chunk] = normalize(hid[chunk], gain_fine[...]).astype(BF16)
    for r in range(2):
        rows = pl.ds(r * ROW, ROW)
        queries[rows] = low_lanes(dot_nt(normed[rows], fine_w[0:128])).astype(BF16)
        kv = dot_nt(normed[rows], fine_w[64:192]).astype(BF16)
        keys[r] = kv
        keys_sent[r] = kv

    pl.semaphore_wait(barrier, TP - 1 + len(lat_peers))
    for made in send_keys:
        made.start()
    gather_w.start()

    kind = lax.div(tp, 2)
    quad = get(cotf, pl.ds(lax.div(kind, 2) * ROW + lax.rem(kind, 2), CTOK, stride=2))
    quad = jnp.where(lax.rem(tp, 2) == 0, quad[:, 0:256], quad[:, 256:512]).astype(BF16)
    lift_terms[...] = dot_nt(quad, up_weight[...]).astype(BF16).reshape(ZH, YS, CSHARE, DC)
    lift.start()

    for made in send_keys:
        made.wait_recv()
    gather_w.forward()

    present = (lat > 0, lat < lat_count - 1)

    def attend(r, half):
        start = r * ROW + half * CTOK
        chunk = pl.ds(start, CTOK)
        mask = fine_mask(half * CTOK)
        query = queries[chunk]
        own = jnp.where(mask, dot_nt(query, keys[r]) * SCALE, NEGATIVE)
        far = dot_nt(query, keys_came[r]) * SCALE
        far = jnp.where(jnp.logical_and(mask, present[r]), far, NEGATIVE)
        own, far = softmax_pair(own, far)
        prob_own[chunk] = own
        prob_other[chunk] = far
        mixture[chunk] = dot(own.astype(BF16), keys[r]) + dot(far.astype(BF16), keys_came[r])

    for r in range(2):
        for half in range(2):
            attend(r, half)
    lane = lax.broadcasted_iota(jnp.int32, (ROW, 128), 1)
    packed = jnp.where(lane < 64, pltpu.roll(mixture[ROW : 2 * ROW], 64, 1), mixture[0:ROW])
    heads_all[:, aligned(tp, 128)] = packed.astype(BF16)
    gather_heads.start()

    lift.middle()
    gather_w.finish()
    gather_heads.forward()
    lift_chunk = lift.finish().astype(BF16)
    lift_all[aligned(tp, CSHARE)] = lift_chunk
    gather_lift.start()
    gather_heads.finish()

    for r in range(2):
        first = 64 if r == 1 else 0
        weight = wexp[:, first : first + 128].reshape(TP * 128, D)
        rows = pl.ds(r * ROW, ROW)
        put(resid, rows, hid[rows] + dot(heads_all[...], weight))

    merged = [get(resid, pl.ds(r * ROW + s, CTOK, stride=2)) for r in range(2) for s in range(2)]
    merged = jnp.concatenate(merged, axis=1)
    merged_norm[...] = normalize(merged, gain_merge[...]).astype(BF16)
    coarse_all[:, aligned(tp, 128)] = dot(merged_norm[...], merge_weight[...]).astype(BF16)
    gather_coarse.start()
    gather_lift.forward()
    gather_coarse.forward()
    gather_lift.finish()
    grad_cmix = [dot_nt(lift_all[...], cexp[head]).astype(BF16) for head in range(2)]
    gather_coarse.finish()

    coarse_f[...] = coarse_all[...].astype(F32)
    cnormed = normalize(coarse_f[...], gain_coarse[...]).astype(BF16)
    for head in range(2):
        ckeys[head] = dot_nt(cnormed, coarse_w[head, 64:192]).astype(BF16)
    send_ckeys.start()
    cq = [low_lanes(dot_nt(cnormed, coarse_w[head, 0:128])).astype(BF16) for head in range(2)]

    row_at = lax.broadcasted_iota(jnp.int32, (CTOK, CTOK), 0)
    col_at = lax.broadcasted_iota(jnp.int32, (CTOK, CTOK), 1)
    cmask = (row_at >> 5) == (col_at >> 5)
    own_scores = [
        jnp.where(cmask, dot_nt(cq[head], ckeys[head]) * SCALE, NEGATIVE) for head in range(2)
    ]
    send_ckeys.wait_recv()
    cgrad_q, cgrad_kv = [], []
    cheads = []
    for head in range(2):
        far = jnp.where(cmask, dot_nt(cq[head], ckeys_came[head]) * SCALE, NEGATIVE)
        own, far = softmax_pair(own_scores[head], far)
        own16, far16 = own.astype(BF16), far.astype(BF16)
        grad_own = dot_nt(grad_cmix[head], ckeys[head])
        grad_far = dot_nt(grad_cmix[head], ckeys_came[head])
        ds_own, ds_far = score_grads(own, far, grad_own, grad_far)
        cback[head] = (dot_tn(ds_far, cq[head]) + dot_tn(far16, grad_cmix[head])).astype(BF16)
        cgrad_kv.append(dot_tn(ds_own, cq[head]) + dot_tn(own16, grad_cmix[head]))
        query_grad = dot(ds_own, ckeys[head]) + dot(ds_far, ckeys_came[head])
        cgrad_q.append(low_lanes(query_grad).astype(BF16))
        cheads.append((dot(own16, ckeys[head]) + dot(far16, ckeys_came[head])).astype(BF16))
    send_cback.start()
    part = dot(cheads[0], cexp[0]) + dot(cheads[1], cexp[1])
    cs_terms[...] = part.astype(BF16).reshape(ZH, YS, CSHARE, DC)
    csum.start()
    part = dot(cgrad_q[0], coarse_w[0, 0:128]) + dot(cgrad_q[1], coarse_w[1, 0:128])
    send_cback.wait_recv()
    for head in range(2):
        total = (cgrad_kv[head] + cback_came[head].astype(F32)).astype(BF16)
        part = part + dot(total, coarse_w[head, 64:192])
    cn_terms[...] = part.astype(BF16).reshape(ZH, YS, CSHARE, DC)
    cnorm.start()
    csum.middle()
    cnorm.middle()

    mine = aligned(tp, CSHARE)
    coarse_chunk = coarse_f[mine]
    grad_cn = cnorm.finish()
    grad_chunk[...] = (
        lift_chunk.astype(F32) + normalize_back(coarse_chunk, gain_coarse[...], grad_cn)
    ).astype(BF16)
    columns.start()
    grad_columns[mine] = grad_chunk[:, aligned(tp, 128)]
    lifted_all[mine] = (coarse_chunk + csum.finish()).astype(BF16)
    gather_lifted.start()
    columns.finish()
    part = dot_nt(grad_columns[...], merge_weight[...])
    mn_terms[...] = part.astype(BF16).reshape(ZH, YS, CSHARE, 4 * D)
    mnorm.start()

    scale = (2 * lat_count * LEV * LON) ** -0.5
    merge_rows = 4 * D // lat_count
    weight_rows = D // lat_count
    term = dot_tn(merged_norm[...], grad_columns[...]) * scale
    mterms[...] = term.astype(BF16).reshape(nx, nz, 2, merge_rows, 128)
    merge_sum.start()
    gather_lifted.forward()
    mnorm.middle()
    gather_lifted.finish()
    up_all[tp] = dot(lifted_all[...], up_weight[...]).astype(BF16)
    gather_up.start()

    grad_mn = mnorm.finish()
    merged_chunk, cot_chunk = [], []
    for r in range(2):
        for s in range(2):
            some = pl.ds(r * ROW + s + tp * SHARE, CSHARE, stride=2)
            merged_chunk.append(get(resid, some))
            cot_chunk.append(get(cotf, some))
    merged_chunk = jnp.concatenate(merged_chunk, axis=1)
    cot_chunk = jnp.concatenate(cot_chunk, axis=1)
    grad_merged = normalize_back(merged_chunk, gain_merge[...], grad_mn)
    grad_quads = (cot_chunk + grad_merged).astype(BF16)
    low = wexp[:, 0:128].reshape(TP * 128, D)
    high = wexp[:, 64:192].reshape(TP * 128, D)
    for s in range(2):
        top = grad_quads[:, s * D : (s + 1) * D]
        bottom = grad_quads[:, (2 + s) * D : (3 + s) * D]
        put(grad_mix, pl.ds(s, CSHARE, stride=2), dot_nt(top, low) + dot_nt(bottom, high))
        put(grad_resid, pl.ds(s, CSHARE, stride=2), top.astype(F32))
        put(grad_resid, pl.ds(SHARE + s, CSHARE, stride=2), bottom.astype(F32))
    grad_mix_send[...] = get(grad_mix, pl.ds(0, SHARE)).astype(BF16)
    mix.start()
    grad_mix_all[aligned(tp, SHARE)] = grad_mix_send[:, aligned(tp, 128)]
    gather_up.forward()
    merge_sum.middle()
    mix.finish()

    both = grad_mix_all[...].astype(F32)
    grad_mix_rows[0:ROW] = high_lanes(both).astype(BF16)
    grad_mix_rows[ROW : 2 * ROW] = high_lanes(pltpu.roll(both, 64, 1)).astype(BF16)

    def attend_back(r, half):
        chunk = pl.ds(r * ROW + half * CTOK, CTOK)
        query, grad_out = queries[chunk], grad_mix_rows[chunk]
        own, far = prob_own[chunk], prob_other[chunk]
        ds_own, ds_far = score_grads(
            own, far, dot_nt(grad_out, keys[r]), dot_nt(grad_out, keys_came[r])
        )
        own16, far16 = own.astype(BF16), far.astype(BF16)
        to_own = dot_tn(ds_own, query) + dot_tn(own16, grad_out)
        to_far = dot_tn(ds_far, query) + dot_tn(far16, grad_out)
        grad_q[chunk] = low_lanes(dot(ds_own, keys[r]) + dot(ds_far, keys_came[r])).astype(BF16)
        return to_own, to_far

    for r in range(2):
        own_a, far_a = attend_back(r, 0)
        own_b, far_b = attend_back(r, 1)
        back[r] = (far_a + far_b).astype(BF16)
        send_back[r].start()
        grad_other[r] = own_a + own_b
    for made in send_back:
        made.wait_recv()
    for r in range(2):
        grad_kv[pl.ds(r * ROW, ROW)] = (grad_other[r] + back_came[r].astype(F32)).astype(BF16)
    for r in range(2):
        rows = pl.ds(r * ROW, ROW)
        part = dot(grad_q[rows], fine_w[0:128]) + dot(grad_kv[rows], fine_w[64:192])
        gn_terms[:, :, r] = part.astype(BF16).reshape(ZH, YS, SHARE, D)
    gnorm.start()

    term_q = dot_tn(normed[...], grad_q[...]) * scale
    term_kv = dot_tn(normed[...], grad_kv[...]) * scale
    term = jnp.concatenate(
        [term_q.reshape(lat_count, weight_rows, 128), term_kv.reshape(lat_count, weight_rows, 128)],
        axis=1,
    )
    fterms[...] = term.astype(BF16).reshape(nx, nz, 2, 2 * weight_rows, 128)
    fine_sum.start()
    gnorm.middle()
    fine_sum.middle()

    gather_up.finish()
    for r in range(2):
        for s in range(2):
            for part in range(2):
                wide = up_all[4 * r + 2 * s + part].astype(F32)
                some = pl.ds(r * ROW + s, CTOK, stride=2)
                up_wide[2 * part, some, :] = wide[:, 0:128]
                up_wide[2 * part + 1, some, :] = wide[:, 128:256]
    for r in range(2):
        for level in range(LEV):
            pieces = []
            for block in range(TP):
                at = r * ROW + block * SHARE + level * 8
                pieces.append(get(resid, pl.ds(at, 8)) + get(up_wide, pl.ds(at, 8)))
            next_fields[r, level] = jnp.concatenate(pieces, axis=0).astype(BF16)

    grad_norm = gnorm.finish()
    for r in range(2):
        own_hidden = hid[pl.ds(pl.multiple_of(r * ROW + tp * SHARE, SHARE), SHARE)]
        grad_hidden = normalize_back(own_hidden, gain_fine[...], grad_norm[r])
        grad_hidden = grad_hidden + get(grad_resid, pl.ds(r * SHARE, SHARE))
        fields_grad[r] = grad_hidden.astype(BF16)
    merge_grad[...] = merge_sum.finish()
    sums = fine_sum.finish()
    fine_grad[:, 0, 0:64] = sums[0:weight_rows, 0:64]
    fine_grad[:, 0, 64:192] = sums[weight_rows : 2 * weight_rows]
    links.finish()


def vmem(*shape, kind=BF16):
    return pltpu.VMEM(shape, kind)


def scatter_buffers(*chunk):
    return [vmem(ZH, YS, *chunk), vmem(YS - 1, ZH, *chunk), vmem(*chunk), vmem(*chunk)]


def lat_buffers(nx, nz, rows):
    return [
        vmem(nx, nz, 2, rows, 128),
        vmem(2 * nx - 1, nz, rows, 128),
        vmem(nz, rows, 128),
        vmem(nz - 1, rows, 128),
    ]


def local(
    lat_count,
    fields,
    classes,
    class_table,
    gain_fine,
    fine_qkv,
    fine_out,
    gain_merge,
    merge_weight,
    gain_coarse,
    coarse_qkv,
    coarse_out,
    up_weight,
    cotangent,
):
    merge_rows, weight_rows = 4 * D // lat_count, D // lat_count
    nz = min(8, lat_count // 4)
    nx = lat_count // (2 * nz)
    whole = pl.BlockSpec(memory_space=pltpu.VMEM)
    copies = 160
    scratch = [
        pltpu.SemaphoreType.DMA((copies,)),
        pltpu.SemaphoreType.DMA((copies,)),
        vmem(2 * ROW, D, kind=F32),
        vmem(4, 2 * ROW, 128, kind=F32),
        vmem(2 * ROW, D),
        vmem(2 * ROW, 128),
        vmem(2, ROW, 128),
        vmem(2, ROW, 128),
        vmem(2, ROW, 128),
        vmem(2 * ROW, ROW, kind=F32),
        vmem(2 * ROW, ROW, kind=F32),
        vmem(2 * ROW, 128, kind=F32),
        vmem(ROW, TP * 128),
        vmem(TP, 192, D),
        vmem(2, 128, DC),
        vmem(4, 2 * ROW, 128, kind=F32),
        vmem(CTOK, 4 * D),
        vmem(CTOK, DC),
        vmem(CTOK, DC, kind=F32),
        vmem(CTOK, DC),
        *scatter_buffers(CSHARE, DC),
        vmem(2, CTOK, 128),
        vmem(2, CTOK, 128),
        vmem(2, CTOK, 128),
        vmem(2, CTOK, 128),
        *scatter_buffers(CSHARE, DC),
        *scatter_buffers(CSHARE, DC),
        vmem(CSHARE, DC),
        vmem(CTOK, 128),
        vmem(CTOK, DC),
        *scatter_buffers(CSHARE, 4 * D),
        vmem(TP, CTOK, 256),
        vmem(4, 2 * ROW, 128, kind=F32),
        vmem(TP, SHARE, 128, kind=F32),
        vmem(SHARE, TP * 128),
        vmem(ROW, 128),
        vmem(2 * ROW, 128),
        vmem(4, 2 * SHARE, 128, kind=F32),
        vmem(2 * ROW, 128),
        vmem(2 * ROW, 128),
        vmem(2, ROW, 128, kind=F32),
        vmem(2, ROW, 128),
        vmem(2, ROW, 128),
        *scatter_buffers(2, SHARE, D),
        *lat_buffers(nx, nz, merge_rows),
        *lat_buffers(nx, nz, 2 * weight_rows),
    ]
    next_fields, fields_grad, fine_grad, merge_grad = pl.pallas_call(
        functools.partial(main_kernel, lat_count, nx, nz),
        out_shape=(
            jax.ShapeDtypeStruct((2, LEV, LON, D), BF16),
            jax.ShapeDtypeStruct((2, SHARE, D), BF16),
            jax.ShapeDtypeStruct((weight_rows, 1, 192), F32),
            jax.ShapeDtypeStruct((merge_rows, 128), F32),
        ),
        in_specs=[whole] * 13,
        out_specs=[whole] * 4,
        scratch_shapes=scratch,
        name="block",
        compiler_params=pltpu.CompilerParams(
            collective_id=0, has_side_effects=True, vmem_limit_bytes=56 * 2**20
        ),
    )(
        fields,
        classes,
        class_table,
        gain_fine.reshape(1, -1),
        fine_qkv.reshape(D, 192).T,
        fine_out.reshape(64, D),
        gain_merge.reshape(1, -1),
        merge_weight,
        gain_coarse.reshape(1, -1),
        coarse_qkv.transpose(1, 2, 0),
        coarse_out.reshape(128, DC),
        up_weight,
        cotangent,
    )
    return next_fields, fields_grad.reshape(2, LEV, LON // TP, D), fine_grad, merge_grad


def solution(mesh):
    placed = (
        P("lat", None, None, None),
        P("lat", None),
        P(),
        P(),
        P(None, "tp", None),
        P("tp", None, None),
        P(),
        P(None, "tp"),
        P(),
        P(None, "tp", None),
        P("tp", None, None),
        P(None, "tp"),
        P("lat", None, None, None),
    )
    return jax.shard_map(
        functools.partial(local, mesh.shape["lat"]),
        mesh=mesh,
        in_specs=placed,
        out_specs=(
            P("lat", None, None, None),
            P("lat", None, "tp", None),
            P("lat", "tp", None),
            P("lat", "tp"),
        ),
        check_vma=False,
    )
```

```python
import functools

import jax
import jax.numpy as jnp
from jax import lax
from jax.experimental import pallas as pl
from jax.experimental.pallas import tpu as pltpu
from jax.sharding import PartitionSpec as P

MESH = pl.DeviceIdType.MESH
F32 = jnp.float32
BF16 = jnp.bfloat16
EPSILON = 1e-05
NEGATIVE = -1e30

D = 512
DC = 1024
LEV = 4
LON = 64
ZH = 2
YS = 4
TP = ZH * YS
ROW = LEV * LON
CTOK = ROW // 2
SHARE = ROW // TP
CSHARE = CTOK // TP
SCALE = 0.125


def dot(a, b):
    return lax.dot_general(a, b, (((1,), (0,)), ((), ())), preferred_element_type=F32)


def dot_nt(a, b):
    return lax.dot_general(a, b, (((1,), (1,)), ((), ())), preferred_element_type=F32)


def dot_tn(a, b):
    return lax.dot_general(a, b, (((0,), (0,)), ((), ())), preferred_element_type=F32)


def standardize(values):
    centred = values - jnp.mean(values, axis=-1, keepdims=True)
    spread = jnp.mean(centred * centred, axis=-1, keepdims=True)
    inverse = lax.rsqrt(spread + EPSILON)
    return centred * inverse, inverse


def normalize_back(values, gain, incoming):
    unit, inverse = standardize(values)
    inner = incoming * gain
    first = jnp.mean(inner, axis=-1, keepdims=True)
    second = jnp.mean(inner * unit, axis=-1, keepdims=True)
    return inverse * (inner - first - unit * second)


class Links:
    def __init__(self, send_sems, recv_sems):
        self.send_sems, self.recv_sems = send_sems, recv_sems
        self.copies = []

    def copy(self, src, dst, device):
        at = len(self.copies)
        made = pltpu.make_async_remote_copy(
            src_ref=src,
            dst_ref=dst,
            send_sem=self.send_sems.at[at],
            recv_sem=self.recv_sems.at[at],
            device_id=device,
            device_id_type=MESH,
        )
        self.copies.append(made)
        return made

    def finish(self):
        for made in self.copies:
            made.wait_send()


class Group:
    def __init__(self, links):
        self.links = links
        self.tp = lax.axis_index("tp")
        self.zh, self.y = lax.div(self.tp, YS), lax.rem(self.tp, YS)
        self.other = lax.rem(self.tp + YS, TP)

    def y_at(self, k):
        return lax.rem(self.y + k, YS)

    def along_y(self, k):
        return {"tp": self.zh * YS + self.y_at(k)}


class Gather:
    def __init__(self, group, view):
        links = group.links
        own, far = view(group.tp), view(group.other)
        self.over_z = links.copy(own, own, {"tp": group.other})
        self.over_y = [links.copy(own, own, group.along_y(k)) for k in range(1, YS)]
        self.passed = [links.copy(far, far, group.along_y(k)) for k in range(1, YS)]

    def start(self):
        for made in [self.over_z] + self.over_y:
            made.start()

    def forward(self):
        self.over_z.wait_recv()
        for made in self.passed:
            made.start()

    def finish(self):
        for made in self.over_y + self.passed:
            made.wait_recv()


class Scatter:
    def __init__(self, group, terms, came_y, half, came_z):
        self.group, self.terms = group, terms
        self.came_y, self.half, self.came_z = came_y, half, came_z
        links = group.links
        self.over_y = [
            links.copy(terms.at[:, group.y_at(k)], came_y.at[k - 1], group.along_y(k))
            for k in range(1, YS)
        ]
        self.over_z = links.copy(half, came_z, {"tp": group.other})

    def start(self):
        for made in self.over_y:
            made.start()

    def summed(self, zh):
        total = self.terms[zh, self.group.y].astype(F32)
        for k in range(YS - 1):
            total = total + self.came_y[k, zh].astype(F32)
        return total

    def middle(self):
        for made in self.over_y:
            made.wait_recv()
        self.half[...] = self.summed(1 - self.group.zh).astype(BF16)
        self.over_z.start()

    def finish(self):
        own = self.summed(self.group.zh)
        self.over_z.wait_recv()
        return own + self.came_z[...].astype(F32)


class Moments:
    def __init__(self, group, own, came_y, half, came_z):
        self.own, self.came_y, self.half, self.came_z = own, came_y, half, came_z
        links = group.links
        self.over_y = [
            links.copy(own, came_y.at[k - 1], group.along_y(k)) for k in range(1, YS)
        ]
        self.over_z = links.copy(half, came_z, {"tp": group.other})

    def start(self, inner, unit):
        first = jnp.mean(inner, axis=-1, keepdims=True)
        second = jnp.mean(inner * unit, axis=-1, keepdims=True)
        lane = lax.broadcasted_iota(jnp.int32, (CTOK, 128), 1)
        both = jnp.where(lane == 0, first, jnp.where(lane == 1, second, 0.0))
        self.own[...] = both.T[0:8]
        for made in self.over_y:
            made.start()

    def middle(self):
        for made in self.over_y:
            made.wait_recv()
        total = self.own[...]
        for k in range(YS - 1):
            total = total + self.came_y[k]
        self.half[...] = total
        self.over_z.start()

    def finish(self):
        self.over_z.wait_recv()
        total = self.half[...] + self.came_z[...]
        both = jnp.concatenate([total, jnp.zeros((CTOK - 8, 128), F32)], axis=0).T
        return both[:, 0:1], both[:, 1:2]


class LatSum:
    def __init__(self, links, place, terms, came_x, part, came_z):
        self.place, self.terms, self.came_x, self.part, self.came_z = (
            place,
            terms,
            came_x,
            part,
            came_z,
        )
        self.over_x = [
            links.copy(terms.at[x, :, core], came_x.at[k], place.at(x, place.z, core))
            for k, (x, core) in enumerate(place.x_peers)
        ]
        self.over_z = [
            links.copy(part.at[z], came_z.at[k], place.at(place.x, z, place.core))
            for k, z in enumerate(place.z_peers)
        ]

    def start(self):
        for made in self.over_x:
            made.start()

    def middle(self):
        for made in self.over_x:
            made.wait_recv()
        total = self.terms[self.place.x, :, self.place.core].astype(F32)
        for k in range(len(self.over_x)):
            total = total + self.came_x[k].astype(F32)
        self.part[...] = total.astype(BF16)
        for made in self.over_z:
            made.start()

    def finish(self):
        for made in self.over_z:
            made.wait_recv()
        total = self.part[self.place.z].astype(F32)
        for k in range(len(self.over_z)):
            total = total + self.came_z[k].astype(F32)
        return total


class Place:
    def __init__(self, nx, nz):
        lat = lax.axis_index("lat")
        self.nz = nz
        self.core = lax.rem(lat, 2)
        self.z = lax.rem(lax.div(lat, 2), nz)
        self.x = lax.div(lat, 2 * nz)
        self.x_peers = [
            (lax.rem(self.x + i, nx), lax.rem(self.core + j, 2))
            for i in range(nx)
            for j in range(2)
            if i or j
        ]
        self.z_peers = [lax.rem(self.z + k, nz) for k in range(1, nz)]

    def at(self, x, z, core):
        return {"lat": (x * self.nz + z) * 2 + core}


def aligned(index, size):
    return pl.ds(pl.multiple_of(index * size, size), size)


def put(ref, rows, values):
    for j in range(values.shape[1] // 128):
        ref[j, rows, :] = values[:, 128 * j : 128 * j + 128]


def get(ref, rows):
    return jnp.concatenate([ref[j, rows, :] for j in range(ref.shape[0])], axis=1)


def softmax_pair(own, other):
    largest = jnp.maximum(
        jnp.max(own, axis=-1, keepdims=True), jnp.max(other, axis=-1, keepdims=True)
    )
    own, other = jnp.exp(own - largest), jnp.exp(other - largest)
    total = jnp.sum(own, axis=-1, keepdims=True) + jnp.sum(other, axis=-1, keepdims=True)
    return own / total, other / total


def score_grads(prob_own, prob_other, grad_own, grad_other):
    mean = jnp.sum(grad_own * prob_own, axis=-1, keepdims=True)
    mean = mean + jnp.sum(grad_other * prob_other, axis=-1, keepdims=True)
    return (
        (prob_own * (grad_own - mean) * SCALE).astype(BF16),
        (prob_other * (grad_other - mean) * SCALE).astype(BF16),
    )


def low_lanes(values):
    lane = lax.broadcasted_iota(jnp.int32, values.shape, 1)
    return jnp.where(lane < 64, values, 0.0)


def high_lanes(values):
    lane = lax.broadcasted_iota(jnp.int32, values.shape, 1)
    return jnp.where(lane >= 64, values, 0.0)


def fine_mask(start):
    def window(index):
        return ((index >> 5) + 7 + ((index & 7) >> 2)) & 7

    query = lax.broadcasted_iota(jnp.int32, (CTOK, ROW), 0) + start
    key = lax.broadcasted_iota(jnp.int32, (CTOK, ROW), 1)
    return window(query) == window(key)


def main_kernel(
    lat_count,
    nx,
    nz,
    fields,
    classes,
    class_table,
    gain_fine,
    fine_w,
    fine_out,
    gain_merge,
    merge_weight_in,
    gain_coarse,
    coarse_w_in,
    coarse_out_in,
    up_weight_in,
    cotangent_in,
    next_fields,
    fields_grad,
    fine_grad,
    merge_grad,
    send_sems,
    recv_sems,
    local_sems,
    merge_weight,
    coarse_w,
    up_weight,
    cotangent,
    fields_out,
    hid,
    cotf,
    normed,
    queries,
    keys,
    keys_sent,
    keys_came,
    prob_own,
    prob_other,
    mixture,
    heads_all,
    wexp,
    cexp,
    resid,
    merged_norm,
    coarse_all,
    coarse_f,
    lift_all,
    lift_terms,
    lift_y,
    lift_half,
    lift_z,
    ckeys,
    ckeys_came,
    cback,
    cback_came,
    cs_terms,
    cs_y,
    cs_half,
    cs_z,
    cn_terms,
    cn_y,
    cn_half,
    cn_z,
    cunit,
    cinverse,
    cm_own,
    cm_y,
    cm_half,
    cm_z,
    grad_columns,
    lifted_all,
    mn_terms,
    mn_y,
    mn_half,
    mn_z,
    up_all,
    up_wide,
    munit,
    minverse,
    mm_own,
    mm_y,
    mm_half,
    mm_z,
    gh_terms,
    gh_y,
    gh_half,
    gh_z,
    grad_mix,
    grad_mix_rows,
    grad_resid,
    grad_q,
    grad_kv,
    grad_other,
    back,
    back_came,
    gn_terms,
    gn_y,
    gn_half,
    gn_z,
    mterms,
    mcame_x,
    mpart,
    mcame_z,
    fterms,
    fcame_x,
    fpart,
    fcame_z,
):
    def fetch(src, dst, at):
        made = pltpu.make_async_copy(src, dst, local_sems.at[at])
        made.start()
        return made

    got_cotangent = fetch(cotangent_in, cotangent, 0)
    got_up = fetch(up_weight_in, up_weight, 1)
    got_merge = fetch(merge_weight_in, merge_weight, 2)
    got_coarse = [fetch(coarse_w_in, coarse_w, 3)]
    for head in range(2):
        rows = coarse_out_in.at[pl.ds(64 * head, 64)]
        got_coarse.append(fetch(rows, cexp.at[head, pl.ds(64, 64)], 4 + head))

    links = Links(send_sems, recv_sems)
    group = Group(links)
    tp = group.tp
    lat = lax.axis_index("lat")
    before, after = lax.rem(lat + lat_count - 1, lat_count), lax.rem(lat + 1, lat_count)
    twin = lat + 1 - 2 * lax.rem(lat, 2)

    barrier = pltpu.get_barrier_semaphore()
    for k in range(1, TP):
        pl.semaphore_signal(
            barrier, inc=1, device_id={"tp": lax.rem(tp + k, TP)}, device_id_type=MESH
        )
    place = Place(nx, nz)
    lat_peers = [{"lat": before}, {"lat": after}]
    lat_peers += [place.at(x, place.z, core) for x, core in place.x_peers]
    lat_peers += [place.at(place.x, z, place.core) for z in place.z_peers]
    for peer in lat_peers:
        pl.semaphore_signal(barrier, inc=1, device_id=peer, device_id_type=MESH)

    blank = jnp.zeros((TP, 64, D), BF16)
    wexp[:, 0:64] = blank
    wexp[:, 128:192] = blank
    wexp[tp, 64:128] = fine_out[...]
    for head in range(2):
        cexp[head, 0:64] = jnp.zeros((64, DC), BF16)

    gather_w = Gather(group, lambda at: wexp.at[at, pl.ds(64, 64)])
    lift = Scatter(group, lift_terms, lift_y, lift_half, lift_z)
    send_keys = [
        links.copy(keys_sent.at[1], keys_came.at[0], {"lat": after}),
        links.copy(keys_sent.at[0], keys_came.at[1], {"lat": before}),
    ]
    gather_heads = [
        Gather(group, lambda at, i=i: heads_all.at[pl.ds(i * 128, 128), aligned(at, 128)])
        for i in range(2)
    ]
    gather_lift = Gather(group, lambda at: lift_all.at[aligned(at, CSHARE)])
    gather_coarse = Gather(group, lambda at: coarse_all.at[:, aligned(at, 128)])
    send_ckeys = links.copy(ckeys, ckeys_came, {"lat": twin})
    send_cback = links.copy(cback, cback_came, {"lat": twin})
    csum = Scatter(group, cs_terms, cs_y, cs_half, cs_z)
    cnorm = Scatter(group, cn_terms, cn_y, cn_half, cn_z)
    cmoments = Moments(group, cm_own, cm_y, cm_half, cm_z)
    gather_lifted = Gather(group, lambda at: lifted_all.at[aligned(at, CSHARE)])
    mnorm = Scatter(group, mn_terms, mn_y, mn_half, mn_z)
    gather_up = Gather(group, lambda at: up_all.at[at])
    mmoments = Moments(group, mm_own, mm_y, mm_half, mm_z)
    gheads = [
        Scatter(group, gh_terms.at[s], gh_y.at[s], gh_half.at[s], gh_z.at[s]) for s in range(2)
    ]
    send_back = [
        links.copy(back.at[0], back_came.at[1], {"lat": before}),
        links.copy(back.at[1], back_came.at[0], {"lat": after}),
    ]
    gnorm = [
        Scatter(group, gn_terms.at[r], gn_y.at[r], gn_half.at[r], gn_z.at[r]) for r in range(2)
    ]
    merge_sum = LatSum(links, place, mterms, mcame_x, mpart, mcame_z)
    fine_sum = LatSum(links, place, fterms, fcame_x, fpart, fcame_z)

    embedded = []
    for r in range(2):
        kinds = lax.broadcasted_iota(jnp.int32, (8, LON), 0)
        onehot = jnp.where(classes[r : r + 1, :] == kinds, 1.0, 0.0).astype(BF16)
        embedded.append(dot_tn(onehot, class_table[...]))
    for r in range(2):
        for level in range(LEV):
            full = fields[r, level].astype(F32) + embedded[r]
            for block in range(TP):
                at = r * ROW + block * SHARE + level * 8
                hid[at : at + 8] = full[8 * block : 8 * block + 8]

    for i in range(4):
        chunk = pl.ds(i * 128, 128)
        unit, _ = standardize(hid[chunk])
        normed[chunk] = (unit * gain_fine[...]).astype(BF16)
    for r in range(2):
        rows = pl.ds(r * ROW, ROW)
        queries[rows] = low_lanes(dot_nt(normed[rows], fine_w[0:128])).astype(BF16)
        kv = dot_nt(normed[rows], fine_w[64:192]).astype(BF16)
        keys[r] = kv
        keys_sent[r] = kv

    pl.semaphore_wait(barrier, TP - 1 + len(lat_peers))
    for made in send_keys:
        made.start()
    gather_w.start()

    got_cotangent.wait()
    got_up.wait()
    for r in range(2):
        for level in range(LEV):
            cots = cotangent[r, level].astype(F32)
            for block in range(TP):
                at = r * ROW + block * SHARE + level * 8
                put(cotf, pl.ds(at, 8), cots[8 * block : 8 * block + 8])
    kind = lax.div(tp, 2)
    quad = get(cotf, pl.ds(lax.div(kind, 2) * ROW + lax.rem(kind, 2), CTOK, stride=2))
    quad = jnp.where(lax.rem(tp, 2) == 0, quad[:, 0:256], quad[:, 256:512]).astype(BF16)
    lift_terms[...] = dot_nt(quad, up_weight[...]).astype(BF16).reshape(ZH, YS, CSHARE, DC)
    lift.start()

    for made in send_keys:
        made.wait_recv()
    gather_w.forward()

    present = (lat > 0, lat < lat_count - 1)

    def attend(r, half):
        start = r * ROW + half * CTOK
        chunk = pl.ds(start, CTOK)
        mask = fine_mask(half * CTOK)
        query = queries[chunk]
        own = jnp.where(mask, dot_nt(query, keys[r]) * SCALE, NEGATIVE)
        far = dot_nt(query, keys_came[r]) * SCALE
        far = jnp.where(jnp.logical_and(mask, present[r]), far, NEGATIVE)
        own, far = softmax_pair(own, far)
        prob_own[chunk] = own
        prob_other[chunk] = far
        mixture[chunk] = dot(own.astype(BF16), keys[r]) + dot(far.astype(BF16), keys_came[r])

    for r in range(2):
        for half in range(2):
            attend(r, half)
    lane = lax.broadcasted_iota(jnp.int32, (ROW, 128), 1)
    packed = jnp.where(lane < 64, pltpu.roll(mixture[ROW : 2 * ROW], 64, 1), mixture[0:ROW])
    heads_all[:, aligned(tp, 128)] = packed.astype(BF16)
    for part in gather_heads:
        part.over_z.start()
    for part in gather_heads:
        for made in part.over_y:
            made.start()

    lift.middle()
    gather_w.finish()
    for part in gather_heads:
        part.forward()
    lift_chunk = lift.finish().astype(BF16)
    lift_all[aligned(tp, CSHARE)] = lift_chunk
    gather_lift.start()
    for part in gather_heads:
        part.finish()

    for r in range(2):
        first = 64 if r == 1 else 0
        weight = wexp[:, first : first + 128].reshape(TP * 128, D)
        rows = pl.ds(r * ROW, ROW)
        put(resid, rows, hid[rows] + dot(heads_all[...], weight))

    merged = [get(resid, pl.ds(r * ROW + s, CTOK, stride=2)) for r in range(2) for s in range(2)]
    merged = jnp.concatenate(merged, axis=1)
    unit, inverse = standardize(merged)
    merged_norm[...] = (unit * gain_merge[...]).astype(BF16)
    got_merge.wait()
    coarse_all[:, aligned(tp, 128)] = dot(merged_norm[...], merge_weight[...]).astype(BF16)
    gather_coarse.start()
    munit[...] = unit
    minverse[...] = jnp.broadcast_to(inverse, (CTOK, 128))
    gather_lift.forward()
    gather_coarse.forward()
    gather_lift.finish()
    for made in got_coarse:
        made.wait()
    grad_cmix = [dot_nt(lift_all[...], cexp[head]).astype(BF16) for head in range(2)]
    gather_coarse.finish()

    coarse_f[...] = coarse_all[...].astype(F32)
    unit, inverse = standardize(coarse_f[...])
    cnormed = (unit * gain_coarse[...]).astype(BF16)
    for head in range(2):
        ckeys[head] = dot_nt(cnormed, coarse_w[head, 64:192]).astype(BF16)
    send_ckeys.start()
    cunit[...] = unit
    cinverse[...] = jnp.broadcast_to(inverse, (CTOK, 128))
    cq = [low_lanes(dot_nt(cnormed, coarse_w[head, 0:128])).astype(BF16) for head in range(2)]

    row_at = lax.broadcasted_iota(jnp.int32, (CTOK, CTOK), 0)
    col_at = lax.broadcasted_iota(jnp.int32, (CTOK, CTOK), 1)
    cmask = (row_at >> 5) == (col_at >> 5)
    own_scores = [
        jnp.where(cmask, dot_nt(cq[head], ckeys[head]) * SCALE, NEGATIVE) for head in range(2)
    ]
    send_ckeys.wait_recv()
    cgrad_q, cgrad_kv = [], []
    cheads = []
    for head in range(2):
        far = jnp.where(cmask, dot_nt(cq[head], ckeys_came[head]) * SCALE, NEGATIVE)
        own, far = softmax_pair(own_scores[head], far)
        own16, far16 = own.astype(BF16), far.astype(BF16)
        grad_own = dot_nt(grad_cmix[head], ckeys[head])
        grad_far = dot_nt(grad_cmix[head], ckeys_came[head])
        ds_own, ds_far = score_grads(own, far, grad_own, grad_far)
        cback[head] = (dot_tn(ds_far, cq[head]) + dot_tn(far16, grad_cmix[head])).astype(BF16)
        cgrad_kv.append(dot_tn(ds_own, cq[head]) + dot_tn(own16, grad_cmix[head]))
        query_grad = dot(ds_own, ckeys[head]) + dot(ds_far, ckeys_came[head])
        cgrad_q.append(low_lanes(query_grad).astype(BF16))
        cheads.append((dot(own16, ckeys[head]) + dot(far16, ckeys_came[head])).astype(BF16))
    send_cback.start()
    part = dot(cheads[0], cexp[0]) + dot(cheads[1], cexp[1])
    cs_terms[...] = part.astype(BF16).reshape(ZH, YS, CSHARE, DC)
    csum.start()
    part = dot(cgrad_q[0], coarse_w[0, 0:128]) + dot(cgrad_q[1], coarse_w[1, 0:128])
    send_cback.wait_recv()
    for head in range(2):
        total = (cgrad_kv[head] + cback_came[head].astype(F32)).astype(BF16)
        part = part + dot(total, coarse_w[head, 64:192])
    for t in range(TP):
        cn_terms[t // YS, t % YS] = part[:, 128 * t : 128 * t + 128].astype(BF16)
    cnorm.start()
    cmoments.start(part * gain_coarse[...], cunit[...])

    own_low, own_high = wexp[tp, 0:128], wexp[tp, 64:192]

    def own_head(top, bottom):
        return dot_nt(top.astype(BF16), own_low) + dot_nt(bottom.astype(BF16), own_high)

    head_cot, head_unit = [], []
    for s in range(2):
        top, bottom = [get(cotf, pl.ds(r * ROW + s, CTOK, stride=2)) for r in range(2)]
        head_cot.append(own_head(top, bottom))
        top, bottom = [munit[:, (2 * r + s) * D : (2 * r + s + 1) * D] for r in range(2)]
        head_unit.append(own_head(top, bottom))
    ones = jnp.ones((8, D), BF16)
    head_ones = own_head(ones, ones)[0:1]

    cnorm.middle()
    cmoments.middle()
    csum.middle()

    lane_block = aligned(tp, 128)
    inner = cnorm.finish() * gain_coarse[:, lane_block]
    first, second = cmoments.finish()
    inner = cinverse[...] * (inner - first - cunit[:, lane_block] * second)
    grad_columns[...] = (lift_all[:, lane_block].astype(F32) + inner).astype(BF16)

    part = dot_nt(grad_columns[...], merge_weight[...])
    inner = part * gain_merge[...]
    inner16 = inner.astype(BF16)
    low = wexp[:, 0:128].reshape(TP * 128, D)
    high = wexp[:, 64:192].reshape(TP * 128, D)
    for s in range(2):
        top, bottom = [inner16[:, (2 * r + s) * D : (2 * r + s + 1) * D] for r in range(2)]
        heads = (dot_nt(top, low) + dot_nt(bottom, high)).astype(BF16)
        for t in range(TP):
            gh_terms[s, t // YS, t % YS] = heads[:, 128 * t : 128 * t + 128]
        gheads[s].start()
    mmoments.start(inner, munit[...])
    mn_terms[...] = part.astype(BF16).reshape(ZH, YS, CSHARE, 4 * D)
    mnorm.start()

    mine = aligned(tp, CSHARE)
    lifted_all[mine] = (coarse_f[mine] + csum.finish()).astype(BF16)
    for part in gheads:
        part.middle()
    mmoments.middle()
    gather_lifted.start()
    mnorm.middle()

    scale = (2 * lat_count * LEV * LON) ** -0.5
    merge_rows = 4 * D // lat_count
    weight_rows = D // lat_count
    term = dot_tn(merged_norm[...], grad_columns[...]) * scale
    mterms[...] = term.astype(BF16).reshape(nx, nz, 2, merge_rows, 128)
    merge_sum.start()
    gather_lifted.forward()

    first, second = mmoments.finish()
    for s in range(2):
        inner = gheads[s].finish() - first * head_ones - second * head_unit[s]
        put(grad_mix, pl.ds(s, CTOK, stride=2), head_cot[s] + minverse[...] * inner)
    both = grad_mix[0]
    grad_mix_rows[0:ROW] = high_lanes(both).astype(BF16)
    grad_mix_rows[ROW : 2 * ROW] = high_lanes(pltpu.roll(both, 64, 1)).astype(BF16)

    def attend_back(r, half):
        chunk = pl.ds(r * ROW + half * CTOK, CTOK)
        query, grad_out = queries[chunk], grad_mix_rows[chunk]
        own, far = prob_own[chunk], prob_other[chunk]
        ds_own, ds_far = score_grads(
            own, far, dot_nt(grad_out, keys[r]), dot_nt(grad_out, keys_came[r])
        )
        own16, far16 = own.astype(BF16), far.astype(BF16)
        to_own = dot_tn(ds_own, query) + dot_tn(own16, grad_out)
        to_far = dot_tn(ds_far, query) + dot_tn(far16, grad_out)
        grad_q[chunk] = low_lanes(dot(ds_own, keys[r]) + dot(ds_far, keys_came[r])).astype(BF16)
        return to_own, to_far

    for r in range(2):
        own_a, far_a = attend_back(r, 0)
        own_b, far_b = attend_back(r, 1)
        back[r] = (far_a + far_b).astype(BF16)
        send_back[r].start()
        grad_other[r] = own_a + own_b
    gather_lifted.finish()
    up_all[tp] = dot(lifted_all[...], up_weight[...]).astype(BF16)
    gather_up.start()
    merge_sum.middle()
    for made in send_back:
        made.wait_recv()
    for r in range(2):
        grad_kv[pl.ds(r * ROW, ROW)] = (grad_other[r] + back_came[r].astype(F32)).astype(BF16)
    for r in range(2):
        rows = pl.ds(r * ROW, ROW)
        part = dot(grad_q[rows], fine_w[0:128]) + dot(grad_kv[rows], fine_w[64:192])
        gn_terms[r] = part.astype(BF16).reshape(ZH, YS, SHARE, D)
        gnorm[r].start()

    term_q = dot_tn(normed[...], grad_q[...]) * scale
    term_kv = dot_tn(normed[...], grad_kv[...]) * scale
    term = jnp.concatenate(
        [term_q.reshape(lat_count, weight_rows, 128), term_kv.reshape(lat_count, weight_rows, 128)],
        axis=1,
    )
    fterms[...] = term.astype(BF16).reshape(nx, nz, 2, 2 * weight_rows, 128)
    fine_sum.start()
    gather_up.forward()
    for part in gnorm:
        part.middle()
    fine_sum.middle()

    grad_mn = mnorm.finish()
    merged_chunk, cot_chunk = [], []
    for r in range(2):
        for s in range(2):
            some = pl.ds(r * ROW + s + tp * SHARE, CSHARE, stride=2)
            merged_chunk.append(get(resid, some))
            cot_chunk.append(get(cotf, some))
    merged_chunk = jnp.concatenate(merged_chunk, axis=1)
    cot_chunk = jnp.concatenate(cot_chunk, axis=1)
    grad_quads = cot_chunk + normalize_back(merged_chunk, gain_merge[...], grad_mn)
    for r in range(2):
        for s in range(2):
            some = grad_quads[:, (2 * r + s) * D : (2 * r + s + 1) * D]
            put(grad_resid, pl.ds(r * SHARE + s, CSHARE, stride=2), some)

    gather_up.finish()
    for r in range(2):
        for s in range(2):
            for part in range(2):
                wide = up_all[4 * r + 2 * s + part].astype(F32)
                some = pl.ds(r * ROW + s, CTOK, stride=2)
                up_wide[2 * part, some, :] = wide[:, 0:128]
                up_wide[2 * part + 1, some, :] = wide[:, 128:256]
    for r in range(2):
        for level in range(LEV):
            pieces = []
            for block in range(TP):
                at = r * ROW + block * SHARE + level * 8
                pieces.append(get(resid, pl.ds(at, 8)) + get(up_wide, pl.ds(at, 8)))
            fields_out[r, level] = jnp.concatenate(pieces, axis=0).astype(BF16)
    written = fetch(fields_out, next_fields, 6)

    for r in range(2):
        grad_norm = gnorm[r].finish()
        own_hidden = hid[pl.ds(pl.multiple_of(r * ROW + tp * SHARE, SHARE), SHARE)]
        grad_hidden = normalize_back(own_hidden, gain_fine[...], grad_norm)
        grad_hidden = grad_hidden + get(grad_resid, pl.ds(r * SHARE, SHARE))
        fields_grad[r] = grad_hidden.astype(BF16)
    merge_grad[...] = merge_sum.finish()
    sums = fine_sum.finish()
    fine_grad[:, 0, 0:64] = sums[0:weight_rows, 0:64]
    fine_grad[:, 0, 64:192] = sums[weight_rows : 2 * weight_rows]
    written.wait()
    links.finish()


def hand_over(*refs):
    for i in range(4):
        refs[4 + i][...] = refs[i][...]


def vmem(*shape, kind=BF16):
    return pltpu.VMEM(shape, kind)


def scatter_buffers(*chunk):
    return [vmem(ZH, YS, *chunk), vmem(YS - 1, ZH, *chunk), vmem(*chunk), vmem(*chunk)]


def halved(*buffers):
    return [vmem(2, *some.shape) for some in buffers]


def moment_buffers():
    return [
        vmem(8, 128, kind=F32),
        vmem(YS - 1, 8, 128, kind=F32),
        vmem(8, 128, kind=F32),
        vmem(8, 128, kind=F32),
    ]


def lat_buffers(nx, nz, rows):
    return [
        vmem(nx, nz, 2, rows, 128),
        vmem(2 * nx - 1, nz, rows, 128),
        vmem(nz, rows, 128),
        vmem(nz - 1, rows, 128),
    ]


def local(
    lat_count,
    fields,
    classes,
    class_table,
    gain_fine,
    fine_qkv,
    fine_out,
    gain_merge,
    merge_weight,
    gain_coarse,
    coarse_qkv,
    coarse_out,
    up_weight,
    cotangent,
):
    merge_rows, weight_rows = 4 * D // lat_count, D // lat_count
    nz = min(8, lat_count // 4)
    nx = lat_count // (2 * nz)
    whole = pl.BlockSpec(memory_space=pltpu.VMEM)
    left = pl.BlockSpec(memory_space=pl.ANY)
    copies = 200
    scratch = [
        pltpu.SemaphoreType.DMA((copies,)),
        pltpu.SemaphoreType.DMA((copies,)),
        pltpu.SemaphoreType.DMA((7,)),
        vmem(4 * D, 128),
        vmem(2, 192, DC),
        vmem(DC, 256),
        vmem(2, LEV, LON, D),
        vmem(2, LEV, LON, D),
        vmem(2 * ROW, D, kind=F32),
        vmem(4, 2 * ROW, 128, kind=F32),
        vmem(2 * ROW, D),
        vmem(2 * ROW, 128),
        vmem(2, ROW, 128),
        vmem(2, ROW, 128),
        vmem(2, ROW, 128),
        vmem(2 * ROW, ROW, kind=F32),
        vmem(2 * ROW, ROW, kind=F32),
        vmem(2 * ROW, 128, kind=F32),
        vmem(ROW, TP * 128),
        vmem(TP, 192, D),
        vmem(2, 128, DC),
        vmem(4, 2 * ROW, 128, kind=F32),
        vmem(CTOK, 4 * D),
        vmem(CTOK, DC),
        vmem(CTOK, DC, kind=F32),
        vmem(CTOK, DC),
        *scatter_buffers(CSHARE, DC),
        vmem(2, CTOK, 128),
        vmem(2, CTOK, 128),
        vmem(2, CTOK, 128),
        vmem(2, CTOK, 128),
        *scatter_buffers(CSHARE, DC),
        *scatter_buffers(CTOK, 128),
        vmem(CTOK, DC, kind=F32),
        vmem(CTOK, 128, kind=F32),
        *moment_buffers(),
        vmem(CTOK, 128),
        vmem(CTOK, DC),
        *scatter_buffers(CSHARE, 4 * D),
        vmem(TP, CTOK, 256),
        vmem(4, 2 * ROW, 128, kind=F32),
        vmem(CTOK, 4 * D, kind=F32),
        vmem(CTOK, 128, kind=F32),
        *moment_buffers(),
        *halved(*scatter_buffers(CTOK, 128)),
        vmem(1, ROW, 128, kind=F32),
        vmem(2 * ROW, 128),
        vmem(4, 2 * SHARE, 128, kind=F32),
        vmem(2 * ROW, 128),
        vmem(2 * ROW, 128),
        vmem(2, ROW, 128, kind=F32),
        vmem(2, ROW, 128),
        vmem(2, ROW, 128),
        *halved(*scatter_buffers(SHARE, D)),
        *lat_buffers(nx, nz, merge_rows),
        *lat_buffers(nx, nz, 2 * weight_rows),
    ]
    results = pl.pallas_call(
        functools.partial(main_kernel, lat_count, nx, nz),
        out_shape=(
            jax.ShapeDtypeStruct((2, LEV, LON, D), BF16),
            jax.ShapeDtypeStruct((2, SHARE, D), BF16),
            jax.ShapeDtypeStruct((weight_rows, 1, 192), F32),
            jax.ShapeDtypeStruct((merge_rows, 128), F32),
        ),
        in_specs=[whole] * 7 + [left, whole] + [left] * 4,
        out_specs=[left] + [whole] * 3,
        scratch_shapes=scratch,
        name="block",
        compiler_params=pltpu.CompilerParams(
            collective_id=0, has_side_effects=True, vmem_limit_bytes=56 * 2**20
        ),
    )(
        fields,
        classes,
        class_table,
        gain_fine.reshape(1, -1),
        fine_qkv.reshape(D, 192).T,
        fine_out.reshape(64, D),
        gain_merge.reshape(1, -1),
        merge_weight,
        gain_coarse.reshape(1, -1),
        coarse_qkv.transpose(1, 2, 0),
        coarse_out.reshape(128, DC),
        up_weight,
        cotangent,
    )
    next_fields, fields_grad, fine_grad, merge_grad = pl.pallas_call(
        hand_over,
        out_shape=tuple(jax.ShapeDtypeStruct(some.shape, some.dtype) for some in results),
        in_specs=[whole] * 4,
        out_specs=[whole] * 4,
        name="hand_over",
    )(*results)
    return next_fields, fields_grad.reshape(2, LEV, LON // TP, D), fine_grad, merge_grad


def solution(mesh):
    placed = (
        P("lat", None, None, None),
        P("lat", None),
        P(),
        P(),
        P(None, "tp", None),
        P("tp", None, None),
        P(),
        P(None, "tp"),
        P(),
        P(None, "tp", None),
        P("tp", None, None),
        P(None, "tp"),
        P("lat", None, None, None),
    )
    return jax.shard_map(
        functools.partial(local, mesh.shape["lat"]),
        mesh=mesh,
        in_specs=placed,
        out_specs=(
            P("lat", None, None, None),
            P("lat", None, "tp", None),
            P("lat", "tp", None),
            P("lat", "tp"),
        ),
        check_vma=False,
    )
```

```python
import functools

import jax
import jax.numpy as jnp
from jax import lax
from jax.experimental import pallas as pl
from jax.experimental.pallas import tpu as pltpu
from jax.sharding import PartitionSpec as P

MESH = pl.DeviceIdType.MESH
F32 = jnp.float32
BF16 = jnp.bfloat16
EPSILON = 1e-05
NEGATIVE = -1e30

D = 512
DC = 1024
LEV = 4
LON = 64
ZH = 2
YS = 4
TP = ZH * YS
ROW = LEV * LON
CTOK = ROW // 2
SHARE = ROW // TP
CSHARE = CTOK // TP
HALF = ROW // ZH
CHALF = CTOK // ZH
SCALE = 0.125


def dot(a, b):
    return lax.dot_general(a, b, (((1,), (0,)), ((), ())), preferred_element_type=F32)


def dot_nt(a, b):
    return lax.dot_general(a, b, (((1,), (1,)), ((), ())), preferred_element_type=F32)


def dot_tn(a, b):
    return lax.dot_general(a, b, (((0,), (0,)), ((), ())), preferred_element_type=F32)


def standardize(values):
    centred = values - jnp.mean(values, axis=-1, keepdims=True)
    spread = jnp.mean(centred * centred, axis=-1, keepdims=True)
    inverse = lax.rsqrt(spread + EPSILON)
    return centred * inverse, inverse


def normalize_back(values, gain, incoming):
    unit, inverse = standardize(values)
    inner = incoming * gain
    first = jnp.mean(inner, axis=-1, keepdims=True)
    second = jnp.mean(inner * unit, axis=-1, keepdims=True)
    return inverse * (inner - first - unit * second)


class Links:
    def __init__(self, send_sems, recv_sems):
        self.send_sems, self.recv_sems = send_sems, recv_sems
        self.copies = []

    def copy(self, src, dst, device):
        at = len(self.copies)
        made = pltpu.make_async_remote_copy(
            src_ref=src,
            dst_ref=dst,
            send_sem=self.send_sems.at[at],
            recv_sem=self.recv_sems.at[at],
            device_id=device,
            device_id_type=MESH,
        )
        self.copies.append(made)
        return made

    def finish(self):
        for made in self.copies:
            made.wait_send()


class Group:
    def __init__(self, links):
        self.links = links
        self.tp = lax.axis_index("tp")
        self.zh, self.y = lax.div(self.tp, YS), lax.rem(self.tp, YS)
        self.other = lax.rem(self.tp + YS, TP)

    def y_at(self, k):
        return lax.rem(self.y + k, YS)

    def along_y(self, k):
        return {"tp": self.zh * YS + self.y_at(k)}


class Gather:
    def __init__(self, group, view):
        links = group.links
        own, far = view(group.tp), view(group.other)
        self.over_z = links.copy(own, own, {"tp": group.other})
        self.over_y = [links.copy(own, own, group.along_y(k)) for k in range(1, YS)]
        self.passed = [links.copy(far, far, group.along_y(k)) for k in range(1, YS)]

    def start(self):
        for made in [self.over_z] + self.over_y:
            made.start()

    def forward(self):
        self.over_z.wait_recv()
        for made in self.passed:
            made.start()

    def finish(self):
        for made in self.over_y + self.passed:
            made.wait_recv()


class HalfGather:
    def __init__(self, group, view, near):
        links, far = group.links, 1 - near
        sent, own, passed = view(group.tp, far), view(group.tp, near), view(group.other, near)
        self.over_z = links.copy(sent, sent, {"tp": group.other})
        self.over_y = [links.copy(own, own, group.along_y(k)) for k in range(1, YS)]
        self.passed = [links.copy(passed, passed, group.along_y(k)) for k in range(1, YS)]

    start, forward, finish = Gather.start, Gather.forward, Gather.finish


class GatherY:
    def __init__(self, group, refs):
        self.copies = [
            group.links.copy(some, some, group.along_y(k)) for k in range(1, YS) for some in refs
        ]

    def start(self):
        for made in self.copies:
            made.start()

    def finish(self):
        for made in self.copies:
            made.wait_recv()


class ScatterY:
    def __init__(self, group, terms, came):
        self.group, self.terms, self.came = group, terms, came
        self.copies = [
            group.links.copy(terms.at[group.y_at(k)], came.at[k - 1], group.along_y(k))
            for k in range(1, YS)
        ]

    start, wait = GatherY.start, GatherY.finish

    def finish(self):
        self.wait()
        total = self.terms[self.group.y].astype(F32)
        for k in range(YS - 1):
            total = total + self.came[k].astype(F32)
        return total


class Scatter:
    def __init__(self, group, terms, came_y, half, came_z):
        self.group, self.terms = group, terms
        self.came_y, self.half, self.came_z = came_y, half, came_z
        links = group.links
        self.over_y = [
            links.copy(terms.at[:, group.y_at(k)], came_y.at[k - 1], group.along_y(k))
            for k in range(1, YS)
        ]
        self.over_z = links.copy(half, came_z, {"tp": group.other})

    def start(self):
        for made in self.over_y:
            made.start()

    def summed(self, zh):
        total = self.terms[zh, self.group.y].astype(F32)
        for k in range(YS - 1):
            total = total + self.came_y[k, zh].astype(F32)
        return total

    def middle(self):
        for made in self.over_y:
            made.wait_recv()
        self.half[...] = self.summed(1 - self.group.zh).astype(BF16)
        self.over_z.start()

    def finish(self):
        own = self.summed(self.group.zh)
        self.over_z.wait_recv()
        return own + self.came_z[...].astype(F32)


class Moments:
    def __init__(self, group, own, came):
        self.own, self.came = own, came
        self.copies = [
            group.links.copy(own, came.at[k - 1], group.along_y(k)) for k in range(1, YS)
        ]

    def start(self, inner, unit):
        first = jnp.mean(inner, axis=-1, keepdims=True)
        second = jnp.mean(inner * unit, axis=-1, keepdims=True)
        lane = lax.broadcasted_iota(jnp.int32, (CHALF, 128), 1)
        both = jnp.where(lane == 0, first, jnp.where(lane == 1, second, 0.0))
        both = jnp.concatenate([both, jnp.zeros((128 - CHALF, 128), F32)], axis=0)
        self.own[...] = both.T[0:8]
        for made in self.copies:
            made.start()

    def finish(self):
        total = self.own[...]
        for k in range(YS - 1):
            self.copies[k].wait_recv()
            total = total + self.came[k]
        both = jnp.concatenate([total, jnp.zeros((120, 128), F32)], axis=0).T
        return both[0:CHALF, 0:1], both[0:CHALF, 1:2]


class LatSum:
    def __init__(self, links, place, terms, came_x, part, came_z):
        self.place, self.terms, self.came_x, self.part, self.came_z = (
            place,
            terms,
            came_x,
            part,
            came_z,
        )
        self.over_x = [
            links.copy(terms.at[x, :, core], came_x.at[k], place.at(x, place.z, core))
            for k, (x, core) in enumerate(place.x_peers)
        ]
        self.over_z = [
            links.copy(part.at[z], came_z.at[k], place.at(place.x, z, place.core))
            for k, z in enumerate(place.z_peers)
        ]

    def start(self):
        for made in self.over_x:
            made.start()

    def middle(self):
        for made in self.over_x:
            made.wait_recv()
        total = self.terms[self.place.x, :, self.place.core].astype(F32)
        for k in range(len(self.over_x)):
            total = total + self.came_x[k].astype(F32)
        self.part[...] = total.astype(BF16)
        for made in self.over_z:
            made.start()

    def finish(self):
        for made in self.over_z:
            made.wait_recv()
        total = self.part[self.place.z].astype(F32)
        for k in range(len(self.over_z)):
            total = total + self.came_z[k].astype(F32)
        return total


class FarWeights:
    def __init__(self, group, place, sources, targets):
        links, nx, nz = group.links, place.nx, place.nz
        mine = 2 * place.x + place.core
        (merge, coarse), (far_merge, far_coarse) = sources, targets
        merge_rows, coarse_rows = 4 * D // (2 * nx), 512 // (2 * nx)
        rows, lanes = merge_rows // nz, DC // nz

        def piece(refs):
            start = pl.multiple_of(mine * merge_rows + place.z * rows, rows)
            return [
                refs[0].at[pl.ds(start, rows)],
                refs[1].at[aligned(mine, coarse_rows), aligned(place.z, lanes)],
            ]

        def plane(x):
            at = 2 * x + place.core
            return [
                far_merge.at[aligned(at, merge_rows)],
                far_coarse.at[aligned(at, coarse_rows)],
            ]

        got = piece(targets)
        self.fetched = [
            links.copy(src, dst, {"tp": group.other}) for src, dst in zip(piece(sources), got)
        ]
        self.along_z = [
            links.copy(some, some, place.at(place.x, z, place.core))
            for z in place.z_peers
            for some in got
        ]
        self.along_x = [
            links.copy(some, some, place.at(x, place.z, core))
            for x, core in place.x_peers[1::2]
            for some in plane(place.x)
        ]
        self.to_twin = [
            links.copy(some, some, place.at(place.x, place.z, 1 - place.core))
            for x in range(nx)
            for some in plane(x)
        ]

    def start(self):
        for made in self.fetched:
            made.start()

    def pass_z(self):
        for made in self.fetched:
            made.wait_recv()
        for made in self.along_z:
            made.start()

    def pass_x(self):
        for made in self.along_z:
            made.wait_recv()
        for made in self.along_x:
            made.start()

    def pass_core(self):
        for made in self.along_x:
            made.wait_recv()
        for made in self.to_twin:
            made.start()

    def finish(self, which):
        for made in self.to_twin[which::2]:
            made.wait_recv()


class Place:
    def __init__(self, nx, nz):
        lat = lax.axis_index("lat")
        self.nx, self.nz = nx, nz
        self.core = lax.rem(lat, 2)
        self.z = lax.rem(lax.div(lat, 2), nz)
        self.x = lax.div(lat, 2 * nz)
        self.x_peers = [
            (lax.rem(self.x + i, nx), lax.rem(self.core + j, 2))
            for i in range(nx)
            for j in range(2)
            if i or j
        ]
        self.z_peers = [lax.rem(self.z + k, nz) for k in range(1, nz)]

    def at(self, x, z, core):
        return {"lat": (x * self.nz + z) * 2 + core}


def aligned(index, size):
    return pl.ds(pl.multiple_of(index * size, size), size)


def put(ref, rows, values):
    for j in range(values.shape[1] // 128):
        ref[j, rows, :] = values[:, 128 * j : 128 * j + 128]


def get(ref, rows):
    return jnp.concatenate([ref[j, rows, :] for j in range(ref.shape[0])], axis=1)


def softmax_pair(own, other):
    largest = jnp.maximum(
        jnp.max(own, axis=-1, keepdims=True), jnp.max(other, axis=-1, keepdims=True)
    )
    own, other = jnp.exp(own - largest), jnp.exp(other - largest)
    total = jnp.sum(own, axis=-1, keepdims=True) + jnp.sum(other, axis=-1, keepdims=True)
    return own / total, other / total


def score_grads(prob_own, prob_other, grad_own, grad_other):
    mean = jnp.sum(grad_own * prob_own, axis=-1, keepdims=True)
    mean = mean + jnp.sum(grad_other * prob_other, axis=-1, keepdims=True)
    return (
        (prob_own * (grad_own - mean) * SCALE).astype(BF16),
        (prob_other * (grad_other - mean) * SCALE).astype(BF16),
    )


def low_lanes(values):
    lane = lax.broadcasted_iota(jnp.int32, values.shape, 1)
    return jnp.where(lane < 64, values, 0.0)


def high_lanes(values):
    lane = lax.broadcasted_iota(jnp.int32, values.shape, 1)
    return jnp.where(lane >= 64, values, 0.0)


def fine_mask(start):
    def window(index):
        return ((index >> 5) + 7 + ((index & 7) >> 2)) & 7

    query = lax.broadcasted_iota(jnp.int32, (CTOK, ROW), 0) + start
    key = lax.broadcasted_iota(jnp.int32, (CTOK, ROW), 1)
    return window(query) == window(key)


def main_kernel(
    lat_count,
    nx,
    nz,
    fields,
    classes,
    class_table,
    gain_fine,
    fine_w,
    fine_out,
    gain_merge,
    merge_weight_in,
    gain_coarse,
    coarse_w_in,
    coarse_out_in,
    up_weight_in,
    cotangent_in,
    next_fields,
    fields_grad,
    fine_grad,
    merge_grad,
    send_sems,
    recv_sems,
    local_sems,
    merge_weight,
    own_coarse,
    far_merge,
    far_coarse,
    up_weight,
    cotangent,
    fields_out,
    hid,
    cotf,
    normed,
    queries,
    keys,
    keys_sent,
    keys_came,
    prob_own,
    prob_other,
    mixture,
    heads_all,
    wexp,
    cexp,
    resid,
    merged_norm,
    coarse_all,
    coarse_f,
    lift_all,
    lift_terms,
    lift_y,
    lift_half,
    lift_z,
    ckeys,
    ckeys_came,
    cback,
    cback_came,
    cs_terms,
    cs_y,
    cn_terms,
    cn_y,
    cunit,
    cinverse,
    cm_own,
    cm_y,
    grad_columns,
    far_columns,
    lifted_all,
    mn_terms,
    mn_y,
    up_all,
    up_wide,
    munit,
    minverse,
    mm_own,
    mm_y,
    gh_terms,
    gh_y,
    mix_sent,
    mix_came,
    grad_mix,
    mix_all,
    grad_mix_rows,
    grad_resid,
    grad_q,
    grad_kv,
    grad_other,
    back,
    back_came,
    gn_terms,
    gn_y,
    gn_half,
    gn_z,
    mterms,
    mcame_x,
    mpart,
    mcame_z,
    fterms,
    fcame_x,
    fpart,
    fcame_z,
):
    def fetch(src, dst, at):
        made = pltpu.make_async_copy(src, dst, local_sems.at[at])
        made.start()
        return made

    got_cotangent = fetch(cotangent_in, cotangent, 0)
    got_up = fetch(up_weight_in, up_weight, 1)
    got_merge = fetch(merge_weight_in, merge_weight, 2)
    got_coarse = [
        fetch(coarse_w_in.at[0], own_coarse.at[pl.ds(0, 192)], 3),
        fetch(coarse_w_in.at[1], own_coarse.at[pl.ds(192, 192)], 4),
        fetch(coarse_out_in, own_coarse.at[pl.ds(384, 128)], 5),
    ]

    links = Links(send_sems, recv_sems)
    group = Group(links)
    tp = group.tp
    lat = lax.axis_index("lat")
    before, after = lax.rem(lat + lat_count - 1, lat_count), lax.rem(lat + 1, lat_count)
    twin = lat + 1 - 2 * lax.rem(lat, 2)

    barrier = pltpu.get_barrier_semaphore()
    for k in range(1, TP):
        pl.semaphore_signal(
            barrier, inc=1, device_id={"tp": lax.rem(tp + k, TP)}, device_id_type=MESH
        )
    place = Place(nx, nz)
    lat_peers = [{"lat": before}, {"lat": after}]
    lat_peers += [place.at(x, place.z, core) for x, core in place.x_peers]
    lat_peers += [place.at(place.x, z, place.core) for z in place.z_peers]
    for peer in lat_peers:
        pl.semaphore_signal(barrier, inc=1, device_id=peer, device_id_type=MESH)

    blank = jnp.zeros((TP, 64, D), BF16)
    wexp[:, 0:64] = blank
    wexp[:, 128:192] = blank
    wexp[tp, 64:128] = fine_out[...]
    for head in range(4):
        cexp[head, 0:64] = jnp.zeros((64, DC), BF16)

    gather_w = Gather(group, lambda at: wexp.at[at, pl.ds(64, 64)])
    lift = Scatter(group, lift_terms, lift_y, lift_half, lift_z)
    send_keys = [
        links.copy(keys_sent.at[1], keys_came.at[0], {"lat": after}),
        links.copy(keys_sent.at[0], keys_came.at[1], {"lat": before}),
    ]
    zh, other = group.zh, group.other
    far_half = 1 - zh

    def head_slot(at, half):
        return heads_all.at[aligned(half, HALF), aligned(at, 128)]

    near_heads = HalfGather(group, head_slot, zh)
    far_heads = HalfGather(group, head_slot, far_half)
    gather_lift = GatherY(group, [lift_all.at[aligned(group.y, CSHARE)]])
    gather_coarse = GatherY(
        group, [coarse_all.at[:, aligned(tp, 128)], coarse_all.at[:, aligned(other, 128)]]
    )
    far = FarWeights(group, place, (merge_weight, own_coarse), (far_merge, far_coarse))
    send_ckeys = links.copy(ckeys, ckeys_came, {"lat": twin})
    send_cback = links.copy(cback, cback_came, {"lat": twin})
    csum = ScatterY(group, cs_terms, cs_y)
    cnorm = ScatterY(group, cn_terms, cn_y)
    cmoments = Moments(group, cm_own, cm_y)
    swap_columns = links.copy(grad_columns.at[far_half], far_columns, {"tp": other})
    gather_lifted = Gather(group, lambda at: lifted_all.at[aligned(at, CSHARE)])
    mnorm = ScatterY(group, mn_terms, mn_y)
    gather_up = Gather(group, lambda at: up_all.at[at])
    mmoments = Moments(group, mm_own, mm_y)
    gheads = [ScatterY(group, gh_terms.at[z], gh_y.at[z]) for z in (far_half, zh)]
    swap_mix = links.copy(mix_sent, mix_came, {"tp": other})
    send_back = [
        links.copy(back.at[0], back_came.at[1], {"lat": before}),
        links.copy(back.at[1], back_came.at[0], {"lat": after}),
    ]
    gnorm = [
        Scatter(group, gn_terms.at[r], gn_y.at[r], gn_half.at[r], gn_z.at[r]) for r in range(2)
    ]
    merge_sum = LatSum(links, place, mterms, mcame_x, mpart, mcame_z)
    fine_sum = LatSum(links, place, fterms, fcame_x, fpart, fcame_z)

    embedded = []
    for r in range(2):
        kinds = lax.broadcasted_iota(jnp.int32, (8, LON), 0)
        onehot = jnp.where(classes[r : r + 1, :] == kinds, 1.0, 0.0).astype(BF16)
        embedded.append(dot_tn(onehot, class_table[...]))
    for r in range(2):
        for level in range(LEV):
            full = fields[r, level].astype(F32) + embedded[r]
            for block in range(TP):
                at = r * ROW + block * SHARE + level * 8
                hid[at : at + 8] = full[8 * block : 8 * block + 8]

    for i in range(4):
        chunk = pl.ds(i * 128, 128)
        unit, _ = standardize(hid[chunk])
        normed[chunk] = (unit * gain_fine[...]).astype(BF16)
    for r in range(2):
        rows = pl.ds(r * ROW, ROW)
        queries[rows] = low_lanes(dot_nt(normed[rows], fine_w[0:128])).astype(BF16)
        kv = dot_nt(normed[rows], fine_w[64:192]).astype(BF16)
        keys[r] = kv
        keys_sent[r] = kv

    pl.semaphore_wait(barrier, TP - 1 + len(lat_peers))
    for made in send_keys:
        made.start()
    gather_w.start()
    got_merge.wait()
    for made in got_coarse:
        made.wait()
    far.start()

    got_cotangent.wait()
    got_up.wait()
    for r in range(2):
        for level in range(LEV):
            cots = cotangent[r, level].astype(F32)
            for block in range(TP):
                at = r * ROW + block * SHARE + level * 8
                put(cotf, pl.ds(at, 8), cots[8 * block : 8 * block + 8])
    kind = lax.div(tp, 2)
    quad = get(cotf, pl.ds(lax.div(kind, 2) * ROW + lax.rem(kind, 2), CTOK, stride=2))
    quad = jnp.where(lax.rem(tp, 2) == 0, quad[:, 0:256], quad[:, 256:512]).astype(BF16)
    lift_terms[...] = dot_nt(quad, up_weight[...]).astype(BF16).reshape(ZH, YS, CSHARE, DC)
    lift.start()
    far.pass_z()

    for made in send_keys:
        made.wait_recv()
    gather_w.forward()

    present = (lat > 0, lat < lat_count - 1)

    def attend(r, half):
        start = r * ROW + half * CTOK
        chunk = pl.ds(start, CTOK)
        mask = fine_mask(half * CTOK)
        query = queries[chunk]
        own = jnp.where(mask, dot_nt(query, keys[r]) * SCALE, NEGATIVE)
        far = dot_nt(query, keys_came[r]) * SCALE
        far = jnp.where(jnp.logical_and(mask, present[r]), far, NEGATIVE)
        own, far = softmax_pair(own, far)
        prob_own[chunk] = own
        prob_other[chunk] = far
        mixture[chunk] = dot(own.astype(BF16), keys[r]) + dot(far.astype(BF16), keys_came[r])

    for r in range(2):
        for half in range(2):
            attend(r, half)
    lane = lax.broadcasted_iota(jnp.int32, (ROW, 128), 1)
    packed = jnp.where(lane < 64, pltpu.roll(mixture[ROW : 2 * ROW], 64, 1), mixture[0:ROW])
    heads_all[:, aligned(tp, 128)] = packed.astype(BF16)
    near_heads.start()
    far_heads.start()

    lift.middle()
    far.pass_x()
    gather_w.finish()
    near_heads.forward()
    lift_chunk = lift.finish().astype(BF16)
    lift_all[aligned(group.y, CSHARE)] = lift_chunk
    gather_lift.start()
    far.pass_core()
    far_heads.forward()
    near_heads.finish()

    low = wexp[:, 0:128].reshape(TP * 128, D)
    high = wexp[:, 64:192].reshape(TP * 128, D)

    def merge(half):
        for r, weight in ((0, low), (1, high)):
            rows = pl.ds(pl.multiple_of(r * ROW + half * HALF, HALF), HALF)
            put(resid, rows, hid[rows] + dot(heads_all[aligned(half, HALF)], weight))
        quads = [
            get(resid, pl.ds(r * ROW + half * HALF + s, CHALF, stride=2))
            for r in range(2)
            for s in range(2)
        ]
        unit, inverse = standardize(jnp.concatenate(quads, axis=1))
        merged_norm[aligned(half, CHALF)] = (unit * gain_merge[...]).astype(BF16)
        return unit, inverse

    unit, inverse = merge(zh)
    near_merged = merged_norm[aligned(zh, CHALF)]
    coarse_all[:, aligned(tp, 128)] = dot(near_merged, merge_weight[...]).astype(BF16)
    far.finish(0)
    coarse_all[:, aligned(other, 128)] = dot(near_merged, far_merge[...]).astype(BF16)
    gather_coarse.start()
    munit[...] = unit
    minverse[...] = jnp.broadcast_to(inverse, (CHALF, 128))
    far.finish(1)
    gather_lift.finish()
    stacks = [(own_coarse, 0), (own_coarse, 1), (far_coarse, 0), (far_coarse, 1)]
    for head, (stack, at) in enumerate(stacks):
        cexp[head, 64:128] = stack[384 + 64 * at : 448 + 64 * at]
    grad_cmix = [dot_nt(lift_all[...], cexp[head]).astype(BF16) for head in range(4)]
    gather_coarse.finish()

    coarse_f[...] = coarse_all[...].astype(F32)
    unit, inverse = standardize(coarse_f[...])
    cnormed = (unit * gain_coarse[...]).astype(BF16)
    for head, (stack, at) in enumerate(stacks):
        rows = stack[192 * at + 64 : 192 * at + 192]
        ckeys[head] = dot_nt(cnormed, rows).astype(BF16)
    send_ckeys.start()
    cunit[...] = unit
    cinverse[...] = jnp.broadcast_to(inverse, (CHALF, 128))
    cq = [
        low_lanes(dot_nt(cnormed, stack[192 * at : 192 * at + 128])).astype(BF16)
        for stack, at in stacks
    ]

    row_at = lax.broadcasted_iota(jnp.int32, (CHALF, CHALF), 0)
    col_at = lax.broadcasted_iota(jnp.int32, (CHALF, CHALF), 1)
    cmask = (row_at >> 5) == (col_at >> 5)
    own_scores = [
        jnp.where(cmask, dot_nt(cq[head], ckeys[head]) * SCALE, NEGATIVE) for head in range(4)
    ]
    send_ckeys.wait_recv()
    cgrad_q, cgrad_kv = [], []
    cheads = []
    for head in range(4):
        away = jnp.where(cmask, dot_nt(cq[head], ckeys_came[head]) * SCALE, NEGATIVE)
        own, away = softmax_pair(own_scores[head], away)
        own16, far16 = own.astype(BF16), away.astype(BF16)
        grad_own = dot_nt(grad_cmix[head], ckeys[head])
        grad_far = dot_nt(grad_cmix[head], ckeys_came[head])
        ds_own, ds_far = score_grads(own, away, grad_own, grad_far)
        cback[head] = (dot_tn(ds_far, cq[head]) + dot_tn(far16, grad_cmix[head])).astype(BF16)
        cgrad_kv.append(dot_tn(ds_own, cq[head]) + dot_tn(own16, grad_cmix[head]))
        query_grad = dot(ds_own, ckeys[head]) + dot(ds_far, ckeys_came[head])
        cgrad_q.append(low_lanes(query_grad).astype(BF16))
        cheads.append((dot(own16, ckeys[head]) + dot(far16, ckeys_came[head])).astype(BF16))
    send_cback.start()
    part = sum(dot(cheads[head], cexp[head]) for head in range(4))
    cs_terms[...] = part.astype(BF16).reshape(YS, CSHARE, DC)
    part = 0.0
    for head, (stack, at) in enumerate(stacks):
        part = part + dot(cgrad_q[head], stack[192 * at : 192 * at + 128])
    send_cback.wait_recv()
    for head, (stack, at) in enumerate(stacks):
        total = (cgrad_kv[head] + cback_came[head].astype(F32)).astype(BF16)
        part = part + dot(total, stack[192 * at + 64 : 192 * at + 192])
    for t in range(TP):
        cn_terms[t % YS, t // YS] = part[:, 128 * t : 128 * t + 128].astype(BF16)
    cnorm.start()
    cmoments.start(part * gain_coarse[...], cunit[...])
    csum.start()

    def one_head(at, top, bottom):
        top, bottom = top.astype(BF16), bottom.astype(BF16)
        return dot_nt(top, wexp[at, 0:128]) + dot_nt(bottom, wexp[at, 64:192])

    ones = jnp.ones((8, D), BF16)
    head_terms = []
    for at in (other, tp):
        terms = []
        for s in range(2):
            cot = [get(cotf, pl.ds(r * ROW + zh * HALF + s, CHALF, stride=2)) for r in range(2)]
            unit = [munit[:, (2 * r + s) * D : (2 * r + s + 1) * D] for r in range(2)]
            terms.append((one_head(at, *cot), one_head(at, *unit)))
        head_terms.append((terms, one_head(at, ones, ones)[0:1]))

    grad_cn = cnorm.finish()
    first, second = cmoments.finish()
    for zc in range(ZH):
        lane_block = aligned(zc * YS + group.y, 128)
        inner = grad_cn[zc] * gain_coarse[:, lane_block]
        inner = cinverse[...] * (inner - first - cunit[:, lane_block] * second)
        grad_columns[zc] = (lift_all[:, lane_block].astype(F32) + inner).astype(BF16)

    part = dot_nt(grad_columns[zh], merge_weight[...])
    part = part + dot_nt(grad_columns[far_half], far_merge[...])
    inner = part * gain_merge[...]
    inner16 = inner.astype(BF16)
    for s in range(2):
        top, bottom = [inner16[:, (2 * r + s) * D : (2 * r + s + 1) * D] for r in range(2)]
        heads = (dot_nt(top, low) + dot_nt(bottom, high)).astype(BF16)
        for t in range(TP):
            some = heads[:, 128 * t : 128 * t + 128]
            gh_terms[t // YS, t % YS, s * CHALF : (s + 1) * CHALF] = some
    for part_sum in gheads:
        part_sum.start()
    mmoments.start(inner, munit[...])
    swap_columns.start()
    mn_terms[...] = part.astype(BF16).reshape(YS, CSHARE, 4 * D)
    mnorm.start()

    mine = aligned(tp, CSHARE)
    near_mine = aligned(group.y, CSHARE)
    lifted_all[mine] = (coarse_f[near_mine] + csum.finish()).astype(BF16)

    first, second = mmoments.finish()
    for i, (terms, head_ones) in enumerate(head_terms):
        grad_heads = gheads[i].finish()
        for s in range(2):
            head_cot, head_unit = terms[s]
            inner = grad_heads[s * CHALF : (s + 1) * CHALF] - first * head_ones - second * head_unit
            put(grad_mix, pl.ds(s, CHALF, stride=2), head_cot + minverse[...] * inner)
        if i == 0:
            mix_sent[...] = grad_mix[0].astype(BF16)
            swap_mix.start()
    mix_all[aligned(zh, HALF)] = grad_mix[0]
    gather_lifted.start()

    far_heads.finish()
    merge(far_half)
    swap_columns.wait_recv()
    scale = (2 * lat_count * LEV * LON) ** -0.5
    merge_rows = 4 * D // lat_count
    weight_rows = D // lat_count
    term = dot_tn(merged_norm[aligned(zh, CHALF)], grad_columns[zh])
    term = term + dot_tn(merged_norm[aligned(far_half, CHALF)], far_columns[...])
    mterms[...] = (term * scale).astype(BF16).reshape(nx, nz, 2, merge_rows, 128)
    swap_mix.wait_recv()
    mix_all[aligned(far_half, HALF)] = mix_came[...].astype(F32)
    merge_sum.start()
    gather_lifted.forward()
    both = mix_all[...]
    grad_mix_rows[0:ROW] = high_lanes(both).astype(BF16)
    grad_mix_rows[ROW : 2 * ROW] = high_lanes(pltpu.roll(both, 64, 1)).astype(BF16)

    def attend_back(r, half):
        chunk = pl.ds(r * ROW + half * CTOK, CTOK)
        query, grad_out = queries[chunk], grad_mix_rows[chunk]
        own, far = prob_own[chunk], prob_other[chunk]
        ds_own, ds_far = score_grads(
            own, far, dot_nt(grad_out, keys[r]), dot_nt(grad_out, keys_came[r])
        )
        own16, far16 = own.astype(BF16), far.astype(BF16)
        to_own = dot_tn(ds_own, query) + dot_tn(own16, grad_out)
        to_far = dot_tn(ds_far, query) + dot_tn(far16, grad_out)
        grad_q[chunk] = low_lanes(dot(ds_own, keys[r]) + dot(ds_far, keys_came[r])).astype(BF16)
        return to_own, to_far

    for r in range(2):
        own_a, far_a = attend_back(r, 0)
        own_b, far_b = attend_back(r, 1)
        back[r] = (far_a + far_b).astype(BF16)
        send_back[r].start()
        grad_other[r] = own_a + own_b
    gather_lifted.finish()
    up_all[tp] = dot(lifted_all[...], up_weight[...]).astype(BF16)
    gather_up.start()
    merge_sum.middle()
    for made in send_back:
        made.wait_recv()
    for r in range(2):
        grad_kv[pl.ds(r * ROW, ROW)] = (grad_other[r] + back_came[r].astype(F32)).astype(BF16)
    for r in range(2):
        rows = pl.ds(r * ROW, ROW)
        part = dot(grad_q[rows], fine_w[0:128]) + dot(grad_kv[rows], fine_w[64:192])
        gn_terms[r] = part.astype(BF16).reshape(ZH, YS, SHARE, D)
        gnorm[r].start()

    term_q = dot_tn(normed[...], grad_q[...]) * scale
    term_kv = dot_tn(normed[...], grad_kv[...]) * scale
    term = jnp.concatenate(
        [term_q.reshape(lat_count, weight_rows, 128), term_kv.reshape(lat_count, weight_rows, 128)],
        axis=1,
    )
    fterms[...] = term.astype(BF16).reshape(nx, nz, 2, 2 * weight_rows, 128)
    fine_sum.start()
    gather_up.forward()
    for part in gnorm:
        part.middle()
    fine_sum.middle()

    grad_mn = mnorm.finish()
    merged_chunk, cot_chunk = [], []
    for r in range(2):
        for s in range(2):
            some = pl.ds(r * ROW + s + tp * SHARE, CSHARE, stride=2)
            merged_chunk.append(get(resid, some))
            cot_chunk.append(get(cotf, some))
    merged_chunk = jnp.concatenate(merged_chunk, axis=1)
    cot_chunk = jnp.concatenate(cot_chunk, axis=1)
    grad_quads = cot_chunk + normalize_back(merged_chunk, gain_merge[...], grad_mn)
    for r in range(2):
        for s in range(2):
            some = grad_quads[:, (2 * r + s) * D : (2 * r + s + 1) * D]
            put(grad_resid, pl.ds(r * SHARE + s, CSHARE, stride=2), some)

    gather_up.finish()
    for r in range(2):
        for s in range(2):
            for part in range(2):
                wide = up_all[4 * r + 2 * s + part].astype(F32)
                some = pl.ds(r * ROW + s, CTOK, stride=2)
                up_wide[2 * part, some, :] = wide[:, 0:128]
                up_wide[2 * part + 1, some, :] = wide[:, 128:256]
    for r in range(2):
        for level in range(LEV):
            pieces = []
            for block in range(TP):
                at = r * ROW + block * SHARE + level * 8
                pieces.append(get(resid, pl.ds(at, 8)) + get(up_wide, pl.ds(at, 8)))
            fields_out[r, level] = jnp.concatenate(pieces, axis=0).astype(BF16)
    written = fetch(fields_out, next_fields, 6)

    for r in range(2):
        grad_norm = gnorm[r].finish()
        own_hidden = hid[pl.ds(pl.multiple_of(r * ROW + tp * SHARE, SHARE), SHARE)]
        grad_hidden = normalize_back(own_hidden, gain_fine[...], grad_norm)
        grad_hidden = grad_hidden + get(grad_resid, pl.ds(r * SHARE, SHARE))
        fields_grad[r] = grad_hidden.astype(BF16)
    merge_grad[...] = merge_sum.finish()
    sums = fine_sum.finish()
    fine_grad[:, 0, 0:64] = sums[0:weight_rows, 0:64]
    fine_grad[:, 0, 64:192] = sums[weight_rows : 2 * weight_rows]
    written.wait()
    links.finish()


def hand_over(*refs):
    for i in range(4):
        refs[4 + i][...] = refs[i][...]


def vmem(*shape, kind=BF16):
    return pltpu.VMEM(shape, kind)


def scatter_buffers(*chunk):
    return [vmem(ZH, YS, *chunk), vmem(YS - 1, ZH, *chunk), vmem(*chunk), vmem(*chunk)]


def halved(*buffers):
    return [vmem(2, *some.shape) for some in buffers]


def y_buffers(*chunk):
    return [vmem(YS, *chunk), vmem(YS - 1, *chunk)]


def moment_buffers():
    return [vmem(8, 128, kind=F32), vmem(YS - 1, 8, 128, kind=F32)]


def lat_buffers(nx, nz, rows):
    return [
        vmem(nx, nz, 2, rows, 128),
        vmem(2 * nx - 1, nz, rows, 128),
        vmem(nz, rows, 128),
        vmem(nz - 1, rows, 128),
    ]


def local(
    lat_count,
    fields,
    classes,
    class_table,
    gain_fine,
    fine_qkv,
    fine_out,
    gain_merge,
    merge_weight,
    gain_coarse,
    coarse_qkv,
    coarse_out,
    up_weight,
    cotangent,
):
    merge_rows, weight_rows = 4 * D // lat_count, D // lat_count
    nz = min(8, lat_count // 4)
    nx = lat_count // (2 * nz)
    whole = pl.BlockSpec(memory_space=pltpu.VMEM)
    left = pl.BlockSpec(memory_space=pl.ANY)
    copies = 240
    scratch = [
        pltpu.SemaphoreType.DMA((copies,)),
        pltpu.SemaphoreType.DMA((copies,)),
        pltpu.SemaphoreType.DMA((7,)),
        vmem(4 * D, 128),
        vmem(512, DC),
        vmem(4 * D, 128),
        vmem(512, DC),
        vmem(DC, 256),
        vmem(2, LEV, LON, D),
        vmem(2, LEV, LON, D),
        vmem(2 * ROW, D, kind=F32),
        vmem(4, 2 * ROW, 128, kind=F32),
        vmem(2 * ROW, D),
        vmem(2 * ROW, 128),
        vmem(2, ROW, 128),
        vmem(2, ROW, 128),
        vmem(2, ROW, 128),
        vmem(2 * ROW, ROW, kind=F32),
        vmem(2 * ROW, ROW, kind=F32),
        vmem(2 * ROW, 128, kind=F32),
        vmem(ROW, TP * 128),
        vmem(TP, 192, D),
        vmem(4, 128, DC),
        vmem(4, 2 * ROW, 128, kind=F32),
        vmem(CTOK, 4 * D),
        vmem(CHALF, DC),
        vmem(CHALF, DC, kind=F32),
        vmem(CHALF, DC),
        *scatter_buffers(CSHARE, DC),
        vmem(4, CHALF, 128),
        vmem(4, CHALF, 128),
        vmem(4, CHALF, 128),
        vmem(4, CHALF, 128),
        *y_buffers(CSHARE, DC),
        *y_buffers(ZH, CHALF, 128),
        vmem(CHALF, DC, kind=F32),
        vmem(CHALF, 128, kind=F32),
        *moment_buffers(),
        vmem(ZH, CHALF, 128),
        vmem(CHALF, 128),
        vmem(CTOK, DC),
        *y_buffers(CSHARE, 4 * D),
        vmem(TP, CTOK, 256),
        vmem(4, 2 * ROW, 128, kind=F32),
        vmem(CHALF, 4 * D, kind=F32),
        vmem(CHALF, 128, kind=F32),
        *moment_buffers(),
        *halved(*y_buffers(2 * CHALF, 128)),
        vmem(HALF, 128),
        vmem(HALF, 128),
        vmem(1, HALF, 128, kind=F32),
        vmem(ROW, 128, kind=F32),
        vmem(2 * ROW, 128),
        vmem(4, 2 * SHARE, 128, kind=F32),
        vmem(2 * ROW, 128),
        vmem(2 * ROW, 128),
        vmem(2, ROW, 128, kind=F32),
        vmem(2, ROW, 128),
        vmem(2, ROW, 128),
        *halved(*scatter_buffers(SHARE, D)),
        *lat_buffers(nx, nz, merge_rows),
        *lat_buffers(nx, nz, 2 * weight_rows),
    ]
    results = pl.pallas_call(
        functools.partial(main_kernel, lat_count, nx, nz),
        out_shape=(
            jax.ShapeDtypeStruct((2, LEV, LON, D), BF16),
            jax.ShapeDtypeStruct((2, SHARE, D), BF16),
            jax.ShapeDtypeStruct((weight_rows, 1, 192), F32),
            jax.ShapeDtypeStruct((merge_rows, 128), F32),
        ),
        in_specs=[whole] * 7 + [left, whole] + [left] * 4,
        out_specs=[left] + [whole] * 3,
        scratch_shapes=scratch,
        name="block",
        compiler_params=pltpu.CompilerParams(
            collective_id=0, has_side_effects=True, vmem_limit_bytes=56 * 2**20
        ),
    )(
        fields,
        classes,
        class_table,
        gain_fine.reshape(1, -1),
        fine_qkv.reshape(D, 192).T,
        fine_out.reshape(64, D),
        gain_merge.reshape(1, -1),
        merge_weight,
        gain_coarse.reshape(1, -1),
        coarse_qkv.transpose(1, 2, 0),
        coarse_out.reshape(128, DC),
        up_weight,
        cotangent,
    )
    next_fields, fields_grad, fine_grad, merge_grad = pl.pallas_call(
        hand_over,
        out_shape=tuple(jax.ShapeDtypeStruct(some.shape, some.dtype) for some in results),
        in_specs=[whole] * 4,
        out_specs=[whole] * 4,
        name="hand_over",
    )(*results)
    return next_fields, fields_grad.reshape(2, LEV, LON // TP, D), fine_grad, merge_grad


def solution(mesh):
    placed = (
        P("lat", None, None, None),
        P("lat", None),
        P(),
        P(),
        P(None, "tp", None),
        P("tp", None, None),
        P(),
        P(None, "tp"),
        P(),
        P(None, "tp", None),
        P("tp", None, None),
        P(None, "tp"),
        P("lat", None, None, None),
    )
    return jax.shard_map(
        functools.partial(local, mesh.shape["lat"]),
        mesh=mesh,
        in_specs=placed,
        out_specs=(
            P("lat", None, None, None),
            P("lat", None, "tp", None),
            P("lat", "tp", None),
            P("lat", "tp"),
        ),
        check_vma=False,
    )
```

```python
import functools

import jax
import jax.numpy as jnp
from jax import lax
from jax.experimental import pallas as pl
from jax.experimental.pallas import tpu as pltpu
from jax.sharding import PartitionSpec as P

MESH = pl.DeviceIdType.MESH
F32 = jnp.float32
BF16 = jnp.bfloat16
EPSILON = 1e-05
NEGATIVE = -1e30

D = 512
DC = 1024
LEV = 4
LON = 64
ZH = 2
YS = 4
TP = ZH * YS
ROW = LEV * LON
CTOK = ROW // 2
SHARE = ROW // TP
CSHARE = CTOK // TP
HALF = ROW // ZH
CHALF = CTOK // ZH
SCALE = 0.125


def dot(a, b):
    return lax.dot_general(a, b, (((1,), (0,)), ((), ())), preferred_element_type=F32)


def dot_nt(a, b):
    return lax.dot_general(a, b, (((1,), (1,)), ((), ())), preferred_element_type=F32)


def dot_tn(a, b):
    return lax.dot_general(a, b, (((0,), (0,)), ((), ())), preferred_element_type=F32)


def standardize(values):
    centred = values - jnp.mean(values, axis=-1, keepdims=True)
    spread = jnp.mean(centred * centred, axis=-1, keepdims=True)
    inverse = lax.rsqrt(spread + EPSILON)
    return centred * inverse, inverse


def normalize_back(values, gain, incoming):
    unit, inverse = standardize(values)
    inner = incoming * gain
    first = jnp.mean(inner, axis=-1, keepdims=True)
    second = jnp.mean(inner * unit, axis=-1, keepdims=True)
    return inverse * (inner - first - unit * second)


class Links:
    def __init__(self, send_sems, recv_sems):
        self.send_sems, self.recv_sems = send_sems, recv_sems
        self.copies = []

    def copy(self, src, dst, device):
        at = len(self.copies)
        made = pltpu.make_async_remote_copy(
            src_ref=src,
            dst_ref=dst,
            send_sem=self.send_sems.at[at],
            recv_sem=self.recv_sems.at[at],
            device_id=device,
            device_id_type=MESH,
        )
        self.copies.append(made)
        return made

    def finish(self):
        for made in self.copies:
            made.wait_send()


class Group:
    def __init__(self, links):
        self.links = links
        self.tp = lax.axis_index("tp")
        self.zh, self.y = lax.div(self.tp, YS), lax.rem(self.tp, YS)
        self.other = lax.rem(self.tp + YS, TP)

    def y_at(self, k):
        return lax.rem(self.y + k, YS)

    def along_y(self, k):
        return {"tp": self.zh * YS + self.y_at(k)}


class Gather:
    def __init__(self, group, view):
        links = group.links
        own, far = view(group.tp), view(group.other)
        self.over_z = links.copy(own, own, {"tp": group.other})
        self.over_y = [links.copy(own, own, group.along_y(k)) for k in range(1, YS)]
        self.passed = [links.copy(far, far, group.along_y(k)) for k in range(1, YS)]

    def start(self):
        for made in [self.over_z] + self.over_y:
            made.start()

    def forward(self):
        self.over_z.wait_recv()
        for made in self.passed:
            made.start()

    def finish(self):
        for made in self.over_y + self.passed:
            made.wait_recv()


class HalfGather:
    def __init__(self, group, view, near):
        links, far = group.links, 1 - near
        sent, own, passed = view(group.tp, far), view(group.tp, near), view(group.other, near)
        self.over_z = links.copy(sent, sent, {"tp": group.other})
        self.over_y = [links.copy(own, own, group.along_y(k)) for k in range(1, YS)]
        self.passed = [links.copy(passed, passed, group.along_y(k)) for k in range(1, YS)]

    start, forward, finish = Gather.start, Gather.forward, Gather.finish


class OutGather:
    def __init__(self, group, place, wexp):
        links, rows = group.links, 64 // place.nx

        def piece(at, x, core):
            return wexp.at[at, pl.ds(64 + x * rows, rows), aligned(core, 256)]

        def slot(at):
            return wexp.at[at, pl.ds(64, 64)]

        own, far = slot(group.tp), slot(group.other)
        sent = piece(group.tp, place.x, place.core)
        got = piece(group.other, place.x, place.core)
        self.over_z = links.copy(sent, sent, {"tp": group.other, **place.mirror})
        self.over_y = [links.copy(own, own, group.along_y(k)) for k in range(1, YS)]
        self.shared = [links.copy(got, got, place.at(x, place.z, c)) for x, c in place.x_peers]
        self.passed = [links.copy(far, far, group.along_y(k)) for k in range(1, YS)]

    def share(self):
        self.over_z.wait_recv()
        for made in self.shared:
            made.start()

    def forward(self):
        for made in self.shared:
            made.wait_recv()
        for made in self.passed:
            made.start()

    start, finish = Gather.start, Gather.finish


class GatherY:
    def __init__(self, group, refs):
        self.copies = [
            group.links.copy(some, some, group.along_y(k)) for k in range(1, YS) for some in refs
        ]

    def start(self):
        for made in self.copies:
            made.start()

    def finish(self):
        for made in self.copies:
            made.wait_recv()


class ScatterY:
    def __init__(self, group, terms, came):
        self.group, self.terms, self.came = group, terms, came
        self.copies = [
            group.links.copy(terms.at[group.y_at(k)], came.at[k - 1], group.along_y(k))
            for k in range(1, YS)
        ]

    start, wait = GatherY.start, GatherY.finish

    def finish(self):
        self.wait()
        total = self.terms[self.group.y].astype(F32)
        for k in range(YS - 1):
            total = total + self.came[k].astype(F32)
        return total


class Scatter:
    def __init__(self, group, terms, came_y, half, came_z):
        self.group, self.terms = group, terms
        self.came_y, self.half, self.came_z = came_y, half, came_z
        links = group.links
        self.over_y = [
            links.copy(terms.at[:, group.y_at(k)], came_y.at[k - 1], group.along_y(k))
            for k in range(1, YS)
        ]
        self.over_z = links.copy(half, came_z, {"tp": group.other})

    def start(self):
        for made in self.over_y:
            made.start()

    def summed(self, zh):
        total = self.terms[zh, self.group.y].astype(F32)
        for k in range(YS - 1):
            total = total + self.came_y[k, zh].astype(F32)
        return total

    def middle(self):
        for made in self.over_y:
            made.wait_recv()
        self.half[...] = self.summed(1 - self.group.zh).astype(BF16)
        self.over_z.start()

    def finish(self):
        own = self.summed(self.group.zh)
        self.over_z.wait_recv()
        return own + self.came_z[...].astype(F32)


class Moments:
    def __init__(self, group, own, came):
        self.own, self.came = own, came
        self.copies = [
            group.links.copy(own, came.at[k - 1], group.along_y(k)) for k in range(1, YS)
        ]

    def start(self, inner, unit):
        first = jnp.mean(inner, axis=-1, keepdims=True)
        second = jnp.mean(inner * unit, axis=-1, keepdims=True)
        lane = lax.broadcasted_iota(jnp.int32, (CHALF, 128), 1)
        both = jnp.where(lane == 0, first, jnp.where(lane == 1, second, 0.0))
        both = jnp.concatenate([both, jnp.zeros((128 - CHALF, 128), F32)], axis=0)
        self.own[...] = both.T[0:8]
        for made in self.copies:
            made.start()

    def finish(self):
        total = self.own[...]
        for k in range(YS - 1):
            self.copies[k].wait_recv()
            total = total + self.came[k]
        both = jnp.concatenate([total, jnp.zeros((120, 128), F32)], axis=0).T
        return both[0:CHALF, 0:1], both[0:CHALF, 1:2]


class LatSum:
    def __init__(self, links, place, terms, came_x, part, came_z):
        self.place, self.terms, self.came_x, self.part, self.came_z = (
            place,
            terms,
            came_x,
            part,
            came_z,
        )
        self.over_x = [
            links.copy(terms.at[x, :, core], came_x.at[k], place.at(x, place.z, core))
            for k, (x, core) in enumerate(place.x_peers)
        ]
        self.over_z = [
            links.copy(part.at[z], came_z.at[k], place.at(place.x, z, place.core))
            for k, z in enumerate(place.z_peers)
        ]

    def start(self):
        for made in self.over_x:
            made.start()

    def middle(self):
        for made in self.over_x:
            made.wait_recv()
        total = self.terms[self.place.x, :, self.place.core].astype(F32)
        for k in range(len(self.over_x)):
            total = total + self.came_x[k].astype(F32)
        self.part[...] = total.astype(BF16)
        for made in self.over_z:
            made.start()

    def finish(self):
        for made in self.over_z:
            made.wait_recv()
        total = self.part[self.place.z].astype(F32)
        for k in range(len(self.over_z)):
            total = total + self.came_z[k].astype(F32)
        return total


class FarWeights:
    def __init__(self, group, place, sources, targets):
        links, nx, nz = group.links, place.nx, place.nz
        mine = 2 * place.x + place.core
        (merge, coarse), (far_merge, far_coarse) = sources, targets
        merge_rows, coarse_rows = 4 * D // (2 * nx), 512 // (2 * nx)
        rows, lanes = merge_rows // nz, DC // nz

        def piece(refs, z):
            start = pl.multiple_of(mine * merge_rows + z * rows, rows)
            return [
                refs[0].at[pl.ds(start, rows)],
                refs[1].at[aligned(mine, coarse_rows), aligned(z, lanes)],
            ]

        def plane(x):
            at = 2 * x + place.core
            return [
                far_merge.at[aligned(at, merge_rows)],
                far_coarse.at[aligned(at, coarse_rows)],
            ]

        got = piece(targets, place.z)
        away = nz - 1 - place.z
        self.fetched = [
            links.copy(src, dst, {"tp": group.other, **place.mirror})
            for src, dst in zip(piece(sources, away), piece(targets, away))
        ]
        self.along_z = [
            links.copy(some, some, place.at(place.x, z, place.core))
            for some in got
            for z in place.z_peers
        ]
        self.along_x = [
            links.copy(some, some, place.at(x, place.z, core))
            for some in plane(place.x)
            for x, core in place.x_peers[1::2]
        ]
        self.to_twin = [
            links.copy(plane(x)[which], plane(x)[which], place.at(place.x, place.z, 1 - place.core))
            for which in range(2)
            for x in range(nx)
        ]

    def start(self):
        for made in self.fetched:
            made.start()

    def pass_z(self):
        self.step(self.fetched, self.along_z)

    def half(self, copies, which):
        count = len(copies) // 2
        return copies[which * count : (which + 1) * count]

    def step(self, before, then):
        for which in range(2):
            for made in self.half(before, which):
                made.wait_recv()
            for made in self.half(then, which):
                made.start()

    def pass_x(self):
        self.step(self.along_z, self.along_x)

    def pass_core(self):
        self.step(self.along_x, self.to_twin)

    def finish(self, which):
        for made in self.half(self.to_twin, which):
            made.wait_recv()


class Place:
    def __init__(self, nx, nz):
        lat = lax.axis_index("lat")
        self.nx, self.nz = nx, nz
        self.core = lax.rem(lat, 2)
        self.z = lax.rem(lax.div(lat, 2), nz)
        self.x = lax.div(lat, 2 * nz)
        self.x_peers = [
            (lax.rem(self.x + i, nx), lax.rem(self.core + j, 2))
            for i in range(nx)
            for j in range(2)
            if i or j
        ]
        self.mirror = self.at(self.x, nz - 1 - self.z, self.core)
        self.z_peers = [lax.rem(self.z + k, nz) for k in range(1, nz)]

    def at(self, x, z, core):
        return {"lat": (x * self.nz + z) * 2 + core}


def aligned(index, size):
    return pl.ds(pl.multiple_of(index * size, size), size)


def put(ref, rows, values):
    for j in range(values.shape[1] // 128):
        ref[j, rows, :] = values[:, 128 * j : 128 * j + 128]


def get(ref, rows):
    return jnp.concatenate([ref[j, rows, :] for j in range(ref.shape[0])], axis=1)


def softmax_pair(own, other):
    largest = jnp.maximum(
        jnp.max(own, axis=-1, keepdims=True), jnp.max(other, axis=-1, keepdims=True)
    )
    own, other = jnp.exp(own - largest), jnp.exp(other - largest)
    total = jnp.sum(own, axis=-1, keepdims=True) + jnp.sum(other, axis=-1, keepdims=True)
    return own / total, other / total


def score_grads(prob_own, prob_other, grad_own, grad_other):
    mean = jnp.sum(grad_own * prob_own, axis=-1, keepdims=True)
    mean = mean + jnp.sum(grad_other * prob_other, axis=-1, keepdims=True)
    return (
        (prob_own * (grad_own - mean) * SCALE).astype(BF16),
        (prob_other * (grad_other - mean) * SCALE).astype(BF16),
    )


def low_lanes(values):
    lane = lax.broadcasted_iota(jnp.int32, values.shape, 1)
    return jnp.where(lane < 64, values, 0.0)


def high_lanes(values):
    lane = lax.broadcasted_iota(jnp.int32, values.shape, 1)
    return jnp.where(lane >= 64, values, 0.0)


def fine_mask(start):
    def window(index):
        return ((index >> 5) + 7 + ((index & 7) >> 2)) & 7

    query = lax.broadcasted_iota(jnp.int32, (CTOK, ROW), 0) + start
    key = lax.broadcasted_iota(jnp.int32, (CTOK, ROW), 1)
    return window(query) == window(key)


def main_kernel(
    lat_count,
    nx,
    nz,
    fields,
    classes,
    class_table,
    gain_fine,
    fine_w,
    fine_out,
    gain_merge,
    merge_weight_in,
    gain_coarse,
    coarse_w_in,
    coarse_out_in,
    up_weight_in,
    cotangent_in,
    next_fields,
    fields_grad,
    fine_grad,
    merge_grad,
    send_sems,
    recv_sems,
    local_sems,
    merge_weight,
    own_coarse,
    far_merge,
    far_coarse,
    up_weight,
    cotangent,
    fields_out,
    hid,
    cotf,
    normed,
    queries,
    keys,
    keys_sent,
    keys_came,
    prob_own,
    prob_other,
    mixture,
    heads_all,
    wexp,
    cexp,
    resid,
    merged_norm,
    coarse_all,
    coarse_f,
    lift_all,
    lift_terms,
    lift_y,
    lift_half,
    lift_z,
    ckeys,
    ckeys_came,
    cback,
    cback_came,
    cs_terms,
    cs_y,
    cn_terms,
    cn_y,
    cunit,
    cinverse,
    cm_own,
    cm_y,
    grad_columns,
    far_columns,
    lifted_all,
    mn_terms,
    mn_y,
    up_all,
    up_wide,
    munit,
    minverse,
    mm_own,
    mm_y,
    gh_terms,
    gh_y,
    mix_sent,
    mix_came,
    grad_mix,
    mix_all,
    grad_mix_rows,
    grad_resid,
    grad_q,
    grad_kv,
    grad_other,
    back,
    back_came,
    gn_terms,
    gn_y,
    gn_half,
    gn_z,
    mterms,
    mcame_x,
    mpart,
    mcame_z,
    fterms,
    fcame_x,
    fpart,
    fcame_z,
):
    def fetch(src, dst, at):
        made = pltpu.make_async_copy(src, dst, local_sems.at[at])
        made.start()
        return made

    got_cotangent = fetch(cotangent_in, cotangent, 0)
    got_up = fetch(up_weight_in, up_weight, 1)
    got_merge = fetch(merge_weight_in, merge_weight, 2)
    got_coarse = [
        fetch(coarse_w_in.at[0], own_coarse.at[pl.ds(0, 192)], 3),
        fetch(coarse_w_in.at[1], own_coarse.at[pl.ds(192, 192)], 4),
        fetch(coarse_out_in, own_coarse.at[pl.ds(384, 128)], 5),
    ]

    links = Links(send_sems, recv_sems)
    group = Group(links)
    tp = group.tp
    lat = lax.axis_index("lat")
    before, after = lax.rem(lat + lat_count - 1, lat_count), lax.rem(lat + 1, lat_count)
    twin = lat + 1 - 2 * lax.rem(lat, 2)

    barrier = pltpu.get_barrier_semaphore()
    for k in range(1, TP):
        pl.semaphore_signal(
            barrier, inc=1, device_id={"tp": lax.rem(tp + k, TP)}, device_id_type=MESH
        )
    place = Place(nx, nz)
    lat_peers = [{"lat": before}, {"lat": after}]
    lat_peers += [place.at(x, place.z, core) for x, core in place.x_peers]
    lat_peers += [place.at(place.x, z, place.core) for z in place.z_peers]
    lat_peers.append({"tp": group.other, **place.mirror})
    for peer in lat_peers:
        pl.semaphore_signal(barrier, inc=1, device_id=peer, device_id_type=MESH)

    blank = jnp.zeros((TP, 64, D), BF16)
    wexp[:, 0:64] = blank
    wexp[:, 128:192] = blank
    wexp[tp, 64:128] = fine_out[...]
    for head in range(4):
        cexp[head, 0:64] = jnp.zeros((64, DC), BF16)

    gather_w = OutGather(group, place, wexp)
    lift = Scatter(group, lift_terms, lift_y, lift_half, lift_z)
    send_keys = [
        links.copy(keys_sent.at[1], keys_came.at[0], {"lat": after}),
        links.copy(keys_sent.at[0], keys_came.at[1], {"lat": before}),
    ]
    zh, other = group.zh, group.other
    far_half = 1 - zh

    def head_slot(at, half):
        return heads_all.at[aligned(half, HALF), aligned(at, 128)]

    near_heads = HalfGather(group, head_slot, zh)
    far_heads = HalfGather(group, head_slot, far_half)
    gather_lift = GatherY(group, [lift_all.at[aligned(group.y, CSHARE)]])
    gather_coarse = GatherY(
        group, [coarse_all.at[:, aligned(tp, 128)], coarse_all.at[:, aligned(other, 128)]]
    )
    far = FarWeights(group, place, (merge_weight, own_coarse), (far_merge, far_coarse))
    send_ckeys = links.copy(ckeys, ckeys_came, {"lat": twin})
    send_cback = links.copy(cback, cback_came, {"lat": twin})
    csum = ScatterY(group, cs_terms, cs_y)
    cnorm = ScatterY(group, cn_terms, cn_y)
    cmoments = Moments(group, cm_own, cm_y)
    swap_columns = links.copy(grad_columns.at[far_half], far_columns, {"tp": other})
    gather_lifted = Gather(group, lambda at: lifted_all.at[aligned(at, CSHARE)])
    mnorm = ScatterY(group, mn_terms, mn_y)
    gather_up = Gather(group, lambda at: up_all.at[at])
    mmoments = Moments(group, mm_own, mm_y)
    gheads = [ScatterY(group, gh_terms.at[z], gh_y.at[z]) for z in (far_half, zh)]
    swap_mix = links.copy(mix_sent, mix_came, {"tp": other})
    send_back = [
        links.copy(back.at[0], back_came.at[1], {"lat": before}),
        links.copy(back.at[1], back_came.at[0], {"lat": after}),
    ]
    gnorm = [
        Scatter(group, gn_terms.at[r], gn_y.at[r], gn_half.at[r], gn_z.at[r]) for r in range(2)
    ]
    merge_sum = LatSum(links, place, mterms, mcame_x, mpart, mcame_z)
    fine_sum = LatSum(links, place, fterms, fcame_x, fpart, fcame_z)

    embedded = []
    for r in range(2):
        kinds = lax.broadcasted_iota(jnp.int32, (8, LON), 0)
        onehot = jnp.where(classes[r : r + 1, :] == kinds, 1.0, 0.0).astype(BF16)
        embedded.append(dot_tn(onehot, class_table[...]))
    for r in range(2):
        for level in range(LEV):
            full = fields[r, level].astype(F32) + embedded[r]
            for block in range(TP):
                at = r * ROW + block * SHARE + level * 8
                hid[at : at + 8] = full[8 * block : 8 * block + 8]

    for i in range(4):
        chunk = pl.ds(i * 128, 128)
        unit, _ = standardize(hid[chunk])
        normed[chunk] = (unit * gain_fine[...]).astype(BF16)
    for r in range(2):
        rows = pl.ds(r * ROW, ROW)
        queries[rows] = low_lanes(dot_nt(normed[rows], fine_w[0:128])).astype(BF16)
        kv = dot_nt(normed[rows], fine_w[64:192]).astype(BF16)
        keys[r] = kv
        keys_sent[r] = kv

    pl.semaphore_wait(barrier, TP - 1 + len(lat_peers))
    got_merge.wait()
    for made in got_coarse:
        made.wait()
    far.start()
    for made in send_keys:
        made.start()
    gather_w.start()

    got_cotangent.wait()
    got_up.wait()
    for r in range(2):
        for level in range(LEV):
            cots = cotangent[r, level].astype(F32)
            for block in range(TP):
                at = r * ROW + block * SHARE + level * 8
                put(cotf, pl.ds(at, 8), cots[8 * block : 8 * block + 8])
    kind = lax.div(tp, 2)
    quad = get(cotf, pl.ds(lax.div(kind, 2) * ROW + lax.rem(kind, 2), CTOK, stride=2))
    quad = jnp.where(lax.rem(tp, 2) == 0, quad[:, 0:256], quad[:, 256:512]).astype(BF16)
    lift_terms[...] = dot_nt(quad, up_weight[...]).astype(BF16).reshape(ZH, YS, CSHARE, DC)
    lift.start()
    far.pass_z()

    for made in send_keys:
        made.wait_recv()
    gather_w.share()

    present = (lat > 0, lat < lat_count - 1)

    def attend(r, half):
        start = r * ROW + half * CTOK
        chunk = pl.ds(start, CTOK)
        mask = fine_mask(half * CTOK)
        query = queries[chunk]
        own = jnp.where(mask, dot_nt(query, keys[r]) * SCALE, NEGATIVE)
        far = dot_nt(query, keys_came[r]) * SCALE
        far = jnp.where(jnp.logical_and(mask, present[r]), far, NEGATIVE)
        own, far = softmax_pair(own, far)
        prob_own[chunk] = own
        prob_other[chunk] = far
        mixture[chunk] = dot(own.astype(BF16), keys[r]) + dot(far.astype(BF16), keys_came[r])

    for r in range(2):
        for half in range(2):
            attend(r, half)
    lane = lax.broadcasted_iota(jnp.int32, (ROW, 128), 1)
    packed = jnp.where(lane < 64, pltpu.roll(mixture[ROW : 2 * ROW], 64, 1), mixture[0:ROW])
    heads_all[:, aligned(tp, 128)] = packed.astype(BF16)
    near_heads.start()
    gather_w.forward()
    far.pass_x()

    lift.middle()
    near_heads.forward()
    lift_chunk = lift.finish().astype(BF16)
    lift_all[aligned(group.y, CSHARE)] = lift_chunk
    gather_lift.start()
    far.pass_core()
    near_heads.finish()
    gather_w.finish()

    low = wexp[:, 0:128].reshape(TP * 128, D)
    high = wexp[:, 64:192].reshape(TP * 128, D)

    def merge(half):
        for r, weight in ((0, low), (1, high)):
            rows = pl.ds(pl.multiple_of(r * ROW + half * HALF, HALF), HALF)
            put(resid, rows, hid[rows] + dot(heads_all[aligned(half, HALF)], weight))
        quads = [
            get(resid, pl.ds(r * ROW + half * HALF + s, CHALF, stride=2))
            for r in range(2)
            for s in range(2)
        ]
        unit, inverse = standardize(jnp.concatenate(quads, axis=1))
        merged_norm[aligned(half, CHALF)] = (unit * gain_merge[...]).astype(BF16)
        return unit, inverse

    unit, inverse = merge(zh)
    near_merged = merged_norm[aligned(zh, CHALF)]
    coarse_all[:, aligned(tp, 128)] = dot(near_merged, merge_weight[...]).astype(BF16)
    far.finish(0)
    coarse_all[:, aligned(other, 128)] = dot(near_merged, far_merge[...]).astype(BF16)
    gather_coarse.start()
    far_heads.start()
    munit[...] = unit
    minverse[...] = jnp.broadcast_to(inverse, (CHALF, 128))
    far.finish(1)
    gather_lift.finish()
    stacks = [(own_coarse, 0), (own_coarse, 1), (far_coarse, 0), (far_coarse, 1)]
    for head, (stack, at) in enumerate(stacks):
        cexp[head, 64:128] = stack[384 + 64 * at : 448 + 64 * at]
    grad_cmix = [dot_nt(lift_all[...], cexp[head]).astype(BF16) for head in range(4)]
    gather_coarse.finish()

    coarse_f[...] = coarse_all[...].astype(F32)
    unit, inverse = standardize(coarse_f[...])
    cnormed = (unit * gain_coarse[...]).astype(BF16)
    for head, (stack, at) in enumerate(stacks):
        rows = stack[192 * at + 64 : 192 * at + 192]
        ckeys[head] = dot_nt(cnormed, rows).astype(BF16)
    send_ckeys.start()
    cunit[...] = unit
    cinverse[...] = jnp.broadcast_to(inverse, (CHALF, 128))
    cq = [
        low_lanes(dot_nt(cnormed, stack[192 * at : 192 * at + 128])).astype(BF16)
        for stack, at in stacks
    ]

    row_at = lax.broadcasted_iota(jnp.int32, (CHALF, CHALF), 0)
    col_at = lax.broadcasted_iota(jnp.int32, (CHALF, CHALF), 1)
    cmask = (row_at >> 5) == (col_at >> 5)
    own_scores = [
        jnp.where(cmask, dot_nt(cq[head], ckeys[head]) * SCALE, NEGATIVE) for head in range(4)
    ]
    send_ckeys.wait_recv()
    cgrad_q, cgrad_kv = [], []
    cheads = []
    for head in range(4):
        away = jnp.where(cmask, dot_nt(cq[head], ckeys_came[head]) * SCALE, NEGATIVE)
        own, away = softmax_pair(own_scores[head], away)
        own16, far16 = own.astype(BF16), away.astype(BF16)
        grad_own = dot_nt(grad_cmix[head], ckeys[head])
        grad_far = dot_nt(grad_cmix[head], ckeys_came[head])
        ds_own, ds_far = score_grads(own, away, grad_own, grad_far)
        cback[head] = (dot_tn(ds_far, cq[head]) + dot_tn(far16, grad_cmix[head])).astype(BF16)
        cgrad_kv.append(dot_tn(ds_own, cq[head]) + dot_tn(own16, grad_cmix[head]))
        query_grad = dot(ds_own, ckeys[head]) + dot(ds_far, ckeys_came[head])
        cgrad_q.append(low_lanes(query_grad).astype(BF16))
        cheads.append((dot(own16, ckeys[head]) + dot(far16, ckeys_came[head])).astype(BF16))
    send_cback.start()
    part = sum(dot(cheads[head], cexp[head]) for head in range(4))
    cs_terms[...] = part.astype(BF16).reshape(YS, CSHARE, DC)
    part = 0.0
    for head, (stack, at) in enumerate(stacks):
        part = part + dot(cgrad_q[head], stack[192 * at : 192 * at + 128])
    send_cback.wait_recv()
    for head, (stack, at) in enumerate(stacks):
        total = (cgrad_kv[head] + cback_came[head].astype(F32)).astype(BF16)
        part = part + dot(total, stack[192 * at + 64 : 192 * at + 192])
    for t in range(TP):
        cn_terms[t % YS, t // YS] = part[:, 128 * t : 128 * t + 128].astype(BF16)
    cnorm.start()
    cmoments.start(part * gain_coarse[...], cunit[...])
    csum.start()
    far_heads.forward()

    def one_head(at, top, bottom):
        top, bottom = top.astype(BF16), bottom.astype(BF16)
        return dot_nt(top, wexp[at, 0:128]) + dot_nt(bottom, wexp[at, 64:192])

    ones = jnp.ones((8, D), BF16)
    head_terms = []
    for at in (other, tp):
        terms = []
        for s in range(2):
            cot = [get(cotf, pl.ds(r * ROW + zh * HALF + s, CHALF, stride=2)) for r in range(2)]
            unit = [munit[:, (2 * r + s) * D : (2 * r + s + 1) * D] for r in range(2)]
            terms.append((one_head(at, *cot), one_head(at, *unit)))
        head_terms.append((terms, one_head(at, ones, ones)[0:1]))

    grad_cn = cnorm.finish()
    first, second = cmoments.finish()
    for zc in range(ZH):
        lane_block = aligned(zc * YS + group.y, 128)
        inner = grad_cn[zc] * gain_coarse[:, lane_block]
        inner = cinverse[...] * (inner - first - cunit[:, lane_block] * second)
        grad_columns[zc] = (lift_all[:, lane_block].astype(F32) + inner).astype(BF16)

    part = dot_nt(grad_columns[zh], merge_weight[...])
    part = part + dot_nt(grad_columns[far_half], far_merge[...])
    inner = part * gain_merge[...]
    inner16 = inner.astype(BF16)
    for s in range(2):
        top, bottom = [inner16[:, (2 * r + s) * D : (2 * r + s + 1) * D] for r in range(2)]
        heads = (dot_nt(top, low) + dot_nt(bottom, high)).astype(BF16)
        for t in range(TP):
            some = heads[:, 128 * t : 128 * t + 128]
            gh_terms[t // YS, t % YS, s * CHALF : (s + 1) * CHALF] = some
    for part_sum in gheads:
        part_sum.start()
    mmoments.start(inner, munit[...])
    swap_columns.start()
    mn_terms[...] = part.astype(BF16).reshape(YS, CSHARE, 4 * D)
    mnorm.start()

    mine = aligned(tp, CSHARE)
    near_mine = aligned(group.y, CSHARE)
    lifted_all[mine] = (coarse_f[near_mine] + csum.finish()).astype(BF16)
    gather_lifted.start()

    first, second = mmoments.finish()
    for i, (terms, head_ones) in enumerate(head_terms):
        grad_heads = gheads[i].finish()
        for s in range(2):
            head_cot, head_unit = terms[s]
            inner = grad_heads[s * CHALF : (s + 1) * CHALF] - first * head_ones - second * head_unit
            put(grad_mix, pl.ds(s, CHALF, stride=2), head_cot + minverse[...] * inner)
        if i == 0:
            mix_sent[...] = grad_mix[0].astype(BF16)
            swap_mix.start()
    mix_all[aligned(zh, HALF)] = grad_mix[0]
    gather_lifted.forward()

    far_heads.finish()
    merge(far_half)
    swap_columns.wait_recv()
    scale = (2 * lat_count * LEV * LON) ** -0.5
    merge_rows = 4 * D // lat_count
    weight_rows = D // lat_count
    term = dot_tn(merged_norm[aligned(zh, CHALF)], grad_columns[zh])
    term = term + dot_tn(merged_norm[aligned(far_half, CHALF)], far_columns[...])
    mterms[...] = (term * scale).astype(BF16).reshape(nx, nz, 2, merge_rows, 128)
    gather_lifted.finish()
    up_all[tp] = dot(lifted_all[...], up_weight[...]).astype(BF16)
    swap_mix.wait_recv()
    mix_all[aligned(far_half, HALF)] = mix_came[...].astype(F32)
    gather_up.start()
    merge_sum.start()
    both = mix_all[...]
    grad_mix_rows[0:ROW] = high_lanes(both).astype(BF16)
    grad_mix_rows[ROW : 2 * ROW] = high_lanes(pltpu.roll(both, 64, 1)).astype(BF16)

    def attend_back(r, half):
        chunk = pl.ds(r * ROW + half * CTOK, CTOK)
        query, grad_out = queries[chunk], grad_mix_rows[chunk]
        own, far = prob_own[chunk], prob_other[chunk]
        ds_own, ds_far = score_grads(
            own, far, dot_nt(grad_out, keys[r]), dot_nt(grad_out, keys_came[r])
        )
        own16, far16 = own.astype(BF16), far.astype(BF16)
        to_own = dot_tn(ds_own, query) + dot_tn(own16, grad_out)
        to_far = dot_tn(ds_far, query) + dot_tn(far16, grad_out)
        grad_q[chunk] = low_lanes(dot(ds_own, keys[r]) + dot(ds_far, keys_came[r])).astype(BF16)
        return to_own, to_far

    for r in range(2):
        own_a, far_a = attend_back(r, 0)
        own_b, far_b = attend_back(r, 1)
        back[r] = (far_a + far_b).astype(BF16)
        send_back[r].start()
        grad_other[r] = own_a + own_b
    merge_sum.middle()
    for made in send_back:
        made.wait_recv()
    for r in range(2):
        grad_kv[pl.ds(r * ROW, ROW)] = (grad_other[r] + back_came[r].astype(F32)).astype(BF16)
    for r in range(2):
        rows = pl.ds(r * ROW, ROW)
        part = dot(grad_q[rows], fine_w[0:128]) + dot(grad_kv[rows], fine_w[64:192])
        gn_terms[r] = part.astype(BF16).reshape(ZH, YS, SHARE, D)
        gnorm[r].start()

    term_q = dot_tn(normed[...], grad_q[...]) * scale
    term_kv = dot_tn(normed[...], grad_kv[...]) * scale
    term = jnp.concatenate(
        [term_q.reshape(lat_count, weight_rows, 128), term_kv.reshape(lat_count, weight_rows, 128)],
        axis=1,
    )
    fterms[...] = term.astype(BF16).reshape(nx, nz, 2, 2 * weight_rows, 128)
    fine_sum.start()
    gather_up.forward()
    for part in gnorm:
        part.middle()
    fine_sum.middle()

    grad_mn = mnorm.finish()
    merged_chunk, cot_chunk = [], []
    for r in range(2):
        for s in range(2):
            some = pl.ds(r * ROW + s + tp * SHARE, CSHARE, stride=2)
            merged_chunk.append(get(resid, some))
            cot_chunk.append(get(cotf, some))
    merged_chunk = jnp.concatenate(merged_chunk, axis=1)
    cot_chunk = jnp.concatenate(cot_chunk, axis=1)
    grad_quads = cot_chunk + normalize_back(merged_chunk, gain_merge[...], grad_mn)
    for r in range(2):
        for s in range(2):
            some = grad_quads[:, (2 * r + s) * D : (2 * r + s + 1) * D]
            put(grad_resid, pl.ds(r * SHARE + s, CSHARE, stride=2), some)

    gather_up.finish()
    for r in range(2):
        for s in range(2):
            for part in range(2):
                wide = up_all[4 * r + 2 * s + part].astype(F32)
                some = pl.ds(r * ROW + s, CTOK, stride=2)
                up_wide[2 * part, some, :] = wide[:, 0:128]
                up_wide[2 * part + 1, some, :] = wide[:, 128:256]
    for r in range(2):
        for level in range(LEV):
            pieces = []
            for block in range(TP):
                at = r * ROW + block * SHARE + level * 8
                pieces.append(get(resid, pl.ds(at, 8)) + get(up_wide, pl.ds(at, 8)))
            fields_out[r, level] = jnp.concatenate(pieces, axis=0).astype(BF16)
    written = fetch(fields_out, next_fields, 6)

    for r in range(2):
        grad_norm = gnorm[r].finish()
        own_hidden = hid[pl.ds(pl.multiple_of(r * ROW + tp * SHARE, SHARE), SHARE)]
        grad_hidden = normalize_back(own_hidden, gain_fine[...], grad_norm)
        grad_hidden = grad_hidden + get(grad_resid, pl.ds(r * SHARE, SHARE))
        fields_grad[r] = grad_hidden.astype(BF16)
    merge_grad[...] = merge_sum.finish()
    sums = fine_sum.finish()
    fine_grad[:, 0, 0:64] = sums[0:weight_rows, 0:64]
    fine_grad[:, 0, 64:192] = sums[weight_rows : 2 * weight_rows]
    written.wait()
    links.finish()


def hand_over(*refs):
    for i in range(4):
        refs[4 + i][...] = refs[i][...]


def vmem(*shape, kind=BF16):
    return pltpu.VMEM(shape, kind)


def scatter_buffers(*chunk):
    return [vmem(ZH, YS, *chunk), vmem(YS - 1, ZH, *chunk), vmem(*chunk), vmem(*chunk)]


def halved(*buffers):
    return [vmem(2, *some.shape) for some in buffers]


def y_buffers(*chunk):
    return [vmem(YS, *chunk), vmem(YS - 1, *chunk)]


def moment_buffers():
    return [vmem(8, 128, kind=F32), vmem(YS - 1, 8, 128, kind=F32)]


def lat_buffers(nx, nz, rows):
    return [
        vmem(nx, nz, 2, rows, 128),
        vmem(2 * nx - 1, nz, rows, 128),
        vmem(nz, rows, 128),
        vmem(nz - 1, rows, 128),
    ]


def local(
    lat_count,
    fields,
    classes,
    class_table,
    gain_fine,
    fine_qkv,
    fine_out,
    gain_merge,
    merge_weight,
    gain_coarse,
    coarse_qkv,
    coarse_out,
    up_weight,
    cotangent,
):
    merge_rows, weight_rows = 4 * D // lat_count, D // lat_count
    nz = min(8, lat_count // 4)
    nx = lat_count // (2 * nz)
    whole = pl.BlockSpec(memory_space=pltpu.VMEM)
    left = pl.BlockSpec(memory_space=pl.ANY)
    copies = 240
    scratch = [
        pltpu.SemaphoreType.DMA((copies,)),
        pltpu.SemaphoreType.DMA((copies,)),
        pltpu.SemaphoreType.DMA((7,)),
        vmem(4 * D, 128),
        vmem(512, DC),
        vmem(4 * D, 128),
        vmem(512, DC),
        vmem(DC, 256),
        vmem(2, LEV, LON, D),
        vmem(2, LEV, LON, D),
        vmem(2 * ROW, D, kind=F32),
        vmem(4, 2 * ROW, 128, kind=F32),
        vmem(2 * ROW, D),
        vmem(2 * ROW, 128),
        vmem(2, ROW, 128),
        vmem(2, ROW, 128),
        vmem(2, ROW, 128),
        vmem(2 * ROW, ROW, kind=F32),
        vmem(2 * ROW, ROW, kind=F32),
        vmem(2 * ROW, 128, kind=F32),
        vmem(ROW, TP * 128),
        vmem(TP, 192, D),
        vmem(4, 128, DC),
        vmem(4, 2 * ROW, 128, kind=F32),
        vmem(CTOK, 4 * D),
        vmem(CHALF, DC),
        vmem(CHALF, DC, kind=F32),
        vmem(CHALF, DC),
        *scatter_buffers(CSHARE, DC),
        vmem(4, CHALF, 128),
        vmem(4, CHALF, 128),
        vmem(4, CHALF, 128),
        vmem(4, CHALF, 128),
        *y_buffers(CSHARE, DC),
        *y_buffers(ZH, CHALF, 128),
        vmem(CHALF, DC, kind=F32),
        vmem(CHALF, 128, kind=F32),
        *moment_buffers(),
        vmem(ZH, CHALF, 128),
        vmem(CHALF, 128),
        vmem(CTOK, DC),
        *y_buffers(CSHARE, 4 * D),
        vmem(TP, CTOK, 256),
        vmem(4, 2 * ROW, 128, kind=F32),
        vmem(CHALF, 4 * D, kind=F32),
        vmem(CHALF, 128, kind=F32),
        *moment_buffers(),
        *halved(*y_buffers(2 * CHALF, 128)),
        vmem(HALF, 128),
        vmem(HALF, 128),
        vmem(1, HALF, 128, kind=F32),
        vmem(ROW, 128, kind=F32),
        vmem(2 * ROW, 128),
        vmem(4, 2 * SHARE, 128, kind=F32),
        vmem(2 * ROW, 128),
        vmem(2 * ROW, 128),
        vmem(2, ROW, 128, kind=F32),
        vmem(2, ROW, 128),
        vmem(2, ROW, 128),
        *halved(*scatter_buffers(SHARE, D)),
        *lat_buffers(nx, nz, merge_rows),
        *lat_buffers(nx, nz, 2 * weight_rows),
    ]
    results = pl.pallas_call(
        functools.partial(main_kernel, lat_count, nx, nz),
        out_shape=(
            jax.ShapeDtypeStruct((2, LEV, LON, D), BF16),
            jax.ShapeDtypeStruct((2, SHARE, D), BF16),
            jax.ShapeDtypeStruct((weight_rows, 1, 192), F32),
            jax.ShapeDtypeStruct((merge_rows, 128), F32),
        ),
        in_specs=[whole] * 7 + [left, whole] + [left] * 4,
        out_specs=[left] + [whole] * 3,
        scratch_shapes=scratch,
        name="block",
        compiler_params=pltpu.CompilerParams(
            collective_id=0, has_side_effects=True, vmem_limit_bytes=56 * 2**20
        ),
    )(
        fields,
        classes,
        class_table,
        gain_fine.reshape(1, -1),
        fine_qkv.reshape(D, 192).T,
        fine_out.reshape(64, D),
        gain_merge.reshape(1, -1),
        merge_weight,
        gain_coarse.reshape(1, -1),
        coarse_qkv.transpose(1, 2, 0),
        coarse_out.reshape(128, DC),
        up_weight,
        cotangent,
    )
    next_fields, fields_grad, fine_grad, merge_grad = pl.pallas_call(
        hand_over,
        out_shape=tuple(jax.ShapeDtypeStruct(some.shape, some.dtype) for some in results),
        in_specs=[whole] * 4,
        out_specs=[whole] * 4,
        name="hand_over",
    )(*results)
    return next_fields, fields_grad.reshape(2, LEV, LON // TP, D), fine_grad, merge_grad


def solution(mesh):
    placed = (
        P("lat", None, None, None),
        P("lat", None),
        P(),
        P(),
        P(None, "tp", None),
        P("tp", None, None),
        P(),
        P(None, "tp"),
        P(),
        P(None, "tp", None),
        P("tp", None, None),
        P(None, "tp"),
        P("lat", None, None, None),
    )
    return jax.shard_map(
        functools.partial(local, mesh.shape["lat"]),
        mesh=mesh,
        in_specs=placed,
        out_specs=(
            P("lat", None, None, None),
            P("lat", None, "tp", None),
            P("lat", "tp", None),
            P("lat", "tp"),
        ),
        check_vma=False,
    )
```

```python
import functools

import jax
import jax.numpy as jnp
from jax import lax
from jax.experimental import pallas as pl
from jax.experimental.pallas import tpu as pltpu
from jax.sharding import PartitionSpec as P

MESH = pl.DeviceIdType.MESH
F32 = jnp.float32
BF16 = jnp.bfloat16
EPSILON = 1e-05
NEGATIVE = -1e30

D = 512
DC = 1024
LEV = 4
LON = 64
ZH = 2
YS = 4
TP = ZH * YS
ROW = LEV * LON
CTOK = ROW // 2
SHARE = ROW // TP
CSHARE = CTOK // TP
HALF = ROW // ZH
CHALF = CTOK // ZH
SCALE = 0.125


def dot(a, b):
    return lax.dot_general(a, b, (((1,), (0,)), ((), ())), preferred_element_type=F32)


def dot_nt(a, b):
    return lax.dot_general(a, b, (((1,), (1,)), ((), ())), preferred_element_type=F32)


def dot_tn(a, b):
    return lax.dot_general(a, b, (((0,), (0,)), ((), ())), preferred_element_type=F32)


def standardize(values):
    centred = values - jnp.mean(values, axis=-1, keepdims=True)
    spread = jnp.mean(centred * centred, axis=-1, keepdims=True)
    inverse = lax.rsqrt(spread + EPSILON)
    return centred * inverse, inverse


def normalize_back(values, gain, incoming):
    unit, inverse = standardize(values)
    inner = incoming * gain
    first = jnp.mean(inner, axis=-1, keepdims=True)
    second = jnp.mean(inner * unit, axis=-1, keepdims=True)
    return inverse * (inner - first - unit * second)


class Links:
    def __init__(self, send_sems, recv_sems):
        self.send_sems, self.recv_sems = send_sems, recv_sems
        self.copies = []

    def copy(self, src, dst, device):
        at = len(self.copies)
        made = pltpu.make_async_remote_copy(
            src_ref=src,
            dst_ref=dst,
            send_sem=self.send_sems.at[at],
            recv_sem=self.recv_sems.at[at],
            device_id=device,
            device_id_type=MESH,
        )
        self.copies.append(made)
        return made

    def finish(self):
        for made in self.copies:
            made.wait_send()


class Group:
    def __init__(self, links):
        self.links = links
        self.tp = lax.axis_index("tp")
        self.zh, self.y = lax.div(self.tp, YS), lax.rem(self.tp, YS)
        self.other = lax.rem(self.tp + YS, TP)

    def y_at(self, k):
        return lax.rem(self.y + k, YS)

    def along_y(self, k):
        return {"tp": self.zh * YS + self.y_at(k)}


class Gather:
    def __init__(self, group, view):
        links = group.links
        own, far = view(group.tp), view(group.other)
        self.over_z = links.copy(own, own, {"tp": group.other})
        self.over_y = [links.copy(own, own, group.along_y(k)) for k in range(1, YS)]
        self.passed = [links.copy(far, far, group.along_y(k)) for k in range(1, YS)]

    def start(self):
        for made in [self.over_z] + self.over_y:
            made.start()

    def forward(self):
        self.over_z.wait_recv()
        for made in self.passed:
            made.start()

    def finish(self):
        for made in self.over_y + self.passed:
            made.wait_recv()


class HalfGather:
    def __init__(self, group, view, near):
        links, far = group.links, 1 - near
        sent, own, passed = view(group.tp, far), view(group.tp, near), view(group.other, near)
        self.over_z = links.copy(sent, sent, {"tp": group.other})
        self.over_y = [links.copy(own, own, group.along_y(k)) for k in range(1, YS)]
        self.passed = [links.copy(passed, passed, group.along_y(k)) for k in range(1, YS)]

    start, forward, finish = Gather.start, Gather.forward, Gather.finish


class OutGather:
    def __init__(self, group, place, wexp):
        links, rows = group.links, 64 // place.nx

        def piece(at, x, core):
            return wexp.at[at, pl.ds(64 + x * rows, rows), aligned(core, 256)]

        def slot(at):
            return wexp.at[at, pl.ds(64, 64)]

        own, far = slot(group.tp), slot(group.other)
        sent = piece(group.tp, place.x, place.core)
        got = piece(group.other, place.x, place.core)
        self.over_z = links.copy(sent, sent, {"tp": group.other, **place.mirror})
        self.over_y = [links.copy(own, own, group.along_y(k)) for k in range(1, YS)]
        self.shared = [links.copy(got, got, place.at(x, place.z, c)) for x, c in place.x_peers]
        self.passed = [links.copy(far, far, group.along_y(k)) for k in range(1, YS)]

    def share(self):
        self.over_z.wait_recv()
        for made in self.shared:
            made.start()

    def forward(self):
        for made in self.shared:
            made.wait_recv()
        for made in self.passed:
            made.start()

    start, finish = Gather.start, Gather.finish


class GatherY:
    def __init__(self, group, refs):
        self.copies = [
            group.links.copy(some, some, group.along_y(k)) for k in range(1, YS) for some in refs
        ]

    def start(self):
        for made in self.copies:
            made.start()

    def finish(self):
        for made in self.copies:
            made.wait_recv()


class ScatterY:
    def __init__(self, group, terms, came):
        self.group, self.terms, self.came = group, terms, came
        self.copies = [
            group.links.copy(terms.at[group.y_at(k)], came.at[k - 1], group.along_y(k))
            for k in range(1, YS)
        ]

    start, wait = GatherY.start, GatherY.finish

    def finish(self):
        self.wait()
        total = self.terms[self.group.y].astype(F32)
        for k in range(YS - 1):
            total = total + self.came[k].astype(F32)
        return total


class Scatter:
    def __init__(self, group, terms, came_y, half, came_z):
        self.group, self.terms = group, terms
        self.came_y, self.half, self.came_z = came_y, half, came_z
        links = group.links
        self.over_y = [
            links.copy(terms.at[:, group.y_at(k)], came_y.at[k - 1], group.along_y(k))
            for k in range(1, YS)
        ]
        self.over_z = links.copy(half, came_z, {"tp": group.other})

    def start(self):
        for made in self.over_y:
            made.start()

    def summed(self, zh):
        total = self.terms[zh, self.group.y].astype(F32)
        for k in range(YS - 1):
            total = total + self.came_y[k, zh].astype(F32)
        return total

    def middle(self):
        for made in self.over_y:
            made.wait_recv()
        self.half[...] = self.summed(1 - self.group.zh).astype(BF16)
        self.over_z.start()

    def finish(self):
        own = self.summed(self.group.zh)
        self.over_z.wait_recv()
        return own + self.came_z[...].astype(F32)


class Moments:
    def __init__(self, group, own, came):
        self.own, self.came = own, came
        self.copies = [
            group.links.copy(own, came.at[k - 1], group.along_y(k)) for k in range(1, YS)
        ]

    def start(self, inner, unit):
        first = jnp.mean(inner, axis=-1, keepdims=True)
        second = jnp.mean(inner * unit, axis=-1, keepdims=True)
        lane = lax.broadcasted_iota(jnp.int32, (CHALF, 128), 1)
        both = jnp.where(lane == 0, first, jnp.where(lane == 1, second, 0.0))
        both = jnp.concatenate([both, jnp.zeros((128 - CHALF, 128), F32)], axis=0)
        self.own[...] = both.T[0:8]
        for made in self.copies:
            made.start()

    def finish(self):
        total = self.own[...]
        for k in range(YS - 1):
            self.copies[k].wait_recv()
            total = total + self.came[k]
        both = jnp.concatenate([total, jnp.zeros((120, 128), F32)], axis=0).T
        return both[0:CHALF, 0:1], both[0:CHALF, 1:2]


class LatSum:
    def __init__(self, links, place, terms, came_x, part, came_z):
        self.place, self.terms, self.came_x, self.part, self.came_z = (
            place,
            terms,
            came_x,
            part,
            came_z,
        )
        self.over_x = [
            links.copy(terms.at[x, :, core], came_x.at[k], place.at(x, place.z, core))
            for k, (x, core) in enumerate(place.x_peers)
        ]
        self.over_z = [
            links.copy(part.at[z], came_z.at[k], place.at(place.x, z, place.core))
            for k, z in enumerate(place.z_peers)
        ]

    def start(self):
        for made in self.over_x:
            made.start()

    def middle(self):
        for made in self.over_x:
            made.wait_recv()
        total = self.terms[self.place.x, :, self.place.core].astype(F32)
        for k in range(len(self.over_x)):
            total = total + self.came_x[k].astype(F32)
        self.part[...] = total.astype(BF16)
        for made in self.over_z:
            made.start()

    def finish(self):
        for made in self.over_z:
            made.wait_recv()
        total = self.part[self.place.z].astype(F32)
        for k in range(len(self.over_z)):
            total = total + self.came_z[k].astype(F32)
        return total


class FarWeights:
    def __init__(self, group, place, sources, targets):
        links, nx, nz = group.links, place.nx, place.nz
        mine = 2 * place.x + place.core
        (merge, coarse), (far_merge, far_coarse) = sources, targets
        merge_rows, coarse_rows = 4 * D // (2 * nx), 512 // (2 * nx)
        rows, lanes = merge_rows // nz, DC // nz

        def piece(refs, z):
            start = pl.multiple_of(mine * merge_rows + z * rows, rows)
            return [
                refs[0].at[pl.ds(start, rows)],
                refs[1].at[aligned(mine, coarse_rows), aligned(z, lanes)],
            ]

        def plane(x):
            at = 2 * x + place.core
            return [
                far_merge.at[aligned(at, merge_rows)],
                far_coarse.at[aligned(at, coarse_rows)],
            ]

        got = piece(targets, place.z)
        away = nz - 1 - place.z
        self.fetched = [
            links.copy(src, dst, {"tp": group.other, **place.mirror})
            for src, dst in zip(piece(sources, away), piece(targets, away))
        ]
        self.along_z = [
            links.copy(some, some, place.at(place.x, z, place.core))
            for some in got
            for z in place.z_peers
        ]
        self.along_x = [
            links.copy(some, some, place.at(x, place.z, core))
            for some in plane(place.x)
            for x, core in place.x_peers[1::2]
        ]
        self.to_twin = [
            links.copy(plane(x)[which], plane(x)[which], place.at(place.x, place.z, 1 - place.core))
            for which in range(2)
            for x in range(nx)
        ]

    def start(self):
        for made in self.fetched:
            made.start()

    def pass_z(self):
        self.step(self.fetched, self.along_z)

    def half(self, copies, which):
        count = len(copies) // 2
        return copies[which * count : (which + 1) * count]

    def step(self, before, then):
        for which in range(2):
            for made in self.half(before, which):
                made.wait_recv()
            for made in self.half(then, which):
                made.start()

    def pass_x(self):
        self.step(self.along_z, self.along_x)

    def pass_core(self):
        self.step(self.along_x, self.to_twin)

    def finish(self, which):
        for made in self.half(self.to_twin, which):
            made.wait_recv()


class Place:
    def __init__(self, nx, nz):
        lat = lax.axis_index("lat")
        self.nx, self.nz = nx, nz
        self.core = lax.rem(lat, 2)
        self.z = lax.rem(lax.div(lat, 2), nz)
        self.x = lax.div(lat, 2 * nz)
        self.x_peers = [
            (lax.rem(self.x + i, nx), lax.rem(self.core + j, 2))
            for i in range(nx)
            for j in range(2)
            if i or j
        ]
        self.mirror = self.at(self.x, nz - 1 - self.z, self.core)
        self.z_peers = [lax.rem(self.z + k, nz) for k in range(1, nz)]

    def at(self, x, z, core):
        return {"lat": (x * self.nz + z) * 2 + core}


def aligned(index, size):
    return pl.ds(pl.multiple_of(index * size, size), size)


def put(ref, rows, values):
    for j in range(values.shape[1] // 128):
        ref[j, rows, :] = values[:, 128 * j : 128 * j + 128]


def get(ref, rows):
    return jnp.concatenate([ref[j, rows, :] for j in range(ref.shape[0])], axis=1)


def softmax_pair(own, other):
    largest = jnp.maximum(
        jnp.max(own, axis=-1, keepdims=True), jnp.max(other, axis=-1, keepdims=True)
    )
    own, other = jnp.exp(own - largest), jnp.exp(other - largest)
    total = jnp.sum(own, axis=-1, keepdims=True) + jnp.sum(other, axis=-1, keepdims=True)
    return own / total, other / total


def score_grads(prob_own, prob_other, grad_own, grad_other):
    mean = jnp.sum(grad_own * prob_own, axis=-1, keepdims=True)
    mean = mean + jnp.sum(grad_other * prob_other, axis=-1, keepdims=True)
    return (
        (prob_own * (grad_own - mean) * SCALE).astype(BF16),
        (prob_other * (grad_other - mean) * SCALE).astype(BF16),
    )


def low_lanes(values):
    lane = lax.broadcasted_iota(jnp.int32, values.shape, 1)
    return jnp.where(lane < 64, values, 0.0)


def high_lanes(values):
    lane = lax.broadcasted_iota(jnp.int32, values.shape, 1)
    return jnp.where(lane >= 64, values, 0.0)


def fine_mask(start):
    def window(index):
        return ((index >> 5) + 7 + ((index & 7) >> 2)) & 7

    query = lax.broadcasted_iota(jnp.int32, (CTOK, ROW), 0) + start
    key = lax.broadcasted_iota(jnp.int32, (CTOK, ROW), 1)
    return window(query) == window(key)


def main_kernel(
    lat_count,
    nx,
    nz,
    fields,
    classes,
    class_table,
    gain_fine,
    fine_w,
    fine_out,
    gain_merge,
    merge_weight_in,
    gain_coarse,
    coarse_w_in,
    coarse_out_in,
    up_weight_in,
    cotangent_in,
    next_fields,
    fields_grad,
    fine_grad,
    merge_grad,
    send_sems,
    recv_sems,
    local_sems,
    merge_weight,
    own_coarse,
    far_merge,
    far_coarse,
    up_weight,
    cotangent,
    fields_out,
    hid,
    cotf,
    normed,
    queries,
    keys,
    keys_sent,
    keys_came,
    prob_own,
    prob_other,
    mixture,
    heads_all,
    wexp,
    cexp,
    resid,
    merged_norm,
    coarse_all,
    coarse_f,
    lift_all,
    lift_terms,
    lift_y,
    lift_half,
    lift_z,
    ckeys,
    ckeys_came,
    cback,
    cback_came,
    cs_terms,
    cs_y,
    cn_terms,
    cn_y,
    cunit,
    cinverse,
    cm_own,
    cm_y,
    grad_columns,
    far_columns,
    lifted_all,
    mn_terms,
    mn_y,
    up_all,
    up_wide,
    munit,
    minverse,
    mm_own,
    mm_y,
    gh_terms,
    gh_y,
    mix_sent,
    mix_came,
    grad_mix,
    mix_all,
    grad_mix_rows,
    grad_resid,
    grad_q,
    grad_kv,
    grad_other,
    back,
    back_came,
    gn_terms,
    gn_y,
    gn_half,
    gn_z,
    mterms,
    mcame_x,
    mpart,
    mcame_z,
    fterms,
    fcame_x,
    fpart,
    fcame_z,
):
    def fetch(src, dst, at):
        made = pltpu.make_async_copy(src, dst, local_sems.at[at])
        made.start()
        return made

    got_cotangent = fetch(cotangent_in, cotangent, 0)
    got_up = fetch(up_weight_in, up_weight, 1)
    got_merge = fetch(merge_weight_in, merge_weight, 2)
    got_coarse = [
        fetch(coarse_w_in.at[0], own_coarse.at[pl.ds(0, 192)], 3),
        fetch(coarse_w_in.at[1], own_coarse.at[pl.ds(192, 192)], 4),
        fetch(coarse_out_in, own_coarse.at[pl.ds(384, 128)], 5),
    ]

    links = Links(send_sems, recv_sems)
    group = Group(links)
    tp = group.tp
    lat = lax.axis_index("lat")
    before, after = lax.rem(lat + lat_count - 1, lat_count), lax.rem(lat + 1, lat_count)
    twin = lat + 1 - 2 * lax.rem(lat, 2)

    barrier = pltpu.get_barrier_semaphore()
    for k in range(1, TP):
        pl.semaphore_signal(
            barrier, inc=1, device_id={"tp": lax.rem(tp + k, TP)}, device_id_type=MESH
        )
    place = Place(nx, nz)
    lat_peers = [{"lat": before}, {"lat": after}]
    lat_peers += [place.at(x, place.z, core) for x, core in place.x_peers]
    lat_peers += [place.at(place.x, z, place.core) for z in place.z_peers]
    lat_peers.append({"tp": group.other, **place.mirror})
    for peer in lat_peers:
        pl.semaphore_signal(barrier, inc=1, device_id=peer, device_id_type=MESH)

    blank = jnp.zeros((TP, 64, D), BF16)
    wexp[:, 0:64] = blank
    wexp[:, 128:192] = blank
    wexp[tp, 64:128] = fine_out[...]
    for head in range(4):
        cexp[head, 0:64] = jnp.zeros((64, DC), BF16)

    gather_w = OutGather(group, place, wexp)
    lift = Scatter(group, lift_terms, lift_y, lift_half, lift_z)
    send_keys = [
        links.copy(keys_sent.at[1], keys_came.at[0], {"lat": after}),
        links.copy(keys_sent.at[0], keys_came.at[1], {"lat": before}),
    ]
    zh, other = group.zh, group.other
    far_half = 1 - zh

    def head_slot(at, half):
        return heads_all.at[aligned(half, HALF), aligned(at, 128)]

    near_heads = HalfGather(group, head_slot, zh)
    far_heads = HalfGather(group, head_slot, far_half)
    gather_lift = GatherY(group, [lift_all.at[aligned(group.y, CSHARE)]])
    gather_coarse = GatherY(
        group, [coarse_all.at[:, aligned(tp, 128)], coarse_all.at[:, aligned(other, 128)]]
    )
    far = FarWeights(group, place, (merge_weight, own_coarse), (far_merge, far_coarse))
    send_ckeys = links.copy(ckeys, ckeys_came, {"lat": twin})
    send_cback = links.copy(cback, cback_came, {"lat": twin})
    csum = ScatterY(group, cs_terms, cs_y)
    cnorm = ScatterY(group, cn_terms, cn_y)
    cmoments = Moments(group, cm_own, cm_y)
    swap_columns = links.copy(grad_columns.at[far_half], far_columns, {"tp": other})
    gather_lifted = Gather(group, lambda at: lifted_all.at[aligned(at, CSHARE)])
    mnorm = ScatterY(group, mn_terms, mn_y)
    gather_up = Gather(group, lambda at: up_all.at[at])
    mmoments = Moments(group, mm_own, mm_y)
    gheads = [ScatterY(group, gh_terms.at[z], gh_y.at[z]) for z in (far_half, zh)]
    swap_mix = links.copy(mix_sent, mix_came, {"tp": other})
    send_back = [
        links.copy(back.at[0], back_came.at[1], {"lat": before}),
        links.copy(back.at[1], back_came.at[0], {"lat": after}),
    ]
    gnorm = [
        Scatter(group, gn_terms.at[r], gn_y.at[r], gn_half.at[r], gn_z.at[r]) for r in range(2)
    ]
    merge_sum = LatSum(links, place, mterms, mcame_x, mpart, mcame_z)
    fine_sum = LatSum(links, place, fterms, fcame_x, fpart, fcame_z)

    embedded = []
    for r in range(2):
        kinds = lax.broadcasted_iota(jnp.int32, (8, LON), 0)
        onehot = jnp.where(classes[r : r + 1, :] == kinds, 1.0, 0.0).astype(BF16)
        embedded.append(dot_tn(onehot, class_table[...]))
    for r in range(2):
        for level in range(LEV):
            full = fields[r, level].astype(F32) + embedded[r]
            for block in range(TP):
                at = r * ROW + block * SHARE + level * 8
                hid[at : at + 8] = full[8 * block : 8 * block + 8]

    for i in range(4):
        chunk = pl.ds(i * 128, 128)
        unit, _ = standardize(hid[chunk])
        normed[chunk] = (unit * gain_fine[...]).astype(BF16)
    for r in range(2):
        rows = pl.ds(r * ROW, ROW)
        queries[rows] = low_lanes(dot_nt(normed[rows], fine_w[0:128])).astype(BF16)
        kv = dot_nt(normed[rows], fine_w[64:192]).astype(BF16)
        keys[r] = kv
        keys_sent[r] = kv

    pl.semaphore_wait(barrier, TP - 1 + len(lat_peers))
    got_merge.wait()
    for made in got_coarse:
        made.wait()
    far.start()
    for made in send_keys:
        made.start()
    gather_w.start()

    got_cotangent.wait()
    got_up.wait()
    for r in range(2):
        for level in range(LEV):
            cots = cotangent[r, level].astype(F32)
            for block in range(TP):
                at = r * ROW + block * SHARE + level * 8
                put(cotf, pl.ds(at, 8), cots[8 * block : 8 * block + 8])
    kind = lax.div(tp, 2)
    quad = get(cotf, pl.ds(lax.div(kind, 2) * ROW + lax.rem(kind, 2), CTOK, stride=2))
    quad = jnp.where(lax.rem(tp, 2) == 0, quad[:, 0:256], quad[:, 256:512]).astype(BF16)
    lift_terms[...] = dot_nt(quad, up_weight[...]).astype(BF16).reshape(ZH, YS, CSHARE, DC)
    lift.start()
    far.pass_z()

    for made in send_keys:
        made.wait_recv()
    gather_w.share()

    present = (lat > 0, lat < lat_count - 1)

    def attend(r, half):
        start = r * ROW + half * CTOK
        chunk = pl.ds(start, CTOK)
        mask = fine_mask(half * CTOK)
        query = queries[chunk]
        own = jnp.where(mask, dot_nt(query, keys[r]) * SCALE, NEGATIVE)
        far = dot_nt(query, keys_came[r]) * SCALE
        far = jnp.where(jnp.logical_and(mask, present[r]), far, NEGATIVE)
        own, far = softmax_pair(own, far)
        prob_own[chunk] = own
        prob_other[chunk] = far
        mixture[chunk] = dot(own.astype(BF16), keys[r]) + dot(far.astype(BF16), keys_came[r])

    for r in range(2):
        for half in range(2):
            attend(r, half)
    lane = lax.broadcasted_iota(jnp.int32, (ROW, 128), 1)
    packed = jnp.where(lane < 64, pltpu.roll(mixture[ROW : 2 * ROW], 64, 1), mixture[0:ROW])
    heads_all[:, aligned(tp, 128)] = packed.astype(BF16)
    near_heads.start()
    gather_w.forward()
    far.pass_x()

    lift.middle()
    near_heads.forward()
    lift_chunk = lift.finish().astype(BF16)
    lift_all[aligned(group.y, CSHARE)] = lift_chunk
    gather_lift.start()
    far.pass_core()
    near_heads.finish()
    gather_w.finish()

    low = wexp[:, 0:128].reshape(TP * 128, D)
    high = wexp[:, 64:192].reshape(TP * 128, D)

    def merge(half):
        for r, weight in ((0, low), (1, high)):
            rows = pl.ds(pl.multiple_of(r * ROW + half * HALF, HALF), HALF)
            put(resid, rows, hid[rows] + dot(heads_all[aligned(half, HALF)], weight))
        quads = [
            get(resid, pl.ds(r * ROW + half * HALF + s, CHALF, stride=2))
            for r in range(2)
            for s in range(2)
        ]
        unit, inverse = standardize(jnp.concatenate(quads, axis=1))
        merged_norm[aligned(half, CHALF)] = (unit * gain_merge[...]).astype(BF16)
        return unit, inverse

    unit, inverse = merge(zh)
    near_merged = merged_norm[aligned(zh, CHALF)]
    coarse_all[:, aligned(tp, 128)] = dot(near_merged, merge_weight[...]).astype(BF16)
    far.finish(0)
    coarse_all[:, aligned(other, 128)] = dot(near_merged, far_merge[...]).astype(BF16)
    gather_coarse.start()
    far_heads.start()
    munit[...] = unit
    minverse[...] = jnp.broadcast_to(inverse, (CHALF, 128))
    far.finish(1)
    gather_lift.finish()
    stacks = [(own_coarse, 0), (own_coarse, 1), (far_coarse, 0), (far_coarse, 1)]
    for head, (stack, at) in enumerate(stacks):
        cexp[head, 64:128] = stack[384 + 64 * at : 448 + 64 * at]
    grad_cmix = [dot_nt(lift_all[...], cexp[head]).astype(BF16) for head in range(4)]
    gather_coarse.finish()

    coarse_f[...] = coarse_all[...].astype(F32)
    unit, inverse = standardize(coarse_f[...])
    cnormed = (unit * gain_coarse[...]).astype(BF16)
    for head, (stack, at) in enumerate(stacks):
        rows = stack[192 * at + 64 : 192 * at + 192]
        ckeys[head] = dot_nt(cnormed, rows).astype(BF16)
    send_ckeys.start()
    cunit[...] = unit
    cinverse[...] = jnp.broadcast_to(inverse, (CHALF, 128))
    cq = [
        low_lanes(dot_nt(cnormed, stack[192 * at : 192 * at + 128])).astype(BF16)
        for stack, at in stacks
    ]

    row_at = lax.broadcasted_iota(jnp.int32, (CHALF, CHALF), 0)
    col_at = lax.broadcasted_iota(jnp.int32, (CHALF, CHALF), 1)
    cmask = (row_at >> 5) == (col_at >> 5)
    own_scores = [
        jnp.where(cmask, dot_nt(cq[head], ckeys[head]) * SCALE, NEGATIVE) for head in range(4)
    ]
    send_ckeys.wait_recv()
    cgrad_q, cgrad_kv = [], []
    cheads = []
    for head in range(4):
        away = jnp.where(cmask, dot_nt(cq[head], ckeys_came[head]) * SCALE, NEGATIVE)
        own, away = softmax_pair(own_scores[head], away)
        own16, far16 = own.astype(BF16), away.astype(BF16)
        grad_own = dot_nt(grad_cmix[head], ckeys[head])
        grad_far = dot_nt(grad_cmix[head], ckeys_came[head])
        ds_own, ds_far = score_grads(own, away, grad_own, grad_far)
        cback[head] = (dot_tn(ds_far, cq[head]) + dot_tn(far16, grad_cmix[head])).astype(BF16)
        cgrad_kv.append(dot_tn(ds_own, cq[head]) + dot_tn(own16, grad_cmix[head]))
        query_grad = dot(ds_own, ckeys[head]) + dot(ds_far, ckeys_came[head])
        cgrad_q.append(low_lanes(query_grad).astype(BF16))
        cheads.append((dot(own16, ckeys[head]) + dot(far16, ckeys_came[head])).astype(BF16))
    send_cback.start()
    part = sum(dot(cheads[head], cexp[head]) for head in range(4))
    cs_terms[...] = part.astype(BF16).reshape(YS, CSHARE, DC)
    part = 0.0
    for head, (stack, at) in enumerate(stacks):
        part = part + dot(cgrad_q[head], stack[192 * at : 192 * at + 128])
    send_cback.wait_recv()
    for head, (stack, at) in enumerate(stacks):
        total = (cgrad_kv[head] + cback_came[head].astype(F32)).astype(BF16)
        part = part + dot(total, stack[192 * at + 64 : 192 * at + 192])
    for t in range(TP):
        cn_terms[t % YS, t // YS] = part[:, 128 * t : 128 * t + 128].astype(BF16)
    cnorm.start()
    cmoments.start(part * gain_coarse[...], cunit[...])
    csum.start()
    far_heads.forward()

    def one_head(at, top, bottom):
        top, bottom = top.astype(BF16), bottom.astype(BF16)
        return dot_nt(top, wexp[at, 0:128]) + dot_nt(bottom, wexp[at, 64:192])

    ones = jnp.ones((8, D), BF16)
    head_terms = []
    for at in (other, tp):
        terms = []
        for s in range(2):
            cot = [get(cotf, pl.ds(r * ROW + zh * HALF + s, CHALF, stride=2)) for r in range(2)]
            unit = [munit[:, (2 * r + s) * D : (2 * r + s + 1) * D] for r in range(2)]
            terms.append((one_head(at, *cot), one_head(at, *unit)))
        head_terms.append((terms, one_head(at, ones, ones)[0:1]))

    grad_cn = cnorm.finish()
    first, second = cmoments.finish()
    for zc in range(ZH):
        lane_block = aligned(zc * YS + group.y, 128)
        inner = grad_cn[zc] * gain_coarse[:, lane_block]
        inner = cinverse[...] * (inner - first - cunit[:, lane_block] * second)
        grad_columns[zc] = (lift_all[:, lane_block].astype(F32) + inner).astype(BF16)

    part = dot_nt(grad_columns[zh], merge_weight[...])
    part = part + dot_nt(grad_columns[far_half], far_merge[...])
    inner = part * gain_merge[...]
    inner16 = inner.astype(BF16)
    for s in range(2):
        top, bottom = [inner16[:, (2 * r + s) * D : (2 * r + s + 1) * D] for r in range(2)]
        heads = (dot_nt(top, low) + dot_nt(bottom, high)).astype(BF16)
        for t in range(TP):
            some = heads[:, 128 * t : 128 * t + 128]
            gh_terms[t // YS, t % YS, s * CHALF : (s + 1) * CHALF] = some
    for part_sum in gheads:
        part_sum.start()
    mmoments.start(inner, munit[...])
    swap_columns.start()
    mn_terms[...] = part.astype(BF16).reshape(YS, CSHARE, 4 * D)
    mnorm.start()

    mine = aligned(tp, CSHARE)
    near_mine = aligned(group.y, CSHARE)
    lifted_all[mine] = (coarse_f[near_mine] + csum.finish()).astype(BF16)
    gather_lifted.start()

    first, second = mmoments.finish()
    for i, (terms, head_ones) in enumerate(head_terms):
        grad_heads = gheads[i].finish()
        for s in range(2):
            head_cot, head_unit = terms[s]
            inner = grad_heads[s * CHALF : (s + 1) * CHALF] - first * head_ones - second * head_unit
            put(grad_mix, pl.ds(s, CHALF, stride=2), head_cot + minverse[...] * inner)
        if i == 0:
            mix_sent[...] = grad_mix[0].astype(BF16)
            swap_mix.start()
    mix_all[aligned(zh, HALF)] = grad_mix[0]
    gather_lifted.forward()

    far_heads.finish()
    merge(far_half)
    swap_columns.wait_recv()
    scale = (2 * lat_count * LEV * LON) ** -0.5
    merge_rows = 4 * D // lat_count
    weight_rows = D // lat_count
    term = dot_tn(merged_norm[aligned(zh, CHALF)], grad_columns[zh])
    term = term + dot_tn(merged_norm[aligned(far_half, CHALF)], far_columns[...])
    mterms[...] = (term * scale).astype(BF16).reshape(nx, nz, 2, merge_rows, 128)
    gather_lifted.finish()
    up_all[tp] = dot(lifted_all[...], up_weight[...]).astype(BF16)
    swap_mix.wait_recv()
    mix_all[aligned(far_half, HALF)] = mix_came[...].astype(F32)
    gather_up.start()
    both = mix_all[...]
    grad_mix_rows[0:ROW] = high_lanes(both).astype(BF16)
    grad_mix_rows[ROW : 2 * ROW] = high_lanes(pltpu.roll(both, 64, 1)).astype(BF16)

    def attend_back(r, half):
        chunk = pl.ds(r * ROW + half * CTOK, CTOK)
        query, grad_out = queries[chunk], grad_mix_rows[chunk]
        own, far = prob_own[chunk], prob_other[chunk]
        ds_own, ds_far = score_grads(
            own, far, dot_nt(grad_out, keys[r]), dot_nt(grad_out, keys_came[r])
        )
        own16, far16 = own.astype(BF16), far.astype(BF16)
        to_own = dot_tn(ds_own, query) + dot_tn(own16, grad_out)
        to_far = dot_tn(ds_far, query) + dot_tn(far16, grad_out)
        grad_q[chunk] = low_lanes(dot(ds_own, keys[r]) + dot(ds_far, keys_came[r])).astype(BF16)
        return to_own, to_far

    for r in range(2):
        own_a, far_a = attend_back(r, 0)
        own_b, far_b = attend_back(r, 1)
        back[r] = (far_a + far_b).astype(BF16)
        send_back[r].start()
        grad_other[r] = own_a + own_b
    merge_sum.start()
    for made in send_back:
        made.wait_recv()
    for r in range(2):
        grad_kv[pl.ds(r * ROW, ROW)] = (grad_other[r] + back_came[r].astype(F32)).astype(BF16)
    for r in range(2):
        rows = pl.ds(r * ROW, ROW)
        part = dot(grad_q[rows], fine_w[0:128]) + dot(grad_kv[rows], fine_w[64:192])
        gn_terms[r] = part.astype(BF16).reshape(ZH, YS, SHARE, D)
        gnorm[r].start()

    term_q = dot_tn(normed[...], grad_q[...]) * scale
    term_kv = dot_tn(normed[...], grad_kv[...]) * scale
    term = jnp.concatenate(
        [term_q.reshape(lat_count, weight_rows, 128), term_kv.reshape(lat_count, weight_rows, 128)],
        axis=1,
    )
    fterms[...] = term.astype(BF16).reshape(nx, nz, 2, 2 * weight_rows, 128)
    fine_sum.start()
    gather_up.forward()
    for part in gnorm:
        part.middle()
    merge_sum.middle()
    fine_sum.middle()

    grad_mn = mnorm.finish()
    merged_chunk, cot_chunk = [], []
    for r in range(2):
        for s in range(2):
            some = pl.ds(r * ROW + s + tp * SHARE, CSHARE, stride=2)
            merged_chunk.append(get(resid, some))
            cot_chunk.append(get(cotf, some))
    merged_chunk = jnp.concatenate(merged_chunk, axis=1)
    cot_chunk = jnp.concatenate(cot_chunk, axis=1)
    grad_quads = cot_chunk + normalize_back(merged_chunk, gain_merge[...], grad_mn)
    for r in range(2):
        for s in range(2):
            some = grad_quads[:, (2 * r + s) * D : (2 * r + s + 1) * D]
            put(grad_resid, pl.ds(r * SHARE + s, CSHARE, stride=2), some)

    gather_up.finish()
    for r in range(2):
        for s in range(2):
            for part in range(2):
                wide = up_all[4 * r + 2 * s + part].astype(F32)
                some = pl.ds(r * ROW + s, CTOK, stride=2)
                up_wide[2 * part, some, :] = wide[:, 0:128]
                up_wide[2 * part + 1, some, :] = wide[:, 128:256]
    for r in range(2):
        for level in range(LEV):
            pieces = []
            for block in range(TP):
                at = r * ROW + block * SHARE + level * 8
                pieces.append(get(resid, pl.ds(at, 8)) + get(up_wide, pl.ds(at, 8)))
            fields_out[r, level] = jnp.concatenate(pieces, axis=0).astype(BF16)
    written = fetch(fields_out, next_fields, 6)

    for r in range(2):
        grad_norm = gnorm[r].finish()
        own_hidden = hid[pl.ds(pl.multiple_of(r * ROW + tp * SHARE, SHARE), SHARE)]
        grad_hidden = normalize_back(own_hidden, gain_fine[...], grad_norm)
        grad_hidden = grad_hidden + get(grad_resid, pl.ds(r * SHARE, SHARE))
        fields_grad[r] = grad_hidden.astype(BF16)
    merge_grad[...] = merge_sum.finish()
    sums = fine_sum.finish()
    fine_grad[:, 0, 0:64] = sums[0:weight_rows, 0:64]
    fine_grad[:, 0, 64:192] = sums[weight_rows : 2 * weight_rows]
    written.wait()
    links.finish()


def hand_over(*refs):
    for i in range(4):
        refs[4 + i][...] = refs[i][...]


def vmem(*shape, kind=BF16):
    return pltpu.VMEM(shape, kind)


def scatter_buffers(*chunk):
    return [vmem(ZH, YS, *chunk), vmem(YS - 1, ZH, *chunk), vmem(*chunk), vmem(*chunk)]


def halved(*buffers):
    return [vmem(2, *some.shape) for some in buffers]


def y_buffers(*chunk):
    return [vmem(YS, *chunk), vmem(YS - 1, *chunk)]


def moment_buffers():
    return [vmem(8, 128, kind=F32), vmem(YS - 1, 8, 128, kind=F32)]


def lat_buffers(nx, nz, rows):
    return [
        vmem(nx, nz, 2, rows, 128),
        vmem(2 * nx - 1, nz, rows, 128),
        vmem(nz, rows, 128),
        vmem(nz - 1, rows, 128),
    ]


def local(
    lat_count,
    fields,
    classes,
    class_table,
    gain_fine,
    fine_qkv,
    fine_out,
    gain_merge,
    merge_weight,
    gain_coarse,
    coarse_qkv,
    coarse_out,
    up_weight,
    cotangent,
):
    merge_rows, weight_rows = 4 * D // lat_count, D // lat_count
    nz = min(8, lat_count // 4)
    nx = lat_count // (2 * nz)
    whole = pl.BlockSpec(memory_space=pltpu.VMEM)
    left = pl.BlockSpec(memory_space=pl.ANY)
    copies = 240
    scratch = [
        pltpu.SemaphoreType.DMA((copies,)),
        pltpu.SemaphoreType.DMA((copies,)),
        pltpu.SemaphoreType.DMA((7,)),
        vmem(4 * D, 128),
        vmem(512, DC),
        vmem(4 * D, 128),
        vmem(512, DC),
        vmem(DC, 256),
        vmem(2, LEV, LON, D),
        vmem(2, LEV, LON, D),
        vmem(2 * ROW, D, kind=F32),
        vmem(4, 2 * ROW, 128, kind=F32),
        vmem(2 * ROW, D),
        vmem(2 * ROW, 128),
        vmem(2, ROW, 128),
        vmem(2, ROW, 128),
        vmem(2, ROW, 128),
        vmem(2 * ROW, ROW, kind=F32),
        vmem(2 * ROW, ROW, kind=F32),
        vmem(2 * ROW, 128, kind=F32),
        vmem(ROW, TP * 128),
        vmem(TP, 192, D),
        vmem(4, 128, DC),
        vmem(4, 2 * ROW, 128, kind=F32),
        vmem(CTOK, 4 * D),
        vmem(CHALF, DC),
        vmem(CHALF, DC, kind=F32),
        vmem(CHALF, DC),
        *scatter_buffers(CSHARE, DC),
        vmem(4, CHALF, 128),
        vmem(4, CHALF, 128),
        vmem(4, CHALF, 128),
        vmem(4, CHALF, 128),
        *y_buffers(CSHARE, DC),
        *y_buffers(ZH, CHALF, 128),
        vmem(CHALF, DC, kind=F32),
        vmem(CHALF, 128, kind=F32),
        *moment_buffers(),
        vmem(ZH, CHALF, 128),
        vmem(CHALF, 128),
        vmem(CTOK, DC),
        *y_buffers(CSHARE, 4 * D),
        vmem(TP, CTOK, 256),
        vmem(4, 2 * ROW, 128, kind=F32),
        vmem(CHALF, 4 * D, kind=F32),
        vmem(CHALF, 128, kind=F32),
        *moment_buffers(),
        *halved(*y_buffers(2 * CHALF, 128)),
        vmem(HALF, 128),
        vmem(HALF, 128),
        vmem(1, HALF, 128, kind=F32),
        vmem(ROW, 128, kind=F32),
        vmem(2 * ROW, 128),
        vmem(4, 2 * SHARE, 128, kind=F32),
        vmem(2 * ROW, 128),
        vmem(2 * ROW, 128),
        vmem(2, ROW, 128, kind=F32),
        vmem(2, ROW, 128),
        vmem(2, ROW, 128),
        *halved(*scatter_buffers(SHARE, D)),
        *lat_buffers(nx, nz, merge_rows),
        *lat_buffers(nx, nz, 2 * weight_rows),
    ]
    results = pl.pallas_call(
        functools.partial(main_kernel, lat_count, nx, nz),
        out_shape=(
            jax.ShapeDtypeStruct((2, LEV, LON, D), BF16),
            jax.ShapeDtypeStruct((2, SHARE, D), BF16),
            jax.ShapeDtypeStruct((weight_rows, 1, 192), F32),
            jax.ShapeDtypeStruct((merge_rows, 128), F32),
        ),
        in_specs=[whole] * 7 + [left, whole] + [left] * 4,
        out_specs=[left] + [whole] * 3,
        scratch_shapes=scratch,
        name="block",
        compiler_params=pltpu.CompilerParams(
            collective_id=0, has_side_effects=True, vmem_limit_bytes=56 * 2**20
        ),
    )(
        fields,
        classes,
        class_table,
        gain_fine.reshape(1, -1),
        fine_qkv.reshape(D, 192).T,
        fine_out.reshape(64, D),
        gain_merge.reshape(1, -1),
        merge_weight,
        gain_coarse.reshape(1, -1),
        coarse_qkv.transpose(1, 2, 0),
        coarse_out.reshape(128, DC),
        up_weight,
        cotangent,
    )
    next_fields, fields_grad, fine_grad, merge_grad = pl.pallas_call(
        hand_over,
        out_shape=tuple(jax.ShapeDtypeStruct(some.shape, some.dtype) for some in results),
        in_specs=[whole] * 4,
        out_specs=[whole] * 4,
        name="hand_over",
    )(*results)
    return next_fields, fields_grad.reshape(2, LEV, LON // TP, D), fine_grad, merge_grad


def solution(mesh):
    placed = (
        P("lat", None, None, None),
        P("lat", None),
        P(),
        P(),
        P(None, "tp", None),
        P("tp", None, None),
        P(),
        P(None, "tp"),
        P(),
        P(None, "tp", None),
        P("tp", None, None),
        P(None, "tp"),
        P("lat", None, None, None),
    )
    return jax.shard_map(
        functools.partial(local, mesh.shape["lat"]),
        mesh=mesh,
        in_specs=placed,
        out_specs=(
            P("lat", None, None, None),
            P("lat", None, "tp", None),
            P("lat", "tp", None),
            P("lat", "tp"),
        ),
        check_vma=False,
    )
```

```python
import functools

import jax
import jax.numpy as jnp
from jax import lax
from jax.experimental import pallas as pl
from jax.experimental.pallas import tpu as pltpu
from jax.sharding import PartitionSpec as P

MESH = pl.DeviceIdType.MESH
F32 = jnp.float32
BF16 = jnp.bfloat16
EPSILON = 1e-05
NEGATIVE = -1e30

D = 512
DC = 1024
LEV = 4
LON = 64
ZH = 2
YS = 4
TP = ZH * YS
ROW = LEV * LON
CTOK = ROW // 2
SHARE = ROW // TP
CSHARE = CTOK // TP
HALF = ROW // ZH
CHALF = CTOK // ZH
SCALE = 0.125


def dot(a, b):
    return lax.dot_general(a, b, (((1,), (0,)), ((), ())), preferred_element_type=F32)


def dot_nt(a, b):
    return lax.dot_general(a, b, (((1,), (1,)), ((), ())), preferred_element_type=F32)


def dot_tn(a, b):
    return lax.dot_general(a, b, (((0,), (0,)), ((), ())), preferred_element_type=F32)


def standardize(values):
    centred = values - jnp.mean(values, axis=-1, keepdims=True)
    spread = jnp.mean(centred * centred, axis=-1, keepdims=True)
    inverse = lax.rsqrt(spread + EPSILON)
    return centred * inverse, inverse


def normalize_back(values, gain, incoming):
    unit, inverse = standardize(values)
    inner = incoming * gain
    first = jnp.mean(inner, axis=-1, keepdims=True)
    second = jnp.mean(inner * unit, axis=-1, keepdims=True)
    return inverse * (inner - first - unit * second)


class Links:
    def __init__(self, send_sems, recv_sems):
        self.send_sems, self.recv_sems = send_sems, recv_sems
        self.copies = []

    def copy(self, src, dst, device):
        at = len(self.copies)
        made = pltpu.make_async_remote_copy(
            src_ref=src,
            dst_ref=dst,
            send_sem=self.send_sems.at[at],
            recv_sem=self.recv_sems.at[at],
            device_id=device,
            device_id_type=MESH,
        )
        self.copies.append(made)
        return made

    def finish(self):
        for made in self.copies:
            made.wait_send()


class Group:
    def __init__(self, links):
        self.links = links
        self.tp = lax.axis_index("tp")
        self.zh, self.y = lax.div(self.tp, YS), lax.rem(self.tp, YS)
        self.other = lax.rem(self.tp + YS, TP)

    def y_at(self, k):
        return lax.rem(self.y + k, YS)

    def along_y(self, k):
        return {"tp": self.zh * YS + self.y_at(k)}


class Gather:
    def __init__(self, group, view):
        links = group.links
        own, far = view(group.tp), view(group.other)
        self.over_z = links.copy(own, own, {"tp": group.other})
        self.over_y = [links.copy(own, own, group.along_y(k)) for k in range(1, YS)]
        self.passed = [links.copy(far, far, group.along_y(k)) for k in range(1, YS)]

    def start(self):
        for made in [self.over_z] + self.over_y:
            made.start()

    def forward(self):
        self.over_z.wait_recv()
        for made in self.passed:
            made.start()

    def finish(self):
        for made in self.over_y + self.passed:
            made.wait_recv()


class HalfGather:
    def __init__(self, group, view, near):
        links, far = group.links, 1 - near
        sent, own, passed = view(group.tp, far), view(group.tp, near), view(group.other, near)
        self.over_z = links.copy(sent, sent, {"tp": group.other})
        self.over_y = [links.copy(own, own, group.along_y(k)) for k in range(1, YS)]
        self.passed = [links.copy(passed, passed, group.along_y(k)) for k in range(1, YS)]

    start, forward, finish = Gather.start, Gather.forward, Gather.finish


class OutGather:
    def __init__(self, group, place, wexp):
        links, rows = group.links, 64 // place.nx

        def piece(at, x, core):
            return wexp.at[at, pl.ds(64 + x * rows, rows), aligned(core, 256)]

        def slot(at):
            return wexp.at[at, pl.ds(64, 64)]

        own, far = slot(group.tp), slot(group.other)
        sent = piece(group.tp, place.x, place.core)
        got = piece(group.other, place.x, place.core)
        self.over_z = links.copy(sent, sent, {"tp": group.other, **place.mirror})
        self.over_y = [links.copy(own, own, group.along_y(k)) for k in range(1, YS)]
        self.shared = [links.copy(got, got, place.at(x, place.z, c)) for x, c in place.x_peers]
        self.passed = [links.copy(far, far, group.along_y(k)) for k in range(1, YS)]

    def share(self):
        self.over_z.wait_recv()
        for made in self.shared:
            made.start()

    def forward(self):
        for made in self.shared:
            made.wait_recv()
        for made in self.passed:
            made.start()

    start, finish = Gather.start, Gather.finish


class GatherY:
    def __init__(self, group, refs):
        self.copies = [
            group.links.copy(some, some, group.along_y(k)) for k in range(1, YS) for some in refs
        ]

    def start(self):
        for made in self.copies:
            made.start()

    def finish(self):
        for made in self.copies:
            made.wait_recv()


class ScatterY:
    def __init__(self, group, terms, came):
        self.group, self.terms, self.came = group, terms, came
        self.copies = [
            group.links.copy(terms.at[group.y_at(k)], came.at[k - 1], group.along_y(k))
            for k in range(1, YS)
        ]

    start, wait = GatherY.start, GatherY.finish

    def finish(self):
        self.wait()
        total = self.terms[self.group.y].astype(F32)
        for k in range(YS - 1):
            total = total + self.came[k].astype(F32)
        return total


class Scatter:
    def __init__(self, group, terms, came_y, half, came_z):
        self.group, self.terms = group, terms
        self.came_y, self.half, self.came_z = came_y, half, came_z
        links = group.links
        self.over_y = [
            links.copy(terms.at[:, group.y_at(k)], came_y.at[k - 1], group.along_y(k))
            for k in range(1, YS)
        ]
        self.over_z = links.copy(half, came_z, {"tp": group.other})

    def start(self):
        for made in self.over_y:
            made.start()

    def summed(self, zh):
        total = self.terms[zh, self.group.y].astype(F32)
        for k in range(YS - 1):
            total = total + self.came_y[k, zh].astype(F32)
        return total

    def middle(self):
        for made in self.over_y:
            made.wait_recv()
        self.half[...] = self.summed(1 - self.group.zh).astype(BF16)
        self.over_z.start()

    def finish(self):
        own = self.summed(self.group.zh)
        self.over_z.wait_recv()
        return own + self.came_z[...].astype(F32)


class Moments:
    def __init__(self, group, own, came):
        self.own, self.came = own, came
        self.copies = [
            group.links.copy(own, came.at[k - 1], group.along_y(k)) for k in range(1, YS)
        ]

    def start(self, inner, unit):
        first = jnp.mean(inner, axis=-1, keepdims=True)
        second = jnp.mean(inner * unit, axis=-1, keepdims=True)
        lane = lax.broadcasted_iota(jnp.int32, (CHALF, 128), 1)
        both = jnp.where(lane == 0, first, jnp.where(lane == 1, second, 0.0))
        both = jnp.concatenate([both, jnp.zeros((128 - CHALF, 128), F32)], axis=0)
        self.own[...] = both.T[0:8]
        for made in self.copies:
            made.start()

    def finish(self):
        total = self.own[...]
        for k in range(YS - 1):
            self.copies[k].wait_recv()
            total = total + self.came[k]
        both = jnp.concatenate([total, jnp.zeros((120, 128), F32)], axis=0).T
        return both[0:CHALF, 0:1], both[0:CHALF, 1:2]


class LatSum:
    def __init__(self, links, place, terms, came_x, part, came_z):
        self.place, self.terms, self.came_x, self.part, self.came_z = (
            place,
            terms,
            came_x,
            part,
            came_z,
        )
        self.over_x = [
            links.copy(terms.at[x, :, core], came_x.at[k], place.at(x, place.z, core))
            for k, (x, core) in enumerate(place.x_peers)
        ]
        self.over_z = [
            links.copy(part.at[z], came_z.at[k], place.at(place.x, z, place.core))
            for k, z in enumerate(place.z_peers)
        ]

    def start(self):
        for made in self.over_x:
            made.start()

    def middle(self):
        for made in self.over_x:
            made.wait_recv()
        total = self.terms[self.place.x, :, self.place.core].astype(F32)
        for k in range(len(self.over_x)):
            total = total + self.came_x[k].astype(F32)
        self.part[...] = total.astype(BF16)
        for made in self.over_z:
            made.start()

    def finish(self):
        for made in self.over_z:
            made.wait_recv()
        total = self.part[self.place.z].astype(F32)
        for k in range(len(self.over_z)):
            total = total + self.came_z[k].astype(F32)
        return total


class FarWeights:
    def __init__(self, group, place, sources, targets):
        links, nx, nz = group.links, place.nx, place.nz
        mine = 2 * place.x + place.core
        (merge, coarse), (far_merge, far_coarse) = sources, targets
        merge_rows, coarse_rows = 4 * D // (2 * nx), 512 // (2 * nx)
        rows, lanes = merge_rows // nz, DC // nz

        def piece(refs, z):
            start = pl.multiple_of(mine * merge_rows + z * rows, rows)
            return [
                refs[0].at[pl.ds(start, rows)],
                refs[1].at[aligned(mine, coarse_rows), aligned(z, lanes)],
            ]

        def plane(x):
            at = 2 * x + place.core
            return [
                far_merge.at[aligned(at, merge_rows)],
                far_coarse.at[aligned(at, coarse_rows)],
            ]

        got = piece(targets, place.z)
        away = nz - 1 - place.z
        self.fetched = [
            links.copy(src, dst, {"tp": group.other, **place.mirror})
            for src, dst in zip(piece(sources, away), piece(targets, away))
        ]
        self.along_z = [
            links.copy(some, some, place.at(place.x, z, place.core))
            for some in got
            for z in place.z_peers
        ]
        self.along_x = [
            links.copy(some, some, place.at(x, place.z, core))
            for some in plane(place.x)
            for x, core in place.x_peers[1::2]
        ]
        self.to_twin = [
            links.copy(plane(x)[which], plane(x)[which], place.at(place.x, place.z, 1 - place.core))
            for which in range(2)
            for x in range(nx)
        ]

    def start(self):
        for made in self.fetched:
            made.start()

    def pass_z(self):
        self.step(self.fetched, self.along_z)

    def half(self, copies, which):
        count = len(copies) // 2
        return copies[which * count : (which + 1) * count]

    def step(self, before, then):
        for which in range(2):
            for made in self.half(before, which):
                made.wait_recv()
            for made in self.half(then, which):
                made.start()

    def pass_x(self):
        self.step(self.along_z, self.along_x)

    def pass_core(self):
        self.step(self.along_x, self.to_twin)

    def finish(self, which):
        for made in self.half(self.to_twin, which):
            made.wait_recv()


class Place:
    def __init__(self, nx, nz):
        lat = lax.axis_index("lat")
        self.nx, self.nz = nx, nz
        self.core = lax.rem(lat, 2)
        self.z = lax.rem(lax.div(lat, 2), nz)
        self.x = lax.div(lat, 2 * nz)
        self.x_peers = [
            (lax.rem(self.x + i, nx), lax.rem(self.core + j, 2))
            for i in range(nx)
            for j in range(2)
            if i or j
        ]
        self.mirror = self.at(self.x, nz - 1 - self.z, self.core)
        self.z_peers = [lax.rem(self.z + k, nz) for k in range(1, nz)]

    def at(self, x, z, core):
        return {"lat": (x * self.nz + z) * 2 + core}


def aligned(index, size):
    return pl.ds(pl.multiple_of(index * size, size), size)


def put(ref, rows, values):
    for j in range(values.shape[1] // 128):
        ref[j, rows, :] = values[:, 128 * j : 128 * j + 128]


def get(ref, rows):
    return jnp.concatenate([ref[j, rows, :] for j in range(ref.shape[0])], axis=1)


def softmax_pair(own, other):
    largest = jnp.maximum(
        jnp.max(own, axis=-1, keepdims=True), jnp.max(other, axis=-1, keepdims=True)
    )
    own, other = jnp.exp(own - largest), jnp.exp(other - largest)
    total = jnp.sum(own, axis=-1, keepdims=True) + jnp.sum(other, axis=-1, keepdims=True)
    return own / total, other / total


def score_grads(prob_own, prob_other, grad_own, grad_other):
    mean = jnp.sum(grad_own * prob_own, axis=-1, keepdims=True)
    mean = mean + jnp.sum(grad_other * prob_other, axis=-1, keepdims=True)
    return (
        (prob_own * (grad_own - mean) * SCALE).astype(BF16),
        (prob_other * (grad_other - mean) * SCALE).astype(BF16),
    )


def low_lanes(values):
    lane = lax.broadcasted_iota(jnp.int32, values.shape, 1)
    return jnp.where(lane < 64, values, 0.0)


def high_lanes(values):
    lane = lax.broadcasted_iota(jnp.int32, values.shape, 1)
    return jnp.where(lane >= 64, values, 0.0)


def fine_mask(start):
    def window(index):
        return ((index >> 5) + 7 + ((index & 7) >> 2)) & 7

    query = lax.broadcasted_iota(jnp.int32, (CTOK, ROW), 0) + start
    key = lax.broadcasted_iota(jnp.int32, (CTOK, ROW), 1)
    return window(query) == window(key)


def main_kernel(
    lat_count,
    nx,
    nz,
    fields,
    classes,
    class_table,
    gain_fine,
    fine_w,
    fine_out,
    gain_merge,
    merge_weight_in,
    gain_coarse,
    coarse_w_in,
    coarse_out_in,
    up_weight_in,
    cotangent_in,
    next_fields,
    fields_grad,
    fine_grad,
    merge_grad,
    send_sems,
    recv_sems,
    local_sems,
    merge_weight,
    own_coarse,
    far_merge,
    far_coarse,
    up_weight,
    cotangent,
    fields_out,
    hid,
    cotf,
    normed,
    queries,
    keys,
    keys_sent,
    keys_came,
    prob_own,
    prob_other,
    mixture,
    heads_all,
    wexp,
    cexp,
    resid,
    merged_norm,
    coarse_all,
    coarse_f,
    lift_all,
    lift_terms,
    lift_y,
    lift_half,
    lift_z,
    ckeys,
    ckeys_came,
    cback,
    cback_came,
    cs_terms,
    cs_y,
    cn_terms,
    cn_y,
    cunit,
    cinverse,
    cm_own,
    cm_y,
    grad_columns,
    far_columns,
    lifted_all,
    mn_terms,
    mn_y,
    up_all,
    up_wide,
    munit,
    minverse,
    mm_own,
    mm_y,
    gh_terms,
    gh_y,
    mix_sent,
    mix_came,
    grad_mix,
    mix_all,
    grad_mix_rows,
    grad_resid,
    grad_q,
    grad_kv,
    grad_other,
    back,
    back_came,
    gn_terms,
    gn_y,
    gn_half,
    gn_z,
    mterms,
    mcame_x,
    mpart,
    mcame_z,
    fterms,
    fcame_x,
    fpart,
    fcame_z,
):
    def fetch(src, dst, at):
        made = pltpu.make_async_copy(src, dst, local_sems.at[at])
        made.start()
        return made

    got_cotangent = fetch(cotangent_in, cotangent, 0)
    got_up = fetch(up_weight_in, up_weight, 1)
    got_merge = fetch(merge_weight_in, merge_weight, 2)
    got_coarse = [
        fetch(coarse_w_in.at[0], own_coarse.at[pl.ds(0, 192)], 3),
        fetch(coarse_w_in.at[1], own_coarse.at[pl.ds(192, 192)], 4),
        fetch(coarse_out_in, own_coarse.at[pl.ds(384, 128)], 5),
    ]

    links = Links(send_sems, recv_sems)
    group = Group(links)
    tp = group.tp
    lat = lax.axis_index("lat")
    before, after = lax.rem(lat + lat_count - 1, lat_count), lax.rem(lat + 1, lat_count)
    twin = lat + 1 - 2 * lax.rem(lat, 2)

    barrier = pltpu.get_barrier_semaphore()
    for k in range(1, TP):
        pl.semaphore_signal(
            barrier, inc=1, device_id={"tp": lax.rem(tp + k, TP)}, device_id_type=MESH
        )
    place = Place(nx, nz)
    lat_peers = [{"lat": before}, {"lat": after}]
    lat_peers += [place.at(x, place.z, core) for x, core in place.x_peers]
    lat_peers += [place.at(place.x, z, place.core) for z in place.z_peers]
    lat_peers.append({"tp": group.other, **place.mirror})
    for peer in lat_peers:
        pl.semaphore_signal(barrier, inc=1, device_id=peer, device_id_type=MESH)

    blank = jnp.zeros((TP, 64, D), BF16)
    wexp[:, 0:64] = blank
    wexp[:, 128:192] = blank
    wexp[tp, 64:128] = fine_out[...]
    for head in range(4):
        cexp[head, 0:64] = jnp.zeros((64, DC), BF16)

    gather_w = OutGather(group, place, wexp)
    lift = Scatter(group, lift_terms, lift_y, lift_half, lift_z)
    send_keys = [
        links.copy(keys_sent.at[1], keys_came.at[0], {"lat": after}),
        links.copy(keys_sent.at[0], keys_came.at[1], {"lat": before}),
    ]
    zh, other = group.zh, group.other
    far_half = 1 - zh

    def head_slot(at, half):
        return heads_all.at[aligned(half, HALF), aligned(at, 128)]

    near_heads = HalfGather(group, head_slot, zh)
    far_heads = HalfGather(group, head_slot, far_half)
    gather_lift = GatherY(group, [lift_all.at[aligned(group.y, CSHARE)]])
    gather_coarse = GatherY(
        group, [coarse_all.at[:, aligned(tp, 128)], coarse_all.at[:, aligned(other, 128)]]
    )
    far = FarWeights(group, place, (merge_weight, own_coarse), (far_merge, far_coarse))
    send_ckeys = links.copy(ckeys, ckeys_came, {"lat": twin})
    send_cback = links.copy(cback, cback_came, {"lat": twin})
    csum = ScatterY(group, cs_terms, cs_y)
    cnorm = ScatterY(group, cn_terms, cn_y)
    cmoments = Moments(group, cm_own, cm_y)
    swap_columns = links.copy(grad_columns.at[far_half], far_columns, {"tp": other})
    gather_lifted = Gather(group, lambda at: lifted_all.at[aligned(at, CSHARE)])
    mnorm = ScatterY(group, mn_terms, mn_y)
    gather_up = Gather(group, lambda at: up_all.at[at])
    mmoments = Moments(group, mm_own, mm_y)
    gheads = [ScatterY(group, gh_terms.at[z], gh_y.at[z]) for z in (far_half, zh)]
    swap_mix = links.copy(mix_sent, mix_came, {"tp": other})
    send_back = [
        links.copy(back.at[0], back_came.at[1], {"lat": before}),
        links.copy(back.at[1], back_came.at[0], {"lat": after}),
    ]
    gnorm = [
        Scatter(group, gn_terms.at[r], gn_y.at[r], gn_half.at[r], gn_z.at[r]) for r in range(2)
    ]
    merge_sum = LatSum(links, place, mterms, mcame_x, mpart, mcame_z)
    fine_sum = LatSum(links, place, fterms, fcame_x, fpart, fcame_z)

    embedded = []
    for r in range(2):
        kinds = lax.broadcasted_iota(jnp.int32, (8, LON), 0)
        onehot = jnp.where(classes[r : r + 1, :] == kinds, 1.0, 0.0).astype(BF16)
        embedded.append(dot_tn(onehot, class_table[...]))
    for r in range(2):
        for level in range(LEV):
            full = fields[r, level].astype(F32) + embedded[r]
            for block in range(TP):
                at = r * ROW + block * SHARE + level * 8
                hid[at : at + 8] = full[8 * block : 8 * block + 8]

    for i in range(4):
        chunk = pl.ds(i * 128, 128)
        unit, _ = standardize(hid[chunk])
        normed[chunk] = (unit * gain_fine[...]).astype(BF16)
    for r in range(2):
        rows = pl.ds(r * ROW, ROW)
        queries[rows] = low_lanes(dot_nt(normed[rows], fine_w[0:128])).astype(BF16)
        kv = dot_nt(normed[rows], fine_w[64:192]).astype(BF16)
        keys[r] = kv
        keys_sent[r] = kv

    pl.semaphore_wait(barrier, TP - 1 + len(lat_peers))
    got_merge.wait()
    for made in got_coarse:
        made.wait()
    far.start()
    for made in send_keys:
        made.start()

    got_cotangent.wait()
    got_up.wait()
    for r in range(2):
        for level in range(LEV):
            cots = cotangent[r, level].astype(F32)
            for block in range(TP):
                at = r * ROW + block * SHARE + level * 8
                put(cotf, pl.ds(at, 8), cots[8 * block : 8 * block + 8])
    kind = lax.div(tp, 2)
    quad = get(cotf, pl.ds(lax.div(kind, 2) * ROW + lax.rem(kind, 2), CTOK, stride=2))
    quad = jnp.where(lax.rem(tp, 2) == 0, quad[:, 0:256], quad[:, 256:512]).astype(BF16)
    lift_terms[...] = dot_nt(quad, up_weight[...]).astype(BF16).reshape(ZH, YS, CSHARE, DC)
    gather_w.start()
    far.pass_z()
    lift.start()

    for made in send_keys:
        made.wait_recv()
    gather_w.share()

    present = (lat > 0, lat < lat_count - 1)

    def attend(r, half):
        start = r * ROW + half * CTOK
        chunk = pl.ds(start, CTOK)
        mask = fine_mask(half * CTOK)
        query = queries[chunk]
        own = jnp.where(mask, dot_nt(query, keys[r]) * SCALE, NEGATIVE)
        far = dot_nt(query, keys_came[r]) * SCALE
        far = jnp.where(jnp.logical_and(mask, present[r]), far, NEGATIVE)
        own, far = softmax_pair(own, far)
        prob_own[chunk] = own
        prob_other[chunk] = far
        mixture[chunk] = dot(own.astype(BF16), keys[r]) + dot(far.astype(BF16), keys_came[r])

    for r in range(2):
        for half in range(2):
            attend(r, half)
    lane = lax.broadcasted_iota(jnp.int32, (ROW, 128), 1)
    packed = jnp.where(lane < 64, pltpu.roll(mixture[ROW : 2 * ROW], 64, 1), mixture[0:ROW])
    heads_all[:, aligned(tp, 128)] = packed.astype(BF16)
    near_heads.start()
    gather_w.forward()
    far.pass_x()

    lift.middle()
    near_heads.forward()
    lift_chunk = lift.finish().astype(BF16)
    lift_all[aligned(group.y, CSHARE)] = lift_chunk
    gather_lift.start()
    far.pass_core()
    near_heads.finish()
    gather_w.finish()

    low = wexp[:, 0:128].reshape(TP * 128, D)
    high = wexp[:, 64:192].reshape(TP * 128, D)

    def merge(half):
        for r, weight in ((0, low), (1, high)):
            rows = pl.ds(pl.multiple_of(r * ROW + half * HALF, HALF), HALF)
            put(resid, rows, hid[rows] + dot(heads_all[aligned(half, HALF)], weight))
        quads = [
            get(resid, pl.ds(r * ROW + half * HALF + s, CHALF, stride=2))
            for r in range(2)
            for s in range(2)
        ]
        unit, inverse = standardize(jnp.concatenate(quads, axis=1))
        merged_norm[aligned(half, CHALF)] = (unit * gain_merge[...]).astype(BF16)
        return unit, inverse

    unit, inverse = merge(zh)
    near_merged = merged_norm[aligned(zh, CHALF)]
    coarse_all[:, aligned(tp, 128)] = dot(near_merged, merge_weight[...]).astype(BF16)
    far.finish(0)
    coarse_all[:, aligned(other, 128)] = dot(near_merged, far_merge[...]).astype(BF16)
    gather_coarse.start()
    far_heads.start()
    munit[...] = unit
    minverse[...] = jnp.broadcast_to(inverse, (CHALF, 128))
    far.finish(1)
    gather_lift.finish()
    stacks = [(own_coarse, 0), (own_coarse, 1), (far_coarse, 0), (far_coarse, 1)]
    for head, (stack, at) in enumerate(stacks):
        cexp[head, 64:128] = stack[384 + 64 * at : 448 + 64 * at]
    grad_cmix = [dot_nt(lift_all[...], cexp[head]).astype(BF16) for head in range(4)]
    gather_coarse.finish()

    coarse_f[...] = coarse_all[...].astype(F32)
    unit, inverse = standardize(coarse_f[...])
    cnormed = (unit * gain_coarse[...]).astype(BF16)
    for head, (stack, at) in enumerate(stacks):
        rows = stack[192 * at + 64 : 192 * at + 192]
        ckeys[head] = dot_nt(cnormed, rows).astype(BF16)
    send_ckeys.start()
    cunit[...] = unit
    cinverse[...] = jnp.broadcast_to(inverse, (CHALF, 128))
    cq = [
        low_lanes(dot_nt(cnormed, stack[192 * at : 192 * at + 128])).astype(BF16)
        for stack, at in stacks
    ]

    row_at = lax.broadcasted_iota(jnp.int32, (CHALF, CHALF), 0)
    col_at = lax.broadcasted_iota(jnp.int32, (CHALF, CHALF), 1)
    cmask = (row_at >> 5) == (col_at >> 5)
    own_scores = [
        jnp.where(cmask, dot_nt(cq[head], ckeys[head]) * SCALE, NEGATIVE) for head in range(4)
    ]
    send_ckeys.wait_recv()
    cgrad_q, cgrad_kv = [], []
    cheads = []
    for head in range(4):
        away = jnp.where(cmask, dot_nt(cq[head], ckeys_came[head]) * SCALE, NEGATIVE)
        own, away = softmax_pair(own_scores[head], away)
        own16, far16 = own.astype(BF16), away.astype(BF16)
        grad_own = dot_nt(grad_cmix[head], ckeys[head])
        grad_far = dot_nt(grad_cmix[head], ckeys_came[head])
        ds_own, ds_far = score_grads(own, away, grad_own, grad_far)
        cback[head] = (dot_tn(ds_far, cq[head]) + dot_tn(far16, grad_cmix[head])).astype(BF16)
        cgrad_kv.append(dot_tn(ds_own, cq[head]) + dot_tn(own16, grad_cmix[head]))
        query_grad = dot(ds_own, ckeys[head]) + dot(ds_far, ckeys_came[head])
        cgrad_q.append(low_lanes(query_grad).astype(BF16))
        cheads.append((dot(own16, ckeys[head]) + dot(far16, ckeys_came[head])).astype(BF16))
    send_cback.start()
    part = sum(dot(cheads[head], cexp[head]) for head in range(4))
    cs_terms[...] = part.astype(BF16).reshape(YS, CSHARE, DC)
    part = 0.0
    for head, (stack, at) in enumerate(stacks):
        part = part + dot(cgrad_q[head], stack[192 * at : 192 * at + 128])
    send_cback.wait_recv()
    for head, (stack, at) in enumerate(stacks):
        total = (cgrad_kv[head] + cback_came[head].astype(F32)).astype(BF16)
        part = part + dot(total, stack[192 * at + 64 : 192 * at + 192])
    for t in range(TP):
        cn_terms[t % YS, t // YS] = part[:, 128 * t : 128 * t + 128].astype(BF16)
    cnorm.start()
    cmoments.start(part * gain_coarse[...], cunit[...])
    csum.start()
    far_heads.forward()

    def one_head(at, top, bottom):
        top, bottom = top.astype(BF16), bottom.astype(BF16)
        return dot_nt(top, wexp[at, 0:128]) + dot_nt(bottom, wexp[at, 64:192])

    ones = jnp.ones((8, D), BF16)
    head_terms = []
    for at in (other, tp):
        terms = []
        for s in range(2):
            cot = [get(cotf, pl.ds(r * ROW + zh * HALF + s, CHALF, stride=2)) for r in range(2)]
            unit = [munit[:, (2 * r + s) * D : (2 * r + s + 1) * D] for r in range(2)]
            terms.append((one_head(at, *cot), one_head(at, *unit)))
        head_terms.append((terms, one_head(at, ones, ones)[0:1]))

    grad_cn = cnorm.finish()
    first, second = cmoments.finish()
    for zc in range(ZH):
        lane_block = aligned(zc * YS + group.y, 128)
        inner = grad_cn[zc] * gain_coarse[:, lane_block]
        inner = cinverse[...] * (inner - first - cunit[:, lane_block] * second)
        grad_columns[zc] = (lift_all[:, lane_block].astype(F32) + inner).astype(BF16)

    part = dot_nt(grad_columns[zh], merge_weight[...])
    part = part + dot_nt(grad_columns[far_half], far_merge[...])
    inner = part * gain_merge[...]
    inner16 = inner.astype(BF16)
    for s in range(2):
        top, bottom = [inner16[:, (2 * r + s) * D : (2 * r + s + 1) * D] for r in range(2)]
        heads = (dot_nt(top, low) + dot_nt(bottom, high)).astype(BF16)
        for t in range(TP):
            some = heads[:, 128 * t : 128 * t + 128]
            gh_terms[t // YS, t % YS, s * CHALF : (s + 1) * CHALF] = some
    for part_sum in gheads:
        part_sum.start()
    mmoments.start(inner, munit[...])
    swap_columns.start()
    mn_terms[...] = part.astype(BF16).reshape(YS, CSHARE, 4 * D)
    mnorm.start()

    mine = aligned(tp, CSHARE)
    near_mine = aligned(group.y, CSHARE)
    lifted_all[mine] = (coarse_f[near_mine] + csum.finish()).astype(BF16)
    gather_lifted.start()

    first, second = mmoments.finish()
    for i, (terms, head_ones) in enumerate(head_terms):
        grad_heads = gheads[i].finish()
        for s in range(2):
            head_cot, head_unit = terms[s]
            inner = grad_heads[s * CHALF : (s + 1) * CHALF] - first * head_ones - second * head_unit
            put(grad_mix, pl.ds(s, CHALF, stride=2), head_cot + minverse[...] * inner)
        if i == 0:
            mix_sent[...] = grad_mix[0].astype(BF16)
            swap_mix.start()
    mix_all[aligned(zh, HALF)] = grad_mix[0]
    gather_lifted.forward()

    far_heads.finish()
    merge(far_half)
    swap_columns.wait_recv()
    scale = (2 * lat_count * LEV * LON) ** -0.5
    merge_rows = 4 * D // lat_count
    weight_rows = D // lat_count
    term = dot_tn(merged_norm[aligned(zh, CHALF)], grad_columns[zh])
    term = term + dot_tn(merged_norm[aligned(far_half, CHALF)], far_columns[...])
    mterms[...] = (term * scale).astype(BF16).reshape(nx, nz, 2, merge_rows, 128)
    gather_lifted.finish()
    up_all[tp] = dot(lifted_all[...], up_weight[...]).astype(BF16)
    swap_mix.wait_recv()
    mix_all[aligned(far_half, HALF)] = mix_came[...].astype(F32)
    gather_up.start()
    both = mix_all[...]
    grad_mix_rows[0:ROW] = high_lanes(both).astype(BF16)
    grad_mix_rows[ROW : 2 * ROW] = high_lanes(pltpu.roll(both, 64, 1)).astype(BF16)

    def attend_back(r, half):
        chunk = pl.ds(r * ROW + half * CTOK, CTOK)
        query, grad_out = queries[chunk], grad_mix_rows[chunk]
        own, far = prob_own[chunk], prob_other[chunk]
        ds_own, ds_far = score_grads(
            own, far, dot_nt(grad_out, keys[r]), dot_nt(grad_out, keys_came[r])
        )
        own16, far16 = own.astype(BF16), far.astype(BF16)
        to_own = dot_tn(ds_own, query) + dot_tn(own16, grad_out)
        to_far = dot_tn(ds_far, query) + dot_tn(far16, grad_out)
        grad_q[chunk] = low_lanes(dot(ds_own, keys[r]) + dot(ds_far, keys_came[r])).astype(BF16)
        return to_own, to_far

    for r in range(2):
        own_a, far_a = attend_back(r, 0)
        own_b, far_b = attend_back(r, 1)
        back[r] = (far_a + far_b).astype(BF16)
        send_back[r].start()
        grad_other[r] = own_a + own_b
    merge_sum.start()
    for made in send_back:
        made.wait_recv()
    for r in range(2):
        grad_kv[pl.ds(r * ROW, ROW)] = (grad_other[r] + back_came[r].astype(F32)).astype(BF16)
    for r in range(2):
        rows = pl.ds(r * ROW, ROW)
        part = dot(grad_q[rows], fine_w[0:128]) + dot(grad_kv[rows], fine_w[64:192])
        gn_terms[r] = part.astype(BF16).reshape(ZH, YS, SHARE, D)
        gnorm[r].start()

    term_q = dot_tn(normed[...], grad_q[...]) * scale
    term_kv = dot_tn(normed[...], grad_kv[...]) * scale
    term = jnp.concatenate(
        [term_q.reshape(lat_count, weight_rows, 128), term_kv.reshape(lat_count, weight_rows, 128)],
        axis=1,
    )
    fterms[...] = term.astype(BF16).reshape(nx, nz, 2, 2 * weight_rows, 128)
    fine_sum.start()
    gather_up.forward()
    for part in gnorm:
        part.middle()
    merge_sum.middle()
    fine_sum.middle()

    grad_mn = mnorm.finish()
    merged_chunk, cot_chunk = [], []
    for r in range(2):
        for s in range(2):
            some = pl.ds(r * ROW + s + tp * SHARE, CSHARE, stride=2)
            merged_chunk.append(get(resid, some))
            cot_chunk.append(get(cotf, some))
    merged_chunk = jnp.concatenate(merged_chunk, axis=1)
    cot_chunk = jnp.concatenate(cot_chunk, axis=1)
    grad_quads = cot_chunk + normalize_back(merged_chunk, gain_merge[...], grad_mn)
    for r in range(2):
        for s in range(2):
            some = grad_quads[:, (2 * r + s) * D : (2 * r + s + 1) * D]
            put(grad_resid, pl.ds(r * SHARE + s, CSHARE, stride=2), some)

    gather_up.finish()
    for r in range(2):
        for s in range(2):
            for part in range(2):
                wide = up_all[4 * r + 2 * s + part].astype(F32)
                some = pl.ds(r * ROW + s, CTOK, stride=2)
                up_wide[2 * part, some, :] = wide[:, 0:128]
                up_wide[2 * part + 1, some, :] = wide[:, 128:256]
    for r in range(2):
        for level in range(LEV):
            pieces = []
            for block in range(TP):
                at = r * ROW + block * SHARE + level * 8
                pieces.append(get(resid, pl.ds(at, 8)) + get(up_wide, pl.ds(at, 8)))
            fields_out[r, level] = jnp.concatenate(pieces, axis=0).astype(BF16)
    written = fetch(fields_out, next_fields, 6)

    for r in range(2):
        grad_norm = gnorm[r].finish()
        own_hidden = hid[pl.ds(pl.multiple_of(r * ROW + tp * SHARE, SHARE), SHARE)]
        grad_hidden = normalize_back(own_hidden, gain_fine[...], grad_norm)
        grad_hidden = grad_hidden + get(grad_resid, pl.ds(r * SHARE, SHARE))
        fields_grad[r] = grad_hidden.astype(BF16)
    merge_grad[...] = merge_sum.finish()
    sums = fine_sum.finish()
    fine_grad[:, 0, 0:64] = sums[0:weight_rows, 0:64]
    fine_grad[:, 0, 64:192] = sums[weight_rows : 2 * weight_rows]
    written.wait()
    links.finish()


def hand_over(*refs):
    for i in range(4):
        refs[4 + i][...] = refs[i][...]


def vmem(*shape, kind=BF16):
    return pltpu.VMEM(shape, kind)


def scatter_buffers(*chunk):
    return [vmem(ZH, YS, *chunk), vmem(YS - 1, ZH, *chunk), vmem(*chunk), vmem(*chunk)]


def halved(*buffers):
    return [vmem(2, *some.shape) for some in buffers]


def y_buffers(*chunk):
    return [vmem(YS, *chunk), vmem(YS - 1, *chunk)]


def moment_buffers():
    return [vmem(8, 128, kind=F32), vmem(YS - 1, 8, 128, kind=F32)]


def lat_buffers(nx, nz, rows):
    return [
        vmem(nx, nz, 2, rows, 128),
        vmem(2 * nx - 1, nz, rows, 128),
        vmem(nz, rows, 128),
        vmem(nz - 1, rows, 128),
    ]


def local(
    lat_count,
    fields,
    classes,
    class_table,
    gain_fine,
    fine_qkv,
    fine_out,
    gain_merge,
    merge_weight,
    gain_coarse,
    coarse_qkv,
    coarse_out,
    up_weight,
    cotangent,
):
    merge_rows, weight_rows = 4 * D // lat_count, D // lat_count
    nz = min(8, lat_count // 4)
    nx = lat_count // (2 * nz)
    whole = pl.BlockSpec(memory_space=pltpu.VMEM)
    left = pl.BlockSpec(memory_space=pl.ANY)
    copies = 240
    scratch = [
        pltpu.SemaphoreType.DMA((copies,)),
        pltpu.SemaphoreType.DMA((copies,)),
        pltpu.SemaphoreType.DMA((7,)),
        vmem(4 * D, 128),
        vmem(512, DC),
        vmem(4 * D, 128),
        vmem(512, DC),
        vmem(DC, 256),
        vmem(2, LEV, LON, D),
        vmem(2, LEV, LON, D),
        vmem(2 * ROW, D, kind=F32),
        vmem(4, 2 * ROW, 128, kind=F32),
        vmem(2 * ROW, D),
        vmem(2 * ROW, 128),
        vmem(2, ROW, 128),
        vmem(2, ROW, 128),
        vmem(2, ROW, 128),
        vmem(2 * ROW, ROW, kind=F32),
        vmem(2 * ROW, ROW, kind=F32),
        vmem(2 * ROW, 128, kind=F32),
        vmem(ROW, TP * 128),
        vmem(TP, 192, D),
        vmem(4, 128, DC),
        vmem(4, 2 * ROW, 128, kind=F32),
        vmem(CTOK, 4 * D),
        vmem(CHALF, DC),
        vmem(CHALF, DC, kind=F32),
        vmem(CHALF, DC),
        *scatter_buffers(CSHARE, DC),
        vmem(4, CHALF, 128),
        vmem(4, CHALF, 128),
        vmem(4, CHALF, 128),
        vmem(4, CHALF, 128),
        *y_buffers(CSHARE, DC),
        *y_buffers(ZH, CHALF, 128),
        vmem(CHALF, DC, kind=F32),
        vmem(CHALF, 128, kind=F32),
        *moment_buffers(),
        vmem(ZH, CHALF, 128),
        vmem(CHALF, 128),
        vmem(CTOK, DC),
        *y_buffers(CSHARE, 4 * D),
        vmem(TP, CTOK, 256),
        vmem(4, 2 * ROW, 128, kind=F32),
        vmem(CHALF, 4 * D, kind=F32),
        vmem(CHALF, 128, kind=F32),
        *moment_buffers(),
        *halved(*y_buffers(2 * CHALF, 128)),
        vmem(HALF, 128),
        vmem(HALF, 128),
        vmem(1, HALF, 128, kind=F32),
        vmem(ROW, 128, kind=F32),
        vmem(2 * ROW, 128),
        vmem(4, 2 * SHARE, 128, kind=F32),
        vmem(2 * ROW, 128),
        vmem(2 * ROW, 128),
        vmem(2, ROW, 128, kind=F32),
        vmem(2, ROW, 128),
        vmem(2, ROW, 128),
        *halved(*scatter_buffers(SHARE, D)),
        *lat_buffers(nx, nz, merge_rows),
        *lat_buffers(nx, nz, 2 * weight_rows),
    ]
    results = pl.pallas_call(
        functools.partial(main_kernel, lat_count, nx, nz),
        out_shape=(
            jax.ShapeDtypeStruct((2, LEV, LON, D), BF16),
            jax.ShapeDtypeStruct((2, SHARE, D), BF16),
            jax.ShapeDtypeStruct((weight_rows, 1, 192), F32),
            jax.ShapeDtypeStruct((merge_rows, 128), F32),
        ),
        in_specs=[whole] * 7 + [left, whole] + [left] * 4,
        out_specs=[left] + [whole] * 3,
        scratch_shapes=scratch,
        name="block",
        compiler_params=pltpu.CompilerParams(
            collective_id=0, has_side_effects=True, vmem_limit_bytes=56 * 2**20
        ),
    )(
        fields,
        classes,
        class_table,
        gain_fine.reshape(1, -1),
        fine_qkv.reshape(D, 192).T,
        fine_out.reshape(64, D),
        gain_merge.reshape(1, -1),
        merge_weight,
        gain_coarse.reshape(1, -1),
        coarse_qkv.transpose(1, 2, 0),
        coarse_out.reshape(128, DC),
        up_weight,
        cotangent,
    )
    next_fields, fields_grad, fine_grad, merge_grad = pl.pallas_call(
        hand_over,
        out_shape=tuple(jax.ShapeDtypeStruct(some.shape, some.dtype) for some in results),
        in_specs=[whole] * 4,
        out_specs=[whole] * 4,
        name="hand_over",
    )(*results)
    return next_fields, fields_grad.reshape(2, LEV, LON // TP, D), fine_grad, merge_grad


def solution(mesh):
    placed = (
        P("lat", None, None, None),
        P("lat", None),
        P(),
        P(),
        P(None, "tp", None),
        P("tp", None, None),
        P(),
        P(None, "tp"),
        P(),
        P(None, "tp", None),
        P("tp", None, None),
        P(None, "tp"),
        P("lat", None, None, None),
    )
    return jax.shard_map(
        functools.partial(local, mesh.shape["lat"]),
        mesh=mesh,
        in_specs=placed,
        out_specs=(
            P("lat", None, None, None),
            P("lat", None, "tp", None),
            P("lat", "tp", None),
            P("lat", "tp"),
        ),
        check_vma=False,
    )
```
